32 devices in a mesh: seq: 4 (over y, core), head: 8 (over z, x).
Axes of the slice: x: 2, y: 2, z: 4, core: 2. Of those that a mesh axis runs over, the one named last changes fastest.
Arguments:
- tokens: bfloat16 [4096, 2048], P(('seq', 'head')), may hold values from -6 to 6
- w_qkvg: bfloat16 [2048, 12288], P('seq', 'head'), may hold values from -0.125 to 0.125
- w_rates: bfloat16 [2048, 32], P('seq', 'head'), may hold values from -0.125 to 0.125
- conv_weight: float32 [4, 8192], P(None, 'head'), may hold values from -3 to 3
- head_bias: float32 [2, 16], P(None, 'head'), may hold values from -12 to -1.5, as said below
- norm_gain: float32 [2048], replicated, may hold values from 0.25 to 1.75
- head_gain: float32 [256], replicated, may hold values from 0.25 to 1.75
- mlp_gain: float32 [2048], replicated, may hold values from 0.25 to 1.75
- w_out: bfloat16 [4096, 2048], P('head', 'seq'), may hold values from -0.09375 to 0.09375
- w_ff_gate: bfloat16 [5632, 2048], P('head', 'seq'), may hold values from -0.125 to 0.125
- w_ff_up: bfloat16 [5632, 2048], P('head', 'seq'), may hold values from -0.125 to 0.125
- w_ff_down: bfloat16 [5632, 2048], P('head', 'seq'), may hold values from -0.078125 to 0.078125
- cotangent: bfloat16 [4096, 2048], P(('seq', 'head')), may hold values from -6 to 6
Outputs:
- output: bfloat16 [4096, 2048], P(('seq', 'head'))
- tokens_grad: float32 [4096, 2048], P(('seq', 'head'))
- w_qkvg_grad: float32 [2048, 12288], P('seq', 'head')
- w_rates_grad: float32 [2048, 32], P('seq', 'head')
- conv_weight_grad: float32 [4, 8192], P(None, 'head')
- head_bias_grad: float32 [2, 16], P(None, 'head')
- norm_gain_grad: float32 [2048], replicated
- head_gain_grad: float32 [256], replicated
- mlp_gain_grad: float32 [2048], replicated
- w_out_grad: float32 [4096, 2048], P('head', 'seq')
- w_ff_gate_grad: float32 [5632, 2048], P('head', 'seq')
- w_ff_up_grad: float32 [5632, 2048], P('head', 'seq')
- w_ff_down_grad: float32 [5632, 2048], P('head', 'seq')
The draws below stay inside these ranges and needn't reach their ends.
Inputs may be any that keep to these rules, and one draw needn't show every extreme that they name: `head_bias`: row 0 shifts each head's decay logit, row 1 its update-strength logit.
All inputs are finite; a program needn't handle non-finite values.
Results may differ from the reference program's by a relative error of at most 0.025.
Values may be sent and summed in bfloat16 or wider, within the bound.
No kernel may reach another device: no remote copies, remote signals or barrier semaphores. Data moves between devices by JAX's collectives and lax.ppermute only.
A program may use at most 320 MiB of HBM per device.

```python
import math
from functools import partial
import jax
import jax.numpy as jnp
from jax import lax

D = 2048
HEADS = 16
DK = 128
DV = 256
FF = 5632
CONV = 4
BLOCK = 64
TOKENS = 4096


def draw_head_bias(key, part):
    key = jax.random.fold_in(key, 11)
    decay_key, rate_key = jax.random.split(key)
    decay_bias = jax.random.uniform(decay_key, (HEADS,), jnp.float32, -12.0, -4.0)
    rate_bias = jax.random.uniform(rate_key, (HEADS,), jnp.float32, -5.0, -1.5)
    return jnp.stack([decay_bias, rate_bias], axis=0)


def shard_levels(stream_key, shape, cuts, least, high):
    def one(dim, blocks):
        draws = jax.random.uniform(jax.random.fold_in(jax.random.fold_in(stream_key, 6), dim), (blocks,), jnp.float32, least / len(cuts), high / len(cuts))
        return jnp.repeat(jnp.exp(draws), shape[dim] // blocks).reshape((-1,) + (1,) * (len(shape) - dim - 1))

    loudness = one(*cuts[0])
    for cut in cuts[1:]:
        loudness = loudness * one(*cut)
    return loudness


def bell_draw(stream_key, dims, width, limit, shards=(), kind=jnp.bfloat16):
    level = shard_levels(stream_key, dims, shards, -0.22, 0.18) if shards else 1.0
    values = jax.random.normal(stream_key, dims, jnp.float32) * width * level
    return jnp.minimum(jnp.maximum(values, -limit), limit).astype(kind)


def setup_inputs(seed: int = 0) -> dict:
    splits = jax.random.split(jax.random.key(seed), 14)
    tokens = bell_draw(splits[0], (TOKENS, D), 1.0, 6.0, ((0, 32),))
    w_qkvg = bell_draw(splits[1], (D, HEADS * (2 * DK + 2 * DV)), D ** -0.5, 0.125, ((0, 4), (1, 8)))
    w_rates = bell_draw(splits[2], (D, 2 * HEADS), D ** -0.5, 0.125, ((0, 4), (1, 8)))
    conv_weight = bell_draw(splits[3], (CONV, HEADS * (2 * DK + DV)), CONV ** -0.5, 3.0, ((1, 8),), jnp.float32)
    head_bias = draw_head_bias(jax.random.fold_in(splits[13], 71), 0)
    norm_gain = jnp.clip(1.0 + 0.15 * jax.random.normal(splits[5], (D,), jnp.float32), 0.25, 1.75)
    head_gain = jnp.clip(1.0 + 0.15 * jax.random.normal(splits[6], (DV,), jnp.float32), 0.25, 1.75)
    mlp_gain = jnp.clip(1.0 + 0.15 * jax.random.normal(splits[7], (D,), jnp.float32), 0.25, 1.75)
    w_out = bell_draw(splits[8], (HEADS * DV, D), (HEADS * DV) ** -0.5, 0.09375, ((0, 8), (1, 4)))
    w_ff_gate = bell_draw(splits[9], (FF, D), D ** -0.5, 0.125, ((0, 8), (1, 4)))
    w_ff_up = bell_draw(splits[10], (FF, D), D ** -0.5, 0.125, ((0, 8), (1, 4)))
    w_ff_down = bell_draw(splits[11], (FF, D), FF ** -0.5, 0.078125, ((0, 8), (1, 4)))
    cotangent = bell_draw(splits[12], (TOKENS, D), 1.0, 6.0, ((0, 32),))
    return dict(tokens=tokens, w_qkvg=w_qkvg, w_rates=w_rates, conv_weight=conv_weight, head_bias=head_bias, norm_gain=norm_gain, head_gain=head_gain, mlp_gain=mlp_gain, w_out=w_out, w_ff_gate=w_ff_gate, w_ff_up=w_ff_up, w_ff_down=w_ff_down, cotangent=cotangent)


@jax.custom_vjp
def low(v):
    return lax.optimization_barrier(v.astype(jnp.bfloat16)).astype(jnp.float32)

@jax.custom_vjp
def low_back(v):
    return v

def low_keep(v):
    return (low(v), None)

def low_pass(kept, grad):
    return (grad,)

def back_keep(v):
    return (v, None)

def back_low(kept, grad):
    return (low(grad),)
low.defvjp(low_keep, low_pass)
low_back.defvjp(back_keep, back_low)
epsilon = 1e-06
highest = lax.Precision.HIGHEST

def exact_product(form, left, right):
    return jnp.einsum(form, left, right, precision=highest)

def unit_lower_inverse(lower_part):
    full_size = lower_part.shape[1]
    identity = jnp.eye(full_size, dtype=jnp.float32)
    result = identity - lower_part
    power = lower_part
    span = 2
    while span < full_size:
        power = exact_product('bij,bjk->bik', power, power)
        result = exact_product('bij,bjk->bik', result, identity + power)
        span = 2 * span
    return result

def unit_rows(matrix):
    return matrix * lax.rsqrt(lax.optimization_barrier(jnp.sum(matrix * matrix, axis=-1, keepdims=True)) + epsilon)

def block_step(carry_state, pieces):
    queries, key_rows, values, log_decay, strength = pieces
    block_count = log_decay.shape[0]
    cumulative = jnp.cumsum(log_decay)
    final_decay = cumulative[-1]
    positions = jnp.arange(block_count)
    included = positions[:, None] >= positions[None, :]
    strictly = positions[:, None] > positions[None, :]
    difference = cumulative[:, None] - cumulative[None, :]
    decays = jnp.where(included, jnp.exp(jnp.where(included, difference, 0.0)), 0.0)
    key_gram = jnp.matmul(key_rows, key_rows.T, precision=highest)
    lower_part = jnp.where(strictly, strength[:, None] * decays * key_gram, 0.0)
    inverse = unit_lower_inverse(lower_part[None])[0]
    updates = jnp.matmul(inverse, strength[:, None] * values, precision=highest)
    weighted = jnp.matmul(inverse, (strength * jnp.exp(cumulative))[:, None] * key_rows, precision=highest)
    errors = updates - jnp.matmul(weighted, carry_state.T, precision=highest)
    scores = jnp.matmul(queries, key_rows.T, precision=highest) * decays
    outputs = jnp.matmul(queries * jnp.exp(cumulative)[:, None], carry_state.T, precision=highest) + jnp.matmul(scores, errors, precision=highest)
    key_tails = key_rows * jnp.exp(final_decay - cumulative)[:, None]
    new_state = jnp.exp(final_decay) * carry_state + jnp.matmul(errors.T, key_tails, precision=highest)
    return (new_state, outputs)

def head_output(normed, weights):
    w_head, w_rate, conv_taps, biases = weights
    row_count = normed.shape[0]
    mixed_width = 2 * DK + DV
    projected = low(low_back(jnp.matmul(normed, w_head, precision=highest)))
    rate_logits = low_back(jnp.matmul(normed, w_rate, precision=highest))
    padded = jnp.concatenate([jnp.zeros((CONV - 1, mixed_width), jnp.float32), projected[:, :mixed_width]], axis=0)
    mixed_rows = jax.nn.silu(sum((conv_taps[tap_index] * padded[tap_index:tap_index + row_count] for tap_index in range(CONV))))
    queries = unit_rows(mixed_rows[:, :DK]) * DK ** (-0.5)
    key_rows = unit_rows(mixed_rows[:, DK:2 * DK])
    values = mixed_rows[:, 2 * DK:]
    log_decay = -jax.nn.softplus(rate_logits[:, 0] + biases[0])
    strength = jax.nn.sigmoid(rate_logits[:, 1] + biases[1])
    blocks = row_count // BLOCK
    zero_state = jnp.zeros((DV, DK), jnp.float32)
    last_state, outputs = lax.scan(jax.checkpoint(block_step), zero_state, (queries.reshape(blocks, BLOCK, DK), key_rows.reshape(blocks, BLOCK, DK), values.reshape(blocks, BLOCK, DV), log_decay.reshape(blocks, BLOCK), strength.reshape(blocks, BLOCK)))
    return (low(low_back(outputs.reshape(row_count, DV))), projected[:, mixed_width:])

def forward(tokens, w_qkvg, w_rates, conv_weight, head_bias, norm_gain, head_gain, mlp_gain, w_out, w_ff_gate, w_ff_up, w_ff_down):
    row_count = tokens.shape[0]
    per_head = 2 * DK + 2 * DV
    mixed_width = 2 * DK + DV
    normed = low(tokens * lax.rsqrt(lax.optimization_barrier(jnp.mean(tokens * tokens, axis=-1, keepdims=True)) + epsilon) * norm_gain)
    head_weights = (jnp.transpose(w_qkvg.reshape(D, HEADS, per_head), (1, 0, 2)), jnp.transpose(w_rates.reshape(D, HEADS, 2), (1, 0, 2)), jnp.transpose(conv_weight.reshape(CONV, HEADS, mixed_width), (1, 0, 2)), head_bias.T)
    mixer_out, gate_out = lax.map(jax.checkpoint(partial(head_output, normed)), head_weights)
    mixer_tokens = jnp.transpose(mixer_out, (1, 0, 2))
    gate_tokens = jnp.transpose(gate_out, (1, 0, 2))
    block_rows = math.gcd(row_count, 4096)
    groups = row_count // block_rows

    def token_block(pieces):
        inputs, mixer_rows, gate_rows = pieces
        head_normed = mixer_rows * lax.rsqrt(lax.optimization_barrier(jnp.mean(mixer_rows * mixer_rows, axis=-1, keepdims=True)) + epsilon)
        gated_rows = low(head_normed * head_gain * jax.nn.silu(gate_rows)).reshape(block_rows, HEADS * DV)
        residual = inputs + low_back(jnp.matmul(gated_rows, w_out, precision=highest))
        mlp_in = low(residual * lax.rsqrt(lax.optimization_barrier(jnp.mean(residual * residual, axis=-1, keepdims=True)) + epsilon) * mlp_gain)
        gate_pre = low_back(jnp.matmul(mlp_in, w_ff_gate.T, precision=highest))
        up_pre = low_back(jnp.matmul(mlp_in, w_ff_up.T, precision=highest))
        hidden = low(jax.nn.silu(gate_pre) * up_pre)
        return residual + low_back(jnp.matmul(hidden, w_ff_down, precision=highest))
    result = lax.map(jax.checkpoint(token_block), (tokens.reshape(groups, block_rows, D), mixer_tokens.reshape(groups, block_rows, HEADS, DV), gate_tokens.reshape(groups, block_rows, HEADS, DV)))
    return result.reshape(row_count, D)

def reference(tokens, w_qkvg, w_rates, conv_weight, head_bias, norm_gain, head_gain, mlp_gain, w_out, w_ff_gate, w_ff_up, w_ff_down, cotangent):
    arrays = [array.astype(jnp.float32) for array in (tokens, w_qkvg, w_rates, conv_weight, head_bias, norm_gain, head_gain, mlp_gain, w_out, w_ff_gate, w_ff_up, w_ff_down)]
    output, pullback = jax.vjp(forward, *arrays)
    gradients = pullback(cotangent.astype(jnp.float32))
    return (output.astype(jnp.bfloat16), gradients[0], gradients[1], gradients[2], gradients[3], gradients[4], gradients[5], gradients[6], gradients[7], gradients[8], gradients[9], gradients[10], gradients[11])
```

```python
import functools
import jax
import jax.numpy as jnp
from jax import lax
from jax.experimental import pallas as pl
from jax.experimental.pallas import tpu as pltpu
from jax.sharding import PartitionSpec as P

DK = 128
DV = 256
CONV = 4
CHUNK = 128
MIX = 2 * DK + DV
PER = 2 * DK + 2 * DV
GROUP = 4
epsilon = 1e-06
highest = lax.Precision.HIGHEST
F32 = jnp.float32
BF16 = jnp.bfloat16
HALO = 16
VMEM_LIMIT = 56 * 1024 * 1024


def shifted(value, axis, steps):
    count = lax.axis_size(axis)
    leading, last = (max(0, -steps), min(count, count - steps))
    return lax.ppermute(value, axis, [(source, source + steps) for source in range(leading, last)])


def entering(shard, axis, combine, identity):
    peers, position = (lax.axis_size(axis), lax.axis_index(axis))
    everything = jax.tree.map(lambda part: lax.all_gather(part, axis), shard)
    start = jax.tree.map(
        lambda part, zero: jnp.broadcast_to(jnp.asarray(zero, part.dtype), part.shape),
        shard,
        identity,
    )

    def turn(k, before):
        reached = k < position
        new = combine(before, jax.tree.map(lambda part: part[k], everything))
        return jax.tree.map(lambda a, b: jnp.where(reached, a, b), new, before)

    return lax.fori_loop(0, peers, turn, start)


def prefix(shard, axis, join, neutral):
    count = lax.axis_size(axis)
    place = lax.axis_index(axis)
    ahead = count - 1 - place
    gathered = jax.tree.map(
        lambda a, kind: lax.all_gather(a.astype(kind), axis), shard, (jnp.bfloat16, jnp.bfloat16)
    )
    state = jax.tree.map(lambda a, e: jnp.zeros_like(a) + jnp.asarray(e, a.dtype), shard, neutral)

    def one(turn, state):
        source = count - 1 - turn
        return join(
            state,
            jax.tree.map(
                lambda a, own: lax.dynamic_index_in_dim(a, source, 0, False).astype(own.dtype),
                gathered,
                shard,
            ),
        )

    return lax.fori_loop(0, ahead, one, state)


def exact_product(form, left, right):
    return jnp.einsum(form, left, right, precision=highest)


def compose(earlier, later):
    return (
        exact_product("hij,hjk->hik", earlier[0], later[0]),
        exact_product("hvj,hjk->hvk", earlier[1], later[0]) + later[1],
    )


def mm(a, b, ca=1, cb=0):
    return lax.dot_general(
        a.astype(BF16), b.astype(BF16), (((ca,), (cb,)), ((), ())), preferred_element_type=F32
    )


def mmx(a, b, ca=1, cb=0):
    return lax.dot_general(
        a, b, (((ca,), (cb,)), ((), ())), preferred_element_type=F32, precision=lax.Precision.HIGHEST
    )


def softplus(x):
    return jnp.maximum(x, 0.0) + jnp.log1p(jnp.exp(-jnp.abs(x)))


def sigmoid(x):
    return 1.0 / (1.0 + jnp.exp(-x))


def iotas(n):
    return (
        lax.broadcasted_iota(jnp.int32, (n, n), 0),
        lax.broadcasted_iota(jnp.int32, (n, n), 1),
    )


def inverse_parts(mats, rows, cols):
    base = 16
    near = (rows // base) == (cols // base)
    diag = [jnp.where(near, a, 0.0) for a in mats]
    result = [-d for d in diag]
    power = [mm(d, d) for d in diag]
    span = 2
    while True:
        result = [r + p + mm(r, p) for r, p in zip(result, power)]
        span *= 2
        if span >= base:
            break
        power = [mm(p, p) for p in power]
    size = base
    n = mats[0].shape[0]
    while size < n:
        cross = ((rows // (2 * size)) == (cols // (2 * size))) & ((rows // size) != (cols // size))
        off = [jnp.where(cross, a, 0.0) for a in mats]
        left = [o + mm(r, o) for o, r in zip(off, result)]
        result = [r - x - mm(x, r) for r, x in zip(result, left)]
        size *= 2
    return result


def conv_scratch(first, proj_ref, prev_ref, halo_ref, x_ref, heads, rows):
    for h in range(heads):
        cols = slice(h * PER, h * PER + MIX)
        before = jnp.where(first, halo_ref[:, cols].astype(F32), prev_ref[:, cols].astype(F32))
        x_ref[0:8, h * MIX : (h + 1) * MIX] = before[HALO - 8 :]
        x_ref[8 : 8 + rows, h * MIX : (h + 1) * MIX] = proj_ref[:, cols].astype(F32)


def conv_pre(x_ref, taps_ref, h, row):
    cols = slice(h * MIX, (h + 1) * MIX)
    total = None
    for i in range(CONV):
        part = taps_ref[i : i + 1, cols] * x_ref[pl.ds(row + 8 - (CONV - 1) + i, CHUNK), cols]
        total = part if total is None else total + part
    return total


def unit(a):
    r = lax.rsqrt(jnp.sum(a * a, axis=-1, keepdims=True) + epsilon)
    return a * r, r


def forward_kernel(
    heads, group,
    proj_ref, prev_ref, halo_ref, rates_ref, bias_ref, taps_ref,
    olocal_ref, qmap_ref, state_ref, uw_ref, inv_ref, trans_ref, qe_ref, end_ref,
    x_ref, carry_ref, n_ref,
):
    step = pl.program_id(0)
    rows_here = CHUNK * group
    conv_scratch(step == 0, proj_ref, prev_ref, halo_ref, x_ref, heads, rows_here)
    ri, ci = iotas(CHUNK)
    included = ri >= ci
    strictly = ri > ci
    lower = jnp.where(included, 1.0, 0.0)
    upper = jnp.where(ri <= ci, 1.0, 0.0)

    @pl.when(step == 0)
    def _():
        for h in range(heads):
            carry_ref[h, :DV, :] = jnp.zeros((DV, DK), F32)
            carry_ref[h, DV:, :] = jnp.where(ri == ci, 1.0, 0.0)

    pairs = [(g, h) for g in range(group) for h in range(heads)]
    logits = rates_ref[...] + bias_ref[...]
    log_decay = -softplus(logits)
    strength = sigmoid(logits)
    cums, cum_rows = [], []
    for g in range(group):
        part = log_decay[g * CHUNK : (g + 1) * CHUNK]
        cums.append(mmx(lower, part))
        cum_rows.append(mmx(part, upper, 0, 0))
    mats, scores, rhs, tails, scaled_q, finals = [], [], [], [], [], []
    for g, h in pairs:
        pre = conv_pre(x_ref, taps_ref, h, g * CHUNK)
        mixed = pre * sigmoid(pre)
        q = unit(mixed[:, :DK])[0] * DK ** (-0.5)
        k = unit(mixed[:, DK : 2 * DK])[0]
        v = mixed[:, 2 * DK :]
        cum = cums[g][:, 2 * h : 2 * h + 1]
        cum_row = cum_rows[g][2 * h : 2 * h + 1, :]
        beta = strength[g * CHUNK : (g + 1) * CHUNK, 2 * h + 1 : 2 * h + 2]
        growth = jnp.exp(cum)
        decays = jnp.where(included, jnp.exp(jnp.where(included, cum - cum_row, 0.0)), 0.0)
        grams = mm(jnp.concatenate([q, k], axis=0), k, 1, 1)
        scores.append(grams[:CHUNK] * decays)
        mats.append(jnp.where(strictly, beta * decays * grams[CHUNK:], 0.0))
        rhs.append(jnp.concatenate([beta * v, beta * growth * k], axis=1))
        last = cum[CHUNK - 1 : CHUNK, :]
        tails.append(k * jnp.exp(last - cum))
        scaled_q.append(growth * q)
        finals.append(jnp.exp(last))
    inverses = inverse_parts(mats, ri, ci)
    solved = [b + mm(r, b) for r, b in zip(inverses, rhs)]
    mixes = [mm(p, u) for p, u in zip(scores, solved)]
    adds = [mm(u, t, 0, 0) for u, t in zip(solved, tails)]
    for j, (g, h) in enumerate(pairs):
        inv_ref[h, g] = inverses[j].astype(BF16)
        uw_ref[h, g] = solved[j].astype(BF16)
        qe_ref[h, g] = (scaled_q[j] - mixes[j][:, DV:]).astype(BF16)
        trans_ref[h, g] = (-adds[j][DV:]).astype(BF16)
        olocal_ref[g * CHUNK : (g + 1) * CHUNK, h * DV : (h + 1) * DV] = mixes[j][:, :DV]
    for h in range(heads):
        now = carry_ref[h]
        for g in range(group):
            j = pairs.index((g, h))
            low = now.astype(BF16)
            state_ref[h, g] = low
            moved = finals[j] * now + mm(low, trans_ref[h, g])
            now = jnp.concatenate([moved[:DV] + adds[j][:DV], moved[DV:]], axis=0)
        carry_ref[h] = now
        end_ref[h] = now
    for j, (g, h) in enumerate(pairs):
        both = mm(qe_ref[h, g], state_ref[h, g], 1, 1)
        rows = slice(g * CHUNK, (g + 1) * CHUNK)
        olocal_ref[rows, h * DV : (h + 1) * DV] += both[:, :DV]
        qmap_ref[rows, h * DK : (h + 1) * DK] = both[:, DV:].astype(BF16)


def mixer_forward(projected, halo, rates, bias_row, taps, group):
    total = projected.shape[0]
    heads = rates.shape[1] // 2
    rows = CHUNK * group
    steps = total // rows
    chunks = total // CHUNK
    whole = lambda i: (0, 0)
    saved = lambda a, b: (
        jax.ShapeDtypeStruct((heads, chunks, a, b), BF16),
        pl.BlockSpec((heads, group, a, b), lambda i: (0, i, 0, 0)),
    )
    outs = [
        (jax.ShapeDtypeStruct((total, heads * DV), F32), pl.BlockSpec((rows, heads * DV), lambda i: (i, 0))),
        (jax.ShapeDtypeStruct((total, heads * DK), BF16), pl.BlockSpec((rows, heads * DK), lambda i: (i, 0))),
        saved(DV + DK, DK),
        saved(CHUNK, DV + DK),
        saved(CHUNK, CHUNK),
        saved(DK, DK),
        saved(CHUNK, DK),
        (jax.ShapeDtypeStruct((heads, DV + DK, DK), F32), pl.BlockSpec((heads, DV + DK, DK), lambda i: (0, 0, 0))),
    ]
    return pl.pallas_call(
        functools.partial(forward_kernel, heads, group),
        grid=(steps,),
        in_specs=[
            pl.BlockSpec((rows, heads * PER), lambda i: (i, 0)),
            pl.BlockSpec((HALO, heads * PER), lambda i: (jnp.maximum(i * (rows // HALO) - 1, 0), 0)),
            pl.BlockSpec((HALO, heads * PER), whole),
            pl.BlockSpec((rows, 2 * heads), lambda i: (i, 0)),
            pl.BlockSpec((1, 2 * heads), whole),
            pl.BlockSpec((CONV, heads * MIX), whole),
        ],
        out_shape=[o[0] for o in outs],
        out_specs=[o[1] for o in outs],
        scratch_shapes=[
            pltpu.VMEM((rows + 8, heads * MIX), F32),
            pltpu.VMEM((heads, DV + DK, DK), F32),
            pltpu.VMEM((8, 128), F32),
        ],
        compiler_params=pltpu.CompilerParams(vmem_limit_bytes=VMEM_LIMIT),
        cost_estimate=pl.CostEstimate(flops=40_000_000_000, bytes_accessed=16_000_000, transcendentals=0),
    )(projected, projected, halo, rates, bias_row, taps)


def backward_kernel(
    heads, group, steps,
    proj_ref, prev_ref, halo_ref, rates_ref, bias_ref, taps_ref,
    state_ref, uw_ref, inv_ref, trans_ref, qe_ref,
    dout_ref, ggate_ref, incoming_ref, dend_ref,
    gp_ref, grates_ref, gtaps_ref, gbias_ref, tail_ref, lead_ref,
    x_ref, d_ref, carry_ref, next_ref,
):
    step = pl.program_id(0)
    rows_here = CHUNK * group
    conv_scratch(step == steps - 1, proj_ref, prev_ref, halo_ref, x_ref, heads, rows_here)
    ri, ci = iotas(CHUNK)
    included = ri >= ci
    strictly = ri > ci
    lower = jnp.where(included, 1.0, 0.0)
    upper = jnp.where(ri <= ci, 1.0, 0.0)

    @pl.when(step == 0)
    def _():
        for h in range(heads):
            carry_ref[h] = dend_ref[h]
        d_ref[rows_here : rows_here + 8, :] = jnp.zeros((8, heads * MIX), F32)
        gtaps_ref[...] = jnp.zeros_like(gtaps_ref)
        gbias_ref[...] = jnp.zeros_like(gbias_ref)

    @pl.when(step > 0)
    def _():
        d_ref[rows_here : rows_here + 8, :] = d_ref[0:8, :]

    pairs = [(g, h) for g in range(group) for h in range(heads)]
    logits = rates_ref[...] + bias_ref[...]
    log_decay = -softplus(logits)
    strength = sigmoid(logits)
    cums, cum_rows = [], []
    for g in range(group):
        part = log_decay[g * CHUNK : (g + 1) * CHUNK]
        cums.append(mmx(lower, part))
        cum_rows.append(mmx(part, upper, 0, 0))
    douts, injections = [], []
    for g, h in pairs:
        do = dout_ref[g * CHUNK : (g + 1) * CHUNK, h * DV : (h + 1) * DV]
        douts.append(do)
        injections.append(mm(do, qe_ref[h, g], 0, 0))
    for h in range(heads):
        now = carry_ref[h]
        for g in reversed(range(group)):
            j = pairs.index((g, h))
            last = cums[g][CHUNK - 1 : CHUNK, 2 * h : 2 * h + 1]
            next_ref[h, g] = now
            now = jnp.exp(last) * now + mm(now, trans_ref[h, g], 1, 1) + injections[j]
        carry_ref[h] = now
    lane = lax.broadcasted_iota(jnp.int32, (CHUNK, 2 * heads), 1)
    row_col = lax.broadcasted_iota(jnp.int32, (CHUNK, 1), 0)
    dcums = [jnp.zeros((CHUNK, 2 * heads), F32) for _ in range(group)]
    dbetas = [jnp.zeros((CHUNK, 2 * heads), F32) for _ in range(group)]
    for j, (g, h) in enumerate(pairs):
        pre = conv_pre(x_ref, taps_ref, h, g * CHUNK)
        sig = sigmoid(pre)
        mixed = pre * sig
        slope = sig * (1.0 + pre * (1.0 - sig))
        uq, rq = unit(mixed[:, :DK])
        q = uq * DK ** (-0.5)
        k, rk = unit(mixed[:, DK : 2 * DK])
        v = mixed[:, 2 * DK :]
        cum = cums[g][:, 2 * h : 2 * h + 1]
        cum_row = cum_rows[g][2 * h : 2 * h + 1, :]
        beta = strength[g * CHUNK : (g + 1) * CHUNK, 2 * h + 1 : 2 * h + 2]
        growth = jnp.exp(cum)
        decays = jnp.where(included, jnp.exp(jnp.where(included, cum - cum_row, 0.0)), 0.0)
        qb, kb = q.astype(BF16), k.astype(BF16)
        grams = mm(jnp.concatenate([qb, kb], axis=0), kb, 1, 1)
        scores = grams[:CHUNK] * decays
        dk_gram = decays * grams[CHUNK:]
        last = cum[CHUNK - 1 : CHUNK, :]
        fade = jnp.exp(last - cum)
        tail = k * fade
        sl = state_ref[h, g]
        state = sl[:DV].astype(F32) + mm(incoming_ref[h], sl[DV:])
        after = next_ref[h, g]
        afterb = after.astype(BF16)
        stateb = state.astype(BF16)
        uw = uw_ref[h, g]
        errors = uw[:, :DV].astype(F32) - mm(uw[:, DV:], stateb, 1, 1)
        eb = errors.astype(BF16)
        do = douts[j]
        de = mm(scores, do, 0, 0) + mm(tail, afterb, 1, 1)
        db = de + mm(inv_ref[h, g], de, 0, 0)
        dbb = db.astype(BF16)
        stacked = jnp.concatenate([do, dbb], axis=0)
        against_e = mm(stacked, eb, 1, 1)
        against_s = mm(stacked, stateb)
        dp = against_e[:CHUNK]
        da = jnp.where(strictly, -against_e[CHUNK:], 0.0)
        dos = against_s[:CHUNK]
        dbs = against_s[CHUNK:]
        dpd = dp * decays
        dg = da * beta * decays
        crossed = dp * scores + da * beta * dk_gram
        dtail = mm(eb, afterb)
        dq = mm(dpd, kb) + growth * dos
        sym = dg + dg.T
        dk = (
            mm(jnp.concatenate([dpd.T, sym], axis=1), jnp.concatenate([qb, kb], axis=0))
            - beta * growth * dbs
            + fade * dtail
        )
        dv = beta * db
        kdbs = jnp.sum(k * dbs, axis=1, keepdims=True)
        dbeta = (
            jnp.sum(db * v, axis=1, keepdims=True)
            - growth * kdbs
            + jnp.sum(da * dk_gram, axis=1, keepdims=True)
        )
        tdot = jnp.sum(tail * dtail, axis=1, keepdims=True)
        dcum = (
            jnp.sum(crossed - crossed.T, axis=1, keepdims=True)
            + growth * jnp.sum(q * dos, axis=1, keepdims=True)
            - beta * growth * kdbs
            - tdot
        )
        at_end = jnp.exp(last) * jnp.sum(jnp.sum(after * state, axis=1, keepdims=True), axis=0, keepdims=True) + jnp.sum(
            tdot, axis=0, keepdims=True
        )
        dcum = dcum + jnp.where(row_col == CHUNK - 1, at_end, 0.0)
        dcums[g] = jnp.where(lane == 2 * h, dcum, dcums[g])
        dbetas[g] = jnp.where(lane == 2 * h + 1, dbeta, dbetas[g])
        dq = dq * DK ** (-0.5)
        dmq = rq * (dq - uq * jnp.sum(uq * dq, axis=1, keepdims=True))
        dmk = rk * (dk - k * jnp.sum(k * dk, axis=1, keepdims=True))
        d_ref[g * CHUNK : (g + 1) * CHUNK, h * MIX : (h + 1) * MIX] = (
            jnp.concatenate([dmq, dmk, dv], axis=1) * slope
        )
    for g in range(group):
        rows = slice(g * CHUNK, (g + 1) * CHUNK)
        s = strength[rows]
        dld = mmx(upper, dcums[g])
        drate = jnp.where(lane % 2 == 0, -sigmoid(logits[rows]) * dld, s * (1.0 - s) * dbetas[g])
        grates_ref[rows, :] = drate
        gbias_ref[...] += jnp.sum(drate, axis=0, keepdims=True)
    for g, h in pairs:
        cols = slice(h * MIX, (h + 1) * MIX)
        row = g * CHUNK
        dpre = d_ref[pl.ds(row, CHUNK), cols]
        total = None
        for i in range(CONV):
            gtaps_ref[i : i + 1, cols] += jnp.sum(
                dpre * x_ref[pl.ds(row + 8 - (CONV - 1) + i, CHUNK), cols], axis=0, keepdims=True
            )
            part = taps_ref[i : i + 1, cols] * d_ref[pl.ds(row + CONV - 1 - i, CHUNK), cols]
            total = part if total is None else total + part
        gp_ref[row : row + CHUNK, h * PER : h * PER + MIX] = total.astype(BF16)
        gp_ref[row : row + CHUNK, h * PER + MIX : (h + 1) * PER] = ggate_ref[
            row : row + CHUNK, h * DV : (h + 1) * DV
        ]
        if g == group - 1:
            @pl.when(step == 0)
            def _(total=total, cols=cols):
                tail_ref[:, cols] = total[CHUNK - HALO :]

    @pl.when(step == steps - 1)
    def _():
        lead_ref[...] = d_ref[0:8, :]


def mixer_backward(projected, halo, rates, bias_row, taps, saved, dout, ggate, incoming, dend, group):
    state, uw, inv, trans, qe = saved
    total = projected.shape[0]
    heads = rates.shape[1] // 2
    rows = CHUNK * group
    steps = total // rows
    whole = lambda i: (0, 0)
    flip = lambda i: (steps - 1 - i, 0)
    keep = lambda a, b: pl.BlockSpec((heads, group, a, b), lambda i: (0, steps - 1 - i, 0, 0))
    return pl.pallas_call(
        functools.partial(backward_kernel, heads, group, steps),
        grid=(steps,),
        in_specs=[
            pl.BlockSpec((rows, heads * PER), flip),
            pl.BlockSpec((HALO, heads * PER), lambda i: (jnp.maximum((steps - 1 - i) * (rows // HALO) - 1, 0), 0)),
            pl.BlockSpec((HALO, heads * PER), whole),
            pl.BlockSpec((rows, 2 * heads), flip),
            pl.BlockSpec((1, 2 * heads), whole),
            pl.BlockSpec((CONV, heads * MIX), whole),
            keep(DV + DK, DK),
            keep(CHUNK, DV + DK),
            keep(CHUNK, CHUNK),
            keep(DK, DK),
            keep(CHUNK, DK),
            pl.BlockSpec((rows, heads * DV), flip),
            pl.BlockSpec((rows, heads * DV), flip),
            pl.BlockSpec((heads, DV, DK), lambda i: (0, 0, 0)),
            pl.BlockSpec((heads, DV, DK), lambda i: (0, 0, 0)),
        ],
        out_shape=[
            jax.ShapeDtypeStruct((total, heads * PER), BF16),
            jax.ShapeDtypeStruct((total, 2 * heads), F32),
            jax.ShapeDtypeStruct((CONV, heads * MIX), F32),
            jax.ShapeDtypeStruct((1, 2 * heads), F32),
            jax.ShapeDtypeStruct((HALO, heads * MIX), F32),
            jax.ShapeDtypeStruct((8, heads * MIX), F32),
        ],
        out_specs=[
            pl.BlockSpec((rows, heads * PER), flip),
            pl.BlockSpec((rows, 2 * heads), flip),
            pl.BlockSpec((CONV, heads * MIX), whole),
            pl.BlockSpec((1, 2 * heads), whole),
            pl.BlockSpec((HALO, heads * MIX), whole),
            pl.BlockSpec((8, heads * MIX), whole),
        ],
        scratch_shapes=[
            pltpu.VMEM((rows + 8, heads * MIX), F32),
            pltpu.VMEM((rows + 8, heads * MIX), F32),
            pltpu.VMEM((heads, DV, DK), F32),
            pltpu.VMEM((heads, group, DV, DK), F32),
        ],
        compiler_params=pltpu.CompilerParams(vmem_limit_bytes=VMEM_LIMIT),
        cost_estimate=pl.CostEstimate(flops=60_000_000_000, bytes_accessed=20_000_000, transcendentals=0),
    )(projected, projected, halo, rates, bias_row, taps, state, uw, inv, trans, qe, dout, ggate, incoming, dend)


def per_device(
    tokens,
    w_qkvg,
    w_rates,
    conv_weight,
    head_bias,
    norm_gain,
    head_gain,
    mlp_gain,
    w_out,
    w_ff_gate,
    w_ff_up,
    w_ff_down,
    cotangent,
):
    heads_here = head_bias.shape[1]
    per_head = 2 * DK + 2 * DV
    mixed_width = 2 * DK + DV
    contract = (((1,), (1,)), ((), ()))
    rows_first = (((0,), (0,)), ((), ()))
    head_index = lax.axis_index("head")
    inputs = tokens.astype(jnp.float32)
    inverse_one = lax.rsqrt(jnp.mean(inputs * inputs, axis=-1, keepdims=True) + epsilon)
    norm_normed = inputs * inverse_one
    block_tokens, block_cotangent = (
        lax.all_gather(tokens, "head", axis=0, tiled=True),
        lax.all_gather(cotangent, "head", axis=0, tiled=True),
    )
    seq_rows = block_tokens.shape[0]
    block_inputs = block_tokens.astype(jnp.float32)
    block_rows = (
        block_inputs
        * lax.rsqrt(jnp.mean(block_inputs * block_inputs, axis=-1, keepdims=True) + epsilon)
        * norm_gain
    ).astype(jnp.bfloat16)
    w_mix, w_rate, out_rows, ff_gate_rows, ff_up_rows, ff_down_rows = (
        lax.all_gather(w_qkvg, "seq", axis=0, tiled=True),
        lax.all_gather(w_rates, "seq", axis=0, tiled=True),
        lax.all_gather(w_out, "seq", axis=1, tiled=True),
        lax.all_gather(w_ff_gate, "seq", axis=1, tiled=True),
        lax.all_gather(w_ff_up, "seq", axis=1, tiled=True),
        lax.all_gather(w_ff_down, "seq", axis=1, tiled=True),
    )
    projected = (
        jnp.dot(block_rows, w_mix, preferred_element_type=jnp.float32)
        .astype(jnp.bfloat16)
        .reshape(seq_rows, heads_here, per_head)
    )
    rate_logits = jnp.dot(block_rows, w_rate, preferred_element_type=jnp.float32).reshape(
        seq_rows, heads_here, 2
    )
    flat_projected = projected.reshape(seq_rows, heads_here * per_head)
    flat_rates = rate_logits.reshape(seq_rows, heads_here * 2)
    bias_row = head_bias.T.reshape(1, 2 * heads_here)
    halo_rows = shifted(flat_projected[seq_rows - HALO :], "seq", 1)
    out_local, query_map, *saved, end_state = mixer_forward(
        flat_projected, halo_rows, flat_rates, bias_row, conv_weight, GROUP
    )
    query_map = query_map.reshape(seq_rows, heads_here, DK)
    transfer = end_state[:, DV:, :]
    injected = end_state[:, :DV, :]
    identity = (
        jnp.broadcast_to(jnp.eye(DK, dtype=jnp.float32), transfer.shape),
        jnp.zeros_like(injected),
    )
    prefix_map, incoming = entering((transfer, injected), "seq", compose, identity)
    attended = out_local.reshape(seq_rows, heads_here, DV) + jnp.einsum(
        "thk,hvk->thv", query_map, incoming.astype(BF16), preferred_element_type=F32
    )
    mixer_val = lax.optimization_barrier(attended.astype(jnp.bfloat16)).astype(jnp.float32)
    gate_val = projected[:, :, mixed_width:].astype(jnp.float32)
    head_inverse = lax.rsqrt(jnp.mean(mixer_val * mixer_val, axis=-1, keepdims=True) + epsilon)
    head_normed = mixer_val * head_inverse
    gate_sigmoid = jax.nn.sigmoid(gate_val)
    gate_silu = gate_val * gate_sigmoid
    gated_rows = (
        (head_normed * head_gain * gate_silu)
        .astype(jnp.bfloat16)
        .reshape(seq_rows, heads_here * DV)
    )
    residual = inputs + lax.psum_scatter(
        jnp.dot(gated_rows, out_rows, preferred_element_type=jnp.float32).astype(jnp.bfloat16),
        "head",
        scatter_dimension=0,
        tiled=True,
    ).astype(jnp.float32)
    own_inverse = lax.rsqrt(jnp.mean(residual * residual, axis=-1, keepdims=True) + epsilon)
    mlp_own = (residual * own_inverse * mlp_gain).astype(jnp.bfloat16)
    mlp_all = lax.all_gather(mlp_own, "head", axis=0, tiled=True)
    inverse_two = lax.rsqrt(jnp.mean(residual * residual, axis=-1, keepdims=True) + epsilon)
    mlp_normed = residual * inverse_two
    gate_pre = lax.dot_general(mlp_all, ff_gate_rows, contract, preferred_element_type=jnp.float32)
    up_pre = lax.dot_general(mlp_all, ff_up_rows, contract, preferred_element_type=jnp.float32)
    ff_sigmoid = jax.nn.sigmoid(gate_pre)
    ff_silu = gate_pre * ff_sigmoid
    hidden = (ff_silu * up_pre).astype(jnp.bfloat16)
    output = (
        residual
        + lax.psum_scatter(
            jnp.dot(hidden, ff_down_rows, preferred_element_type=jnp.float32).astype(jnp.bfloat16),
            "head",
            scatter_dimension=0,
            tiled=True,
        ).astype(jnp.float32)
    ).astype(jnp.bfloat16)
    grad_down = lax.dot_general(
        hidden, block_cotangent, rows_first, preferred_element_type=jnp.float32
    )
    grad_hidden = lax.dot_general(
        block_cotangent, ff_down_rows, contract, preferred_element_type=jnp.float32
    )
    ff_slope = ff_sigmoid * (1.0 + gate_pre * (1.0 - ff_sigmoid))
    grad_gate_pre = (grad_hidden * up_pre * ff_slope).astype(jnp.bfloat16)
    grad_up_pre = (grad_hidden * ff_silu).astype(jnp.bfloat16)
    grad_gate_w = lax.dot_general(
        grad_gate_pre, mlp_all, rows_first, preferred_element_type=jnp.float32
    )
    grad_up_w = lax.dot_general(
        grad_up_pre, mlp_all, rows_first, preferred_element_type=jnp.float32
    )
    grad_mlp_in = lax.psum_scatter(
        (
            jnp.dot(grad_gate_pre, ff_gate_rows, preferred_element_type=jnp.float32)
            + jnp.dot(grad_up_pre, ff_up_rows, preferred_element_type=jnp.float32)
        ).astype(jnp.bfloat16),
        "head",
        scatter_dimension=0,
        tiled=True,
    ).astype(jnp.float32)
    mlp_gain_part = jnp.sum(grad_mlp_in * mlp_normed, axis=0)
    scaled_two = grad_mlp_in * mlp_gain
    grad_residual = cotangent.astype(jnp.float32) + inverse_two * (
        scaled_two - mlp_normed * jnp.mean(scaled_two * mlp_normed, axis=-1, keepdims=True)
    )
    grad_branch = grad_residual.astype(jnp.bfloat16)
    branch_block = lax.all_gather(grad_branch, "head", axis=0, tiled=True)
    grad_out_w = lax.dot_general(
        gated_rows, branch_block, rows_first, preferred_element_type=jnp.float32
    )
    grad_gated = lax.dot_general(
        branch_block, out_rows, contract, preferred_element_type=jnp.float32
    ).reshape(seq_rows, heads_here, DV)
    grad_normed_head = grad_gated * gate_silu
    gate_slope = gate_sigmoid * (1.0 + gate_val * (1.0 - gate_sigmoid))
    grad_gate_mix = (grad_gated * head_normed * head_gain * gate_slope).astype(jnp.bfloat16)
    head_gain_part = jnp.sum(grad_normed_head * head_normed, axis=(0, 1))
    scaled_head = grad_normed_head * head_gain
    grad_mixer = (
        head_inverse
        * (scaled_head - head_normed * jnp.mean(scaled_head * head_normed, axis=-1, keepdims=True))
    ).astype(jnp.bfloat16)
    local_grad = jnp.einsum("thv,thk->hvk", grad_mixer, query_map, preferred_element_type=F32)
    transposed = jnp.swapaxes(transfer, 1, 2)
    suffix_map, grad_end = prefix((transposed, local_grad), "seq", compose, identity)
    grad_projected, grad_rates, grad_taps, grad_bias_row, tail_rows, lead_rows = mixer_backward(
        flat_projected,
        halo_rows,
        flat_rates,
        bias_row,
        conv_weight,
        saved,
        grad_mixer.reshape(seq_rows, heads_here * DV),
        grad_gate_mix.reshape(seq_rows, heads_here * DV),
        incoming,
        grad_end,
        GROUP,
    )
    grad_biases = grad_bias_row.reshape(heads_here, 2).T
    later_rows = shifted(lead_rows, "seq", -1)
    padded = jnp.concatenate([jnp.zeros((HALO, heads_here * mixed_width), F32), later_rows])
    last_rows = tail_rows + sum(
        conv_weight[i] * padded[CONV - 1 - i : CONV - 1 - i + HALO] for i in range(CONV)
    )
    for h in range(heads_here):
        grad_projected = lax.dynamic_update_slice(
            grad_projected,
            last_rows[:, h * mixed_width : (h + 1) * mixed_width].astype(BF16),
            (seq_rows - HALO, h * per_head),
        )
    grad_rate_low = grad_rates.astype(jnp.bfloat16)
    grad_w_mix = lax.dot_general(
        block_rows, grad_projected, rows_first, preferred_element_type=jnp.float32
    )
    grad_w_rate = lax.dot_general(
        block_rows, grad_rate_low, rows_first, preferred_element_type=jnp.float32
    )
    grad_w_mix_s, grad_w_rate_s, grad_out_s, grad_gate_s, grad_up_s, grad_down_s = (
        lax.psum_scatter(
            grad_w_mix.astype(jnp.bfloat16), "seq", scatter_dimension=0, tiled=True
        ).astype(jnp.float32),
        lax.psum_scatter(
            grad_w_rate.astype(jnp.bfloat16), "seq", scatter_dimension=0, tiled=True
        ).astype(jnp.float32),
        lax.psum_scatter(
            grad_out_w.astype(jnp.bfloat16), "seq", scatter_dimension=1, tiled=True
        ).astype(jnp.float32),
        lax.psum_scatter(
            grad_gate_w.astype(jnp.bfloat16), "seq", scatter_dimension=1, tiled=True
        ).astype(jnp.float32),
        lax.psum_scatter(
            grad_up_w.astype(jnp.bfloat16), "seq", scatter_dimension=1, tiled=True
        ).astype(jnp.float32),
        lax.psum_scatter(
            grad_down.astype(jnp.bfloat16), "seq", scatter_dimension=1, tiled=True
        ).astype(jnp.float32),
    )
    grad_normed = lax.psum_scatter(
        (
            lax.dot_general(grad_projected, w_mix, contract, preferred_element_type=jnp.float32)
            + lax.dot_general(grad_rate_low, w_rate, contract, preferred_element_type=jnp.float32)
        ).astype(jnp.bfloat16),
        "head",
        scatter_dimension=0,
        tiled=True,
    ).astype(jnp.float32)
    norm_gain_part = jnp.sum(grad_normed * norm_normed, axis=0)
    scaled_one = grad_normed * norm_gain
    grad_input = grad_residual + inverse_one * (
        scaled_one - norm_normed * jnp.mean(scaled_one * norm_normed, axis=-1, keepdims=True)
    )
    head_groups = lax.axis_size("head")
    taps_full = jnp.zeros((CONV, head_groups, heads_here * mixed_width), jnp.float32)
    taps_full = lax.dynamic_update_slice_in_dim(
        taps_full, grad_taps.reshape(CONV, 1, heads_here * mixed_width), head_index, 1
    )
    bias_full = jnp.zeros((2, head_groups, heads_here), jnp.float32)
    bias_full = lax.dynamic_update_slice_in_dim(
        bias_full, grad_biases.reshape(2, 1, heads_here), head_index, 1
    )
    taps_sum, bias_sum, norm_gain_grad, mlp_gain_grad, head_gain_grad = lax.psum(
        (taps_full, bias_full, norm_gain_part, mlp_gain_part, head_gain_part), ("seq", "head")
    )
    conv_grad = lax.dynamic_index_in_dim(taps_sum, head_index, 1, False)
    bias_grad = lax.dynamic_index_in_dim(bias_sum, head_index, 1, False)
    return (
        output,
        grad_input,
        grad_w_mix_s,
        grad_w_rate_s,
        conv_grad,
        bias_grad,
        norm_gain_grad,
        head_gain_grad,
        mlp_gain_grad,
        grad_out_s,
        grad_gate_s,
        grad_up_s,
        grad_down_s,
    )


def solution(mesh):
    in_specs = (
        P(("seq", "head"), None),
        P("seq", "head"),
        P("seq", "head"),
        P(None, "head"),
        P(None, "head"),
        P(),
        P(),
        P(),
        P("head", "seq"),
        P("head", "seq"),
        P("head", "seq"),
        P("head", "seq"),
        P(("seq", "head"), None),
    )
    out_specs = (
        P(("seq", "head"), None),
        P(("seq", "head"), None),
        P("seq", "head"),
        P("seq", "head"),
        P(None, "head"),
        P(None, "head"),
        P(),
        P(),
        P(),
        P("head", "seq"),
        P("head", "seq"),
        P("head", "seq"),
        P("head", "seq"),
    )
    return jax.shard_map(
        per_device, mesh=mesh, in_specs=in_specs, out_specs=out_specs, check_vma=False
    )
```

```python
import functools
import jax
import jax.numpy as jnp
from jax import lax
from jax.experimental import pallas as pl
from jax.experimental.pallas import tpu as pltpu
from jax.sharding import PartitionSpec as P

DK = 128
DV = 256
CONV = 4
CHUNK = 128
MIX = 2 * DK + DV
PER = 2 * DK + 2 * DV
GROUP = 4
epsilon = 1e-06
F32 = jnp.float32
BF16 = jnp.bfloat16
HALO = 16
VMEM_LIMIT = 56 * 1024 * 1024


def shifted(value, axis, steps):
    count = lax.axis_size(axis)
    leading, last = (max(0, -steps), min(count, count - steps))
    return lax.ppermute(value, axis, [(source, source + steps) for source in range(leading, last)])


def mm(a, b, ca=1, cb=0):
    return lax.dot_general(
        a.astype(BF16), b.astype(BF16), (((ca,), (cb,)), ((), ())), preferred_element_type=F32
    )


def mmx(a, b, ca=1, cb=0):
    return lax.dot_general(
        a, b, (((ca,), (cb,)), ((), ())), preferred_element_type=F32, precision=lax.Precision.HIGHEST
    )


def softplus(x):
    return jnp.maximum(x, 0.0) + jnp.log1p(jnp.exp(-jnp.abs(x)))


def sigmoid(x):
    return 1.0 / (1.0 + jnp.exp(-x))


def iotas(n):
    return (
        lax.broadcasted_iota(jnp.int32, (n, n), 0),
        lax.broadcasted_iota(jnp.int32, (n, n), 1),
    )


def inverse_parts(mats, rows, cols):
    base = 16
    near = (rows // base) == (cols // base)
    diag = [jnp.where(near, a, 0.0) for a in mats]
    result = [-d for d in diag]
    power = [mm(d, d) for d in diag]
    span = 2
    while True:
        result = [r + p + mm(r, p) for r, p in zip(result, power)]
        span *= 2
        if span >= base:
            break
        power = [mm(p, p) for p in power]
    size = base
    n = mats[0].shape[0]
    while size < n:
        cross = ((rows // (2 * size)) == (cols // (2 * size))) & ((rows // size) != (cols // size))
        off = [jnp.where(cross, a, 0.0) for a in mats]
        left = [o + mm(r, o) for o, r in zip(off, result)]
        result = [r - x - mm(x, r) for r, x in zip(result, left)]
        size *= 2
    return result


def conv_scratch(first, proj_ref, prev_ref, halo_ref, x_ref, heads, rows):
    for h in range(heads):
        cols = slice(h * PER, h * PER + MIX)
        before = jnp.where(first, halo_ref[:, cols].astype(F32), prev_ref[:, cols].astype(F32))
        x_ref[0:8, h * MIX : (h + 1) * MIX] = before[HALO - 8 :]
        x_ref[8 : 8 + rows, h * MIX : (h + 1) * MIX] = proj_ref[:, cols].astype(F32)


def conv_pre(x_ref, taps_ref, h, row):
    cols = slice(h * MIX, (h + 1) * MIX)
    total = None
    for i in range(CONV):
        part = taps_ref[i : i + 1, cols] * x_ref[pl.ds(row + 8 - (CONV - 1) + i, CHUNK), cols]
        total = part if total is None else total + part
    return total


def unit(a):
    r = lax.rsqrt(jnp.sum(a * a, axis=-1, keepdims=True) + epsilon)
    return a * r, r


def forward_kernel(
    heads, group,
    proj_ref, prev_ref, halo_ref, rates_ref, bias_ref, taps_ref,
    olocal_ref, qmap_ref, state_ref, uw_ref, inv_ref, trans_ref, qe_ref, end_ref,
    x_ref, carry_ref,
):
    step = pl.program_id(0)
    rows_here = CHUNK * group
    conv_scratch(step == 0, proj_ref, prev_ref, halo_ref, x_ref, heads, rows_here)
    ri, ci = iotas(CHUNK)
    included = ri >= ci
    strictly = ri > ci
    lower = jnp.where(included, 1.0, 0.0)
    upper = jnp.where(ri <= ci, 1.0, 0.0)

    @pl.when(step == 0)
    def _():
        for h in range(heads):
            carry_ref[h, :DV, :] = jnp.zeros((DV, DK), F32)
            carry_ref[h, DV:, :] = jnp.where(ri == ci, 1.0, 0.0)

    pairs = [(g, h) for g in range(group) for h in range(heads)]
    logits = rates_ref[...] + bias_ref[...]
    log_decay = -softplus(logits)
    strength = sigmoid(logits)
    cums, cum_rows = [], []
    for g in range(group):
        part = log_decay[g * CHUNK : (g + 1) * CHUNK]
        cums.append(mmx(lower, part))
        cum_rows.append(mmx(part, upper, 0, 0))
    mats, scores, rhs, tails, scaled_q, finals = [], [], [], [], [], []
    for g, h in pairs:
        pre = conv_pre(x_ref, taps_ref, h, g * CHUNK)
        mixed = pre * sigmoid(pre)
        q = unit(mixed[:, :DK])[0] * DK ** (-0.5)
        k = unit(mixed[:, DK : 2 * DK])[0]
        v = mixed[:, 2 * DK :]
        cum = cums[g][:, 2 * h : 2 * h + 1]
        cum_row = cum_rows[g][2 * h : 2 * h + 1, :]
        beta = strength[g * CHUNK : (g + 1) * CHUNK, 2 * h + 1 : 2 * h + 2]
        growth = jnp.exp(cum)
        decays = jnp.where(included, jnp.exp(jnp.where(included, cum - cum_row, 0.0)), 0.0)
        grams = mm(jnp.concatenate([q, k], axis=0), k, 1, 1)
        scores.append(grams[:CHUNK] * decays)
        mats.append(jnp.where(strictly, beta * decays * grams[CHUNK:], 0.0))
        rhs.append(jnp.concatenate([beta * v, beta * growth * k], axis=1))
        last = cum[CHUNK - 1 : CHUNK, :]
        tails.append(k * jnp.exp(last - cum))
        scaled_q.append(growth * q)
        finals.append(jnp.exp(last))
    inverses = inverse_parts(mats, ri, ci)
    solved = [b + mm(r, b) for r, b in zip(inverses, rhs)]
    mixes = [mm(p, u) for p, u in zip(scores, solved)]
    adds = [mm(u, t, 0, 0) for u, t in zip(solved, tails)]
    for j, (g, h) in enumerate(pairs):
        inv_ref[h, g] = inverses[j].astype(BF16)
        uw_ref[h, g] = solved[j].astype(BF16)
        qe_ref[h, g] = (scaled_q[j] - mixes[j][:, DV:]).astype(BF16)
        trans_ref[h, g] = (-adds[j][DV:]).astype(BF16)
        olocal_ref[g * CHUNK : (g + 1) * CHUNK, h * DV : (h + 1) * DV] = mixes[j][:, :DV]
    for h in range(heads):
        now = carry_ref[h]
        for g in range(group):
            j = pairs.index((g, h))
            low = now.astype(BF16)
            state_ref[h, g] = low
            moved = finals[j] * now + mm(low, trans_ref[h, g])
            now = jnp.concatenate([moved[:DV] + adds[j][:DV], moved[DV:]], axis=0)
        carry_ref[h] = now
        end_ref[h] = now.astype(BF16)
    for j, (g, h) in enumerate(pairs):
        both = mm(qe_ref[h, g], state_ref[h, g], 1, 1)
        rows = slice(g * CHUNK, (g + 1) * CHUNK)
        olocal_ref[rows, h * DV : (h + 1) * DV] += both[:, :DV]
        qmap_ref[rows, h * DK : (h + 1) * DK] = both[:, DV:].astype(BF16)


def mixer_forward(projected, halo, rates, bias_row, taps, group):
    total = projected.shape[0]
    heads = rates.shape[1] // 2
    rows = CHUNK * group
    steps = total // rows
    chunks = total // CHUNK
    whole = lambda i: (0, 0)
    saved = lambda a, b: (
        jax.ShapeDtypeStruct((heads, chunks, a, b), BF16),
        pl.BlockSpec((heads, group, a, b), lambda i: (0, i, 0, 0)),
    )
    outs = [
        (jax.ShapeDtypeStruct((total, heads * DV), F32), pl.BlockSpec((rows, heads * DV), lambda i: (i, 0))),
        (jax.ShapeDtypeStruct((total, heads * DK), BF16), pl.BlockSpec((rows, heads * DK), lambda i: (i, 0))),
        saved(DV + DK, DK),
        saved(CHUNK, DV + DK),
        saved(CHUNK, CHUNK),
        saved(DK, DK),
        saved(CHUNK, DK),
        (jax.ShapeDtypeStruct((heads, DV + DK, DK), BF16), pl.BlockSpec((heads, DV + DK, DK), lambda i: (0, 0, 0))),
    ]
    return pl.pallas_call(
        functools.partial(forward_kernel, heads, group),
        grid=(steps,),
        in_specs=[
            pl.BlockSpec((rows, heads * PER), lambda i: (i, 0)),
            pl.BlockSpec((HALO, heads * PER), lambda i: (jnp.maximum(i * (rows // HALO) - 1, 0), 0)),
            pl.BlockSpec((HALO, heads * PER), whole),
            pl.BlockSpec((rows, 2 * heads), lambda i: (i, 0)),
            pl.BlockSpec((1, 2 * heads), whole),
            pl.BlockSpec((CONV, heads * MIX), whole),
        ],
        out_shape=[o[0] for o in outs],
        out_specs=[o[1] for o in outs],
        scratch_shapes=[
            pltpu.VMEM((rows + 8, heads * MIX), F32),
            pltpu.VMEM((heads, DV + DK, DK), F32),
        ],
        compiler_params=pltpu.CompilerParams(vmem_limit_bytes=VMEM_LIMIT),
        cost_estimate=pl.CostEstimate(flops=40_000_000_000, bytes_accessed=16_000_000, transcendentals=0),
    )(projected, projected, halo, rates, bias_row, taps)


def backward_kernel(
    heads, group, steps, peers,
    proj_ref, prev_ref, halo_ref, rates_ref, bias_ref, taps_ref,
    state_ref, uw_ref, inv_ref, trans_ref, qe_ref,
    dout_ref, ggate_ref, value_ref, incoming_ref, place_ref, maps_ref, local_ref,
    gp_ref, grates_ref, gtaps_ref, gbias_ref, tail_ref, lead_ref,
    x_ref, d_ref, carry_ref, next_ref,
):
    step = pl.program_id(0)
    rows_here = CHUNK * group
    conv_scratch(step == steps - 1, proj_ref, prev_ref, halo_ref, x_ref, heads, rows_here)
    ri, ci = iotas(CHUNK)
    included = ri >= ci
    strictly = ri > ci
    lower = jnp.where(included, 1.0, 0.0)
    upper = jnp.where(ri <= ci, 1.0, 0.0)

    @pl.when(step == 0)
    def _():
        for h in range(heads):
            grad = jnp.zeros((DV, DK), F32)
            for turn in range(peers - 1):
                source = peers - 1 - turn
                moved = mm(grad, maps_ref[source, h, DV:, :], 1, 1) + local_ref[source, h].astype(F32)
                grad = jnp.where(source > place_ref[0], moved, grad)
            carry_ref[h] = grad
        d_ref[rows_here : rows_here + 8, :] = jnp.zeros((8, heads * MIX), F32)
        gtaps_ref[...] = jnp.zeros_like(gtaps_ref)
        gbias_ref[...] = jnp.zeros_like(gbias_ref)

    @pl.when(step > 0)
    def _():
        d_ref[rows_here : rows_here + 8, :] = d_ref[0:8, :]

    pairs = [(g, h) for g in range(group) for h in range(heads)]
    logits = rates_ref[...] + bias_ref[...]
    log_decay = -softplus(logits)
    strength = sigmoid(logits)
    cums, cum_rows = [], []
    for g in range(group):
        part = log_decay[g * CHUNK : (g + 1) * CHUNK]
        cums.append(mmx(lower, part))
        cum_rows.append(mmx(part, upper, 0, 0))
    douts, injections = [], []
    for g, h in pairs:
        do = dout_ref[g * CHUNK : (g + 1) * CHUNK, h * DV : (h + 1) * DV]
        douts.append(do)
        injections.append(mm(do, qe_ref[h, g], 0, 0))
    for h in range(heads):
        now = carry_ref[h]
        for g in reversed(range(group)):
            j = pairs.index((g, h))
            last = cums[g][CHUNK - 1 : CHUNK, 2 * h : 2 * h + 1]
            next_ref[h, g] = now
            now = jnp.exp(last) * now + mm(now, trans_ref[h, g], 1, 1) + injections[j]
        carry_ref[h] = now
    lane = lax.broadcasted_iota(jnp.int32, (CHUNK, 2 * heads), 1)
    row_col = lax.broadcasted_iota(jnp.int32, (CHUNK, 1), 0)
    dcums = [jnp.zeros((CHUNK, 2 * heads), F32) for _ in range(group)]
    dlogits = [jnp.zeros((CHUNK, 2 * heads), F32) for _ in range(group)]
    for j, (g, h) in enumerate(pairs):
        pre = conv_pre(x_ref, taps_ref, h, g * CHUNK)
        sig = sigmoid(pre)
        mixed = pre * sig
        slope = sig * (1.0 + pre * (1.0 - sig))
        uq, rq = unit(mixed[:, :DK])
        q = uq * DK ** (-0.5)
        k, rk = unit(mixed[:, DK : 2 * DK])
        v = mixed[:, 2 * DK :]
        cum = cums[g][:, 2 * h : 2 * h + 1]
        cum_row = cum_rows[g][2 * h : 2 * h + 1, :]
        beta = strength[g * CHUNK : (g + 1) * CHUNK, 2 * h + 1 : 2 * h + 2]
        growth = jnp.exp(cum)
        decays = jnp.where(included, jnp.exp(jnp.where(included, cum - cum_row, 0.0)), 0.0)
        qb, kb = q.astype(BF16), k.astype(BF16)
        grams = mm(jnp.concatenate([qb, kb], axis=0), kb, 1, 1)
        scores = grams[:CHUNK] * decays
        last = cum[CHUNK - 1 : CHUNK, :]
        fade = jnp.exp(last - cum)
        tail = k * fade
        sl = state_ref[h, g]
        state = sl[:DV].astype(F32) + mm(incoming_ref[h], sl[DV:])
        after = next_ref[h, g]
        afterb = after.astype(BF16)
        stateb = state.astype(BF16)
        uw = uw_ref[h, g]
        errors = uw[:, :DV].astype(F32) - mm(uw[:, DV:], stateb, 1, 1)
        eb = errors.astype(BF16)
        do = douts[j]
        de = mm(scores, do, 0, 0) + mm(tail, afterb, 1, 1)
        db = de + mm(inv_ref[h, g], de, 0, 0)
        dbb = db.astype(BF16)
        stacked = jnp.concatenate([do, dbb], axis=0)
        against_e = mm(stacked, eb, 1, 1)
        against_s = mm(stacked, stateb)
        dp = against_e[:CHUNK]
        da = jnp.where(strictly, -against_e[CHUNK:], 0.0)
        dos = against_s[:CHUNK]
        dbs = against_s[CHUNK:]
        dpd = dp * decays
        dg = da * beta * decays
        dtail = mm(eb, afterb)
        dq = mm(dpd, kb) + growth * dos
        sym = dg + dg.T
        dk = (
            mm(jnp.concatenate([dpd.T, sym], axis=1), jnp.concatenate([qb, kb], axis=0))
            - beta * growth * dbs
            + fade * dtail
        )
        dv = beta * db
        dlogit = (1.0 - beta) * jnp.sum(db * errors, axis=1, keepdims=True)
        tdot = jnp.sum(tail * dtail, axis=1, keepdims=True)
        out = value_ref[g * CHUNK : (g + 1) * CHUNK, h * DV : (h + 1) * DV].astype(F32)
        dcum = jnp.sum(do.astype(F32) * out, axis=1, keepdims=True) - beta * jnp.sum(
            v * db, axis=1, keepdims=True
        )
        at_end = jnp.exp(last) * jnp.sum(jnp.sum(after * state, axis=1, keepdims=True), axis=0, keepdims=True) + jnp.sum(
            tdot, axis=0, keepdims=True
        )
        dcum = dcum + jnp.where(row_col == CHUNK - 1, at_end, 0.0)
        dcums[g] = jnp.where(lane == 2 * h, dcum, dcums[g])
        dlogits[g] = jnp.where(lane == 2 * h + 1, dlogit, dlogits[g])
        dq = dq * DK ** (-0.5)
        dmq = rq * (dq - uq * jnp.sum(uq * dq, axis=1, keepdims=True))
        dmk = rk * (dk - k * jnp.sum(k * dk, axis=1, keepdims=True))
        d_ref[g * CHUNK : (g + 1) * CHUNK, h * MIX : (h + 1) * MIX] = (
            jnp.concatenate([dmq, dmk, dv], axis=1) * slope
        )
    for g in range(group):
        rows = slice(g * CHUNK, (g + 1) * CHUNK)
        dld = mmx(upper, dcums[g])
        drate = jnp.where(lane % 2 == 0, -sigmoid(logits[rows]) * dld, dlogits[g])
        grates_ref[rows, :] = drate
        gbias_ref[...] += jnp.sum(drate, axis=0, keepdims=True)
    for g, h in pairs:
        cols = slice(h * MIX, (h + 1) * MIX)
        row = g * CHUNK
        dpre = d_ref[pl.ds(row, CHUNK), cols]
        total = None
        for i in range(CONV):
            gtaps_ref[i : i + 1, cols] += jnp.sum(
                dpre * x_ref[pl.ds(row + 8 - (CONV - 1) + i, CHUNK), cols], axis=0, keepdims=True
            )
            part = taps_ref[i : i + 1, cols] * d_ref[pl.ds(row + CONV - 1 - i, CHUNK), cols]
            total = part if total is None else total + part
        gp_ref[row : row + CHUNK, h * PER : h * PER + MIX] = total.astype(BF16)
        gp_ref[row : row + CHUNK, h * PER + MIX : (h + 1) * PER] = ggate_ref[
            row : row + CHUNK, h * DV : (h + 1) * DV
        ]
        if g == group - 1:
            @pl.when(step == 0)
            def _(total=total, cols=cols):
                tail_ref[:, cols] = total[CHUNK - HALO :]

    @pl.when(step == steps - 1)
    def _():
        lead_ref[...] = d_ref[0:8, :]


def mixer_backward(projected, halo, rates, bias_row, taps, saved, dout, ggate, value, incoming, place, maps, local, group):
    state, uw, inv, trans, qe = saved
    total = projected.shape[0]
    heads = rates.shape[1] // 2
    rows = CHUNK * group
    steps = total // rows
    whole = lambda i: (0, 0)
    flip = lambda i: (steps - 1 - i, 0)
    keep = lambda a, b: pl.BlockSpec((heads, group, a, b), lambda i: (0, steps - 1 - i, 0, 0))
    return pl.pallas_call(
        functools.partial(backward_kernel, heads, group, steps, maps.shape[0]),
        grid=(steps,),
        in_specs=[
            pl.BlockSpec((rows, heads * PER), flip),
            pl.BlockSpec((HALO, heads * PER), lambda i: (jnp.maximum((steps - 1 - i) * (rows // HALO) - 1, 0), 0)),
            pl.BlockSpec((HALO, heads * PER), whole),
            pl.BlockSpec((rows, 2 * heads), flip),
            pl.BlockSpec((1, 2 * heads), whole),
            pl.BlockSpec((CONV, heads * MIX), whole),
            keep(DV + DK, DK),
            keep(CHUNK, DV + DK),
            keep(CHUNK, CHUNK),
            keep(DK, DK),
            keep(CHUNK, DK),
            pl.BlockSpec((rows, heads * DV), flip),
            pl.BlockSpec((rows, heads * DV), flip),
            pl.BlockSpec((rows, heads * DV), flip),
            pl.BlockSpec(incoming.shape, lambda i: (0, 0, 0)),
            pl.BlockSpec(memory_space=pltpu.SMEM),
            pl.BlockSpec(maps.shape, lambda i: (0, 0, 0, 0)),
            pl.BlockSpec(local.shape, lambda i: (0, 0, 0, 0)),
        ],
        out_shape=[
            jax.ShapeDtypeStruct((total, heads * PER), BF16),
            jax.ShapeDtypeStruct((total, 2 * heads), F32),
            jax.ShapeDtypeStruct((CONV, heads * MIX), F32),
            jax.ShapeDtypeStruct((1, 2 * heads), F32),
            jax.ShapeDtypeStruct((HALO, heads * MIX), F32),
            jax.ShapeDtypeStruct((8, heads * MIX), F32),
        ],
        out_specs=[
            pl.BlockSpec((rows, heads * PER), flip),
            pl.BlockSpec((rows, 2 * heads), flip),
            pl.BlockSpec((CONV, heads * MIX), whole),
            pl.BlockSpec((1, 2 * heads), whole),
            pl.BlockSpec((HALO, heads * MIX), whole),
            pl.BlockSpec((8, heads * MIX), whole),
        ],
        scratch_shapes=[
            pltpu.VMEM((rows + 8, heads * MIX), F32),
            pltpu.VMEM((rows + 8, heads * MIX), F32),
            pltpu.VMEM((heads, DV, DK), F32),
            pltpu.VMEM((heads, group, DV, DK), F32),
        ],
        compiler_params=pltpu.CompilerParams(vmem_limit_bytes=VMEM_LIMIT),
        cost_estimate=pl.CostEstimate(flops=60_000_000_000, bytes_accessed=20_000_000, transcendentals=0),
    )(projected, projected, halo, rates, bias_row, taps, state, uw, inv, trans, qe, dout, ggate, value, incoming, place, maps, local)


def gate_kernel(
    heads, peers,
    ids_ref, place_ref, maps_ref, olocal_ref, qmap_ref, proj_ref, gain_ref, w_ref,
    value_ref, gated_ref, part_ref, incoming_ref,
):
    @pl.when(pl.program_id(0) == 0)
    def _():
        for h in range(heads):
            state = jnp.zeros((DV, DK), F32)
            for source in range(peers - 1):
                moved = mm(state, maps_ref[source, h, DV:, :]) + maps_ref[source, h, :DV, :].astype(F32)
                state = jnp.where(source < place_ref[0], moved, state)
            incoming_ref[h] = state.astype(BF16)

    for h in range(heads):
        cols = slice(h * DV, (h + 1) * DV)
        out = olocal_ref[:, cols] + mm(qmap_ref[:, h * DK : (h + 1) * DK], incoming_ref[h], 1, 1)
        low = out.astype(BF16)
        value_ref[:, cols] = low
        value = low.astype(F32)
        normed = value * lax.rsqrt(jnp.mean(value * value, axis=-1, keepdims=True) + epsilon)
        gate = proj_ref[:, h * PER + MIX : (h + 1) * PER].astype(F32)
        gated_ref[:, cols] = (normed * gain_ref[...] * (gate * sigmoid(gate))).astype(BF16)
    part_ref[...] = mm(gated_ref[...], w_ref[...]).astype(BF16)


def gate_output(ids, place, maps, out_local, query_map, projected, gain, w_out):
    heads = maps.shape[1]
    total = projected.shape[0]
    count = ids.shape[0]
    rows = total // count
    width = w_out.shape[1]
    theirs = lambda i, ids, place: (ids[i], 0)
    mine = lambda i, ids, place: (i, 0)
    whole = lambda i, ids, place: (0, 0)
    return pl.pallas_call(
        functools.partial(gate_kernel, heads, maps.shape[0]),
        grid_spec=pltpu.PrefetchScalarGridSpec(
            num_scalar_prefetch=2,
            grid=(count,),
            in_specs=[
                pl.BlockSpec(maps.shape, lambda i, ids, place: (0, 0, 0, 0)),
                pl.BlockSpec((rows, heads * DV), theirs),
                pl.BlockSpec((rows, heads * DK), theirs),
                pl.BlockSpec((rows, heads * PER), theirs),
                pl.BlockSpec((1, DV), whole),
                pl.BlockSpec(w_out.shape, whole),
            ],
            out_specs=[
                pl.BlockSpec((rows, heads * DV), theirs),
                pl.BlockSpec((rows, heads * DV), mine),
                pl.BlockSpec((rows, width), mine),
                pl.BlockSpec((heads, DV, DK), lambda i, ids, place: (0, 0, 0)),
            ],
        ),
        out_shape=[
            jax.ShapeDtypeStruct((total, heads * DV), BF16),
            jax.ShapeDtypeStruct((total, heads * DV), BF16),
            jax.ShapeDtypeStruct((total, width), BF16),
            jax.ShapeDtypeStruct((heads, DV, DK), BF16),
        ],
        compiler_params=pltpu.CompilerParams(vmem_limit_bytes=VMEM_LIMIT),
        cost_estimate=pl.CostEstimate(flops=8_000_000_000, bytes_accessed=16_000_000, transcendentals=0),
    )(ids, place, maps, out_local, query_map, projected, gain, w_out)


def gate_back_kernel(
    heads,
    ids_ref, branch_ref, w_ref, value_ref, proj_ref, qmap_ref, gain_ref,
    ggate_ref, dout_ref, gain_grad_ref, local_ref,
):
    @pl.when(pl.program_id(0) == 0)
    def _():
        gain_grad_ref[...] = jnp.zeros_like(gain_grad_ref)
        local_ref[...] = jnp.zeros_like(local_ref)

    grads = mm(branch_ref[...], w_ref[...], 1, 1)
    gain = gain_ref[...]
    for h in range(heads):
        cols = slice(h * DV, (h + 1) * DV)
        value = value_ref[:, cols].astype(F32)
        inverse = lax.rsqrt(jnp.mean(value * value, axis=-1, keepdims=True) + epsilon)
        normed = value * inverse
        gate = proj_ref[:, h * PER + MIX : (h + 1) * PER].astype(F32)
        sig = sigmoid(gate)
        grad = grads[:, cols]
        through = grad * (gate * sig)
        ggate_ref[:, cols] = (grad * normed * gain * (sig * (1.0 + gate * (1.0 - sig)))).astype(BF16)
        gain_grad_ref[...] += jnp.sum(through * normed, axis=0, keepdims=True)
        scaled = through * gain
        low = (inverse * (scaled - normed * jnp.mean(scaled * normed, axis=-1, keepdims=True))).astype(BF16)
        dout_ref[:, cols] = low
        local_ref[h] += mm(low, qmap_ref[:, h * DK : (h + 1) * DK], 0, 0)


def gate_backward(ids, branch, w_out, value, projected, query_map, gain, heads):
    total = projected.shape[0]
    count = ids.shape[0]
    rows = total // count
    theirs = lambda i, ids: (ids[i], 0)
    mine = lambda i, ids: (i, 0)
    whole = lambda i, ids: (0, 0)
    return pl.pallas_call(
        functools.partial(gate_back_kernel, heads),
        grid_spec=pltpu.PrefetchScalarGridSpec(
            num_scalar_prefetch=1,
            grid=(count,),
            in_specs=[
                pl.BlockSpec((rows, branch.shape[1]), mine),
                pl.BlockSpec(w_out.shape, whole),
                pl.BlockSpec((rows, heads * DV), theirs),
                pl.BlockSpec((rows, heads * PER), theirs),
                pl.BlockSpec((rows, heads * DK), theirs),
                pl.BlockSpec((1, DV), whole),
            ],
            out_specs=[
                pl.BlockSpec((rows, heads * DV), theirs),
                pl.BlockSpec((rows, heads * DV), theirs),
                pl.BlockSpec((1, DV), whole),
                pl.BlockSpec((heads, DV, DK), lambda i, ids: (0, 0, 0)),
            ],
        ),
        out_shape=[
            jax.ShapeDtypeStruct((total, heads * DV), BF16),
            jax.ShapeDtypeStruct((total, heads * DV), BF16),
            jax.ShapeDtypeStruct((1, DV), F32),
            jax.ShapeDtypeStruct((heads, DV, DK), F32),
        ],
        compiler_params=pltpu.CompilerParams(vmem_limit_bytes=VMEM_LIMIT),
        cost_estimate=pl.CostEstimate(flops=8_000_000_000, bytes_accessed=16_000_000, transcendentals=0),
    )(ids, branch, w_out, value, projected, query_map, gain)


def ring_order(count):
    return list(range(0, count, 2)) + list(range(1, count, 2))[::-1]


def ring_step(value, axis, step):
    order = ring_order(lax.axis_size(axis))
    count = len(order)
    return lax.ppermute(value, axis, [(order[i], order[(i + step) % count]) for i in range(count)])


def ring_ids(axis):
    order = ring_order(lax.axis_size(axis))
    count = len(order)
    place = {device: i for i, device in enumerate(order)}
    table = [[order[(place[device] + k) % count] for k in range(count)] for device in range(count)]
    return lax.dynamic_index_in_dim(jnp.array(table, jnp.int32), lax.axis_index(axis), 0, False)


def ring_gather(shard, axis):
    count = lax.axis_size(axis)
    half = shard.shape[0] // 2
    halves = []
    for part in range(2):
        piece = shard[part * half : (part + 1) * half]
        found = {0: piece}
        forward = backward = piece
        for s in range(1, count // 2):
            forward = ring_step(forward, axis, 1)
            backward = ring_step(backward, axis, -1)
            found[count - s] = forward
            found[s] = backward
        if count > 1:
            found[count // 2] = ring_step(forward if part == 0 else backward, axis, 1 if part == 0 else -1)
        halves.append(found)
    return halves


def gathered_near(halves):
    count = len(halves[0])
    return jnp.concatenate([found[k] for k in range(count) for found in halves], axis=0)


def gathered_whole(halves, ids):
    count = len(halves[0])
    half, width = halves[0][0].shape
    buffer = jnp.zeros((count * 2 * half, width), halves[0][0].dtype)
    for k in range(count):
        for part, found in enumerate(halves):
            buffer = lax.dynamic_update_slice(buffer, found[k], (ids[k] * (2 * half) + part * half, 0))
    return buffer


def ring_scatter(take, rows, axis):
    count = lax.axis_size(axis)
    half = rows // 2
    totals = []
    for part in range(2):
        piece = lambda k: take(k, part * half, half)
        forward = backward = None
        if count > 1:
            if part == 0:
                forward = ring_step(piece(count // 2), axis, 1)
            else:
                backward = ring_step(piece(count // 2), axis, -1)
        for s in range(count // 2 - 1, 0, -1):
            forward = piece(s) if forward is None else forward + piece(s)
            backward = piece(count - s) if backward is None else backward + piece(count - s)
            forward = ring_step(forward, axis, 1)
            backward = ring_step(backward, axis, -1)
        total = piece(0).astype(F32)
        for other in (forward, backward):
            if other is not None:
                total = total + other.astype(F32)
        totals.append(total)
    return jnp.concatenate(totals, axis=0)


def near_rows(array, rows):
    return lambda k, start, size: lax.slice_in_dim(array, k * rows + start, k * rows + start + size, axis=0)


def whole_rows(array, rows, ids):
    return lambda k, start, size: lax.dynamic_slice_in_dim(array, ids[k] * rows + start, size, 0)


def swap(value, axis, bit):
    count = lax.axis_size(axis)
    return lax.ppermute(value, axis, [(i, i ^ bit) for i in range(count)])


def pair_gather(shard, axis, dim):
    if lax.axis_size(axis) != 4:
        return lax.all_gather(shard, axis, axis=dim, tiled=True)
    me = lax.axis_index(axis)
    far = swap(shard, axis, 2)
    near = swap(shard, axis, 1)
    both = swap(far, axis, 1)
    size = shard.shape[dim]
    shape = list(shard.shape)
    shape[dim] = 4 * size
    buffer = jnp.zeros(shape, shard.dtype)
    for bit, piece in enumerate((shard, near, far, both)):
        buffer = lax.dynamic_update_slice_in_dim(buffer, piece, (me ^ bit) * size, dim)
    return buffer


def pair_scatter(array, axis, dim):
    if lax.axis_size(axis) != 4:
        return lax.psum_scatter(array, axis, scatter_dimension=dim, tiled=True).astype(F32)
    me = lax.axis_index(axis)
    size = array.shape[dim] // 4
    piece = lambda bit: lax.dynamic_slice_in_dim(array, (me ^ bit) * size, size, dim)
    across = swap(piece(3), axis, 1)
    near = swap(piece(1), axis, 1)
    far = swap(piece(2) + across, axis, 2)
    return piece(0).astype(F32) + near.astype(F32) + far.astype(F32)


def butterfly(value, axis):
    count = lax.axis_size(axis)
    bit = 1
    while bit < count:
        value = value + swap(value, axis, bit)
        bit *= 2
    return value


def after(value, *earlier):
    return lax.optimization_barrier((value, *earlier))[0]


def per_device(
    tokens,
    w_qkvg,
    w_rates,
    conv_weight,
    head_bias,
    norm_gain,
    head_gain,
    mlp_gain,
    w_out,
    w_ff_gate,
    w_ff_up,
    w_ff_down,
    cotangent,
):
    heads = head_bias.shape[1]
    own_rows = tokens.shape[0]
    contract = (((1,), (1,)), ((), ()))
    rows_first = (((0,), (0,)), ((), ()))
    dot = lambda a, b, dims: lax.dot_general(a, b, dims, preferred_element_type=F32)
    plain = (((1,), (0,)), ((), ()))
    ids = ring_ids("head")
    place = lax.axis_index("seq").reshape(1)
    gain_row = head_gain.reshape(1, DV)
    bias_row = head_bias.T.reshape(1, 2 * heads)

    inputs = tokens.astype(F32)
    inverse_one = lax.rsqrt(jnp.mean(inputs * inputs, axis=-1, keepdims=True) + epsilon)
    norm_normed = inputs * inverse_one
    normed_halves = ring_gather((norm_normed * norm_gain).astype(BF16), "head")
    w_mix = pair_gather(w_qkvg, "seq", 0)
    w_rate = pair_gather(w_rates.T, "seq", 1)
    out_rows = pair_gather(after(w_out, w_mix), "seq", 1)
    gate_w = pair_gather(after(w_ff_gate, out_rows), "seq", 1)
    up_w = pair_gather(after(w_ff_up, gate_w), "seq", 1)
    down_w = pair_gather(after(w_ff_down, up_w), "seq", 1)
    normed = gathered_whole(normed_halves, ids)
    seq_rows = normed.shape[0]
    cotangent_near = gathered_near(ring_gather(after(cotangent, normed), "head"))

    projected = dot(normed, w_mix, plain).astype(BF16)
    rates = dot(normed, w_rate, contract)
    halo_rows = shifted(projected[seq_rows - HALO :], "seq", 1)
    out_local, query_map, *saved, end_state = mixer_forward(
        projected, halo_rows, rates, bias_row, conv_weight, GROUP
    )
    maps = lax.all_gather(end_state, "seq")
    value, gated, branch_part, incoming = gate_output(
        ids, place, maps, out_local, query_map, projected, gain_row, out_rows
    )
    residual = inputs + ring_scatter(near_rows(branch_part, own_rows), own_rows, "head")
    inverse_two = lax.rsqrt(jnp.mean(residual * residual, axis=-1, keepdims=True) + epsilon)
    mlp_normed = residual * inverse_two
    mlp_near = gathered_near(ring_gather((mlp_normed * mlp_gain).astype(BF16), "head"))

    grad_hidden = dot(cotangent_near, down_w, contract)
    gate_pre = dot(mlp_near, gate_w, contract)
    up_pre = dot(mlp_near, up_w, contract)
    ff_sigmoid = jax.nn.sigmoid(gate_pre)
    ff_silu = gate_pre * ff_sigmoid
    hidden = (ff_silu * up_pre).astype(BF16)
    ff_slope = ff_sigmoid * (1.0 + gate_pre * (1.0 - ff_sigmoid))
    grad_gate_pre = (grad_hidden * up_pre * ff_slope).astype(BF16)
    grad_up_pre = (grad_hidden * ff_silu).astype(BF16)
    grad_mlp_part = (dot(grad_gate_pre, gate_w, plain) + dot(grad_up_pre, up_w, plain)).astype(BF16)
    grad_mlp_in = ring_scatter(near_rows(grad_mlp_part, own_rows), own_rows, "head")

    grad_down_s = pair_scatter(dot(hidden, cotangent_near, rows_first).astype(BF16), "seq", 1)
    grad_gate_s = pair_scatter(dot(grad_gate_pre, mlp_near, rows_first).astype(BF16), "seq", 1)
    grad_up_s = pair_scatter(dot(grad_up_pre, mlp_near, rows_first).astype(BF16), "seq", 1)

    mlp_gain_part = jnp.sum(grad_mlp_in * mlp_normed, axis=0)
    scaled_two = grad_mlp_in * mlp_gain
    grad_residual = cotangent.astype(F32) + inverse_two * (
        scaled_two - mlp_normed * jnp.mean(scaled_two * mlp_normed, axis=-1, keepdims=True)
    )
    branch_near = gathered_near(ring_gather(grad_residual.astype(BF16), "head"))
    grad_gate_mix, grad_mixer, head_gain_part, local_grad = gate_backward(
        ids, branch_near, out_rows, value, projected, query_map, gain_row, heads
    )
    locals_all = lax.all_gather(local_grad.astype(BF16), "seq")
    output_part = after(dot(hidden, down_w, plain).astype(BF16), branch_near)
    output = (residual + ring_scatter(near_rows(output_part, own_rows), own_rows, "head")).astype(BF16)
    grad_out_s = pair_scatter(dot(gated, branch_near, rows_first).astype(BF16), "seq", 1)

    grad_projected, grad_rates, grad_taps, grad_bias_row, tail_rows, lead_rows = mixer_backward(
        projected, halo_rows, rates, bias_row, conv_weight, saved,
        grad_mixer, grad_gate_mix, value, incoming, place, maps, locals_all, GROUP,
    )
    later_rows = shifted(lead_rows, "seq", -1)
    padded = jnp.concatenate([jnp.zeros((HALO, heads * MIX), F32), later_rows])
    last_rows = tail_rows + sum(
        conv_weight[i] * padded[CONV - 1 - i : CONV - 1 - i + HALO] for i in range(CONV)
    )
    for h in range(heads):
        grad_projected = lax.dynamic_update_slice(
            grad_projected, last_rows[:, h * MIX : (h + 1) * MIX].astype(BF16), (seq_rows - HALO, h * PER)
        )
    grad_rate_low = grad_rates.astype(BF16)
    grad_normed_part = (
        dot(grad_projected, w_mix, contract) + dot(grad_rate_low, w_rate, plain)
    ).astype(BF16)
    grad_normed = ring_scatter(whole_rows(grad_normed_part, own_rows, ids), own_rows, "head")
    grad_w_mix_s = pair_scatter(dot(normed, grad_projected, rows_first).astype(BF16), "seq", 0)
    grad_rate_t = dot(grad_rate_low, normed, rows_first)
    norm_gain_part = jnp.sum(grad_normed_part.astype(F32) * normed.astype(F32), axis=0) / norm_gain

    scaled_one = grad_normed * norm_gain
    grad_input = grad_residual + inverse_one * (
        scaled_one - norm_normed * jnp.mean(scaled_one * norm_normed, axis=-1, keepdims=True)
    )
    width = norm_gain.shape[0]
    flat = lambda a: jnp.pad(a.reshape(-1), (0, -a.size % 128)).reshape(-1, 128)
    seq_pack = [flat(a) for a in (grad_taps, grad_rate_t, grad_bias_row)]
    all_pack = [flat(a) for a in (norm_gain_part, mlp_gain_part, head_gain_part)]
    sizes = [a.shape[0] for a in seq_pack + all_pack]
    split = len(seq_pack)
    pack = butterfly(jnp.concatenate(seq_pack + all_pack, axis=0), "seq")
    cut = sum(sizes[:split])
    rest = butterfly(pack[cut:], "head")
    parts = []
    start = 0
    for i, size in enumerate(sizes):
        parts.append(pack[start : start + size] if i < split else rest[start - cut : start - cut + size])
        start += size
    conv_grad = parts[0].reshape(CONV, heads * MIX)
    rate_sum = parts[1].reshape(2 * heads, width)
    per_seq = w_rates.shape[0]
    grad_rates_s = lax.dynamic_slice_in_dim(rate_sum, lax.axis_index("seq") * per_seq, per_seq, 1).T
    bias_grad = parts[2].reshape(-1)[: 2 * heads].reshape(heads, 2).T
    return (
        output,
        grad_input,
        grad_w_mix_s,
        grad_rates_s,
        conv_grad,
        bias_grad,
        parts[3].reshape(width),
        parts[5].reshape(DV),
        parts[4].reshape(width),
        grad_out_s,
        grad_gate_s,
        grad_up_s,
        grad_down_s,
    )


def solution(mesh):
    in_specs = (
        P(("seq", "head"), None),
        P("seq", "head"),
        P("seq", "head"),
        P(None, "head"),
        P(None, "head"),
        P(),
        P(),
        P(),
        P("head", "seq"),
        P("head", "seq"),
        P("head", "seq"),
        P("head", "seq"),
        P(("seq", "head"), None),
    )
    out_specs = (
        P(("seq", "head"), None),
        P(("seq", "head"), None),
        P("seq", "head"),
        P("seq", "head"),
        P(None, "head"),
        P(None, "head"),
        P(),
        P(),
        P(),
        P("head", "seq"),
        P("head", "seq"),
        P("head", "seq"),
        P("head", "seq"),
    )
    return jax.shard_map(
        per_device, mesh=mesh, in_specs=in_specs, out_specs=out_specs, check_vma=False
    )
```

```python
import functools
import jax
import jax.numpy as jnp
from jax import lax
from jax.experimental import pallas as pl
from jax.experimental.pallas import tpu as pltpu
from jax.sharding import PartitionSpec as P

DK = 128
DV = 256
CONV = 4
CHUNK = 128
MIX = 2 * DK + DV
PER = 2 * DK + 2 * DV
GROUP = 4
epsilon = 1e-06
F32 = jnp.float32
BF16 = jnp.bfloat16
HALO = 16
VMEM_LIMIT = 56 * 1024 * 1024
LIGHT = pl.CostEstimate(flops=1, bytes_accessed=1, transcendentals=0)


def shifted(value, axis, steps):
    count = lax.axis_size(axis)
    leading, last = (max(0, -steps), min(count, count - steps))
    return lax.ppermute(value, axis, [(source, source + steps) for source in range(leading, last)])


def mm(a, b, ca=1, cb=0):
    return lax.dot_general(
        a.astype(BF16), b.astype(BF16), (((ca,), (cb,)), ((), ())), preferred_element_type=F32
    )


def mmx(a, b, ca=1, cb=0):
    return lax.dot_general(
        a, b, (((ca,), (cb,)), ((), ())), preferred_element_type=F32, precision=lax.Precision.HIGHEST
    )


def block_columns(spots_ref, b, width):
    return pl.ds(pl.multiple_of(spots_ref[b] * width, 128), width)


def softplus(x):
    return jnp.maximum(x, 0.0) + jnp.log1p(jnp.exp(-jnp.abs(x)))


def sigmoid(x):
    return 1.0 / (1.0 + jnp.exp(-x))


def iotas(n):
    return (
        lax.broadcasted_iota(jnp.int32, (n, n), 0),
        lax.broadcasted_iota(jnp.int32, (n, n), 1),
    )


def inverse_parts(mats, rows, cols):
    base = 16
    near = (rows // base) == (cols // base)
    diag = [jnp.where(near, a, 0.0) for a in mats]
    result = [-d for d in diag]
    power = [mm(d, d) for d in diag]
    span = 2
    while True:
        result = [r + p + mm(r, p) for r, p in zip(result, power)]
        span *= 2
        if span >= base:
            break
        power = [mm(p, p) for p in power]
    size = base
    n = mats[0].shape[0]
    while size < n:
        cross = ((rows // (2 * size)) == (cols // (2 * size))) & ((rows // size) != (cols // size))
        off = [jnp.where(cross, a, 0.0) for a in mats]
        left = [o + mm(r, o) for o, r in zip(off, result)]
        result = [r - x - mm(x, r) for r, x in zip(result, left)]
        size *= 2
    return result


def conv_scratch(first, proj_ref, prev_ref, halo_ref, x_ref, heads, rows):
    for h in range(heads):
        cols = slice(h * PER, h * PER + MIX)
        before = jnp.where(first, halo_ref[:, cols].astype(F32), prev_ref[:, cols].astype(F32))
        x_ref[0:8, h * MIX : (h + 1) * MIX] = before[HALO - 8 :]
        x_ref[8 : 8 + rows, h * MIX : (h + 1) * MIX] = proj_ref[:, cols].astype(F32)


def conv_pre(x_ref, taps_ref, h, row):
    cols = slice(h * MIX, (h + 1) * MIX)
    total = None
    for i in range(CONV):
        part = taps_ref[i : i + 1, cols] * x_ref[pl.ds(row + 8 - (CONV - 1) + i, CHUNK), cols]
        total = part if total is None else total + part
    return total


def unit(a):
    r = lax.rsqrt(jnp.sum(a * a, axis=-1, keepdims=True) + epsilon)
    return a * r, r


def forward_kernel(
    heads, group,
    proj_ref, prev_ref, halo_ref, rates_ref, bias_ref, taps_ref,
    olocal_ref, qmap_ref, state_ref, uw_ref, inv_ref, trans_ref, qe_ref, end_ref,
    x_ref, carry_ref,
):
    step = pl.program_id(0)
    rows_here = CHUNK * group
    conv_scratch(step == 0, proj_ref, prev_ref, halo_ref, x_ref, heads, rows_here)
    ri, ci = iotas(CHUNK)
    included = ri >= ci
    strictly = ri > ci
    lower = jnp.where(included, 1.0, 0.0)
    upper = jnp.where(ri <= ci, 1.0, 0.0)

    @pl.when(step == 0)
    def _():
        for h in range(heads):
            carry_ref[h, :DV, :] = jnp.zeros((DV, DK), F32)
            carry_ref[h, DV:, :] = jnp.where(ri == ci, 1.0, 0.0)

    pairs = [(g, h) for g in range(group) for h in range(heads)]
    logits = rates_ref[...] + bias_ref[...]
    log_decay = -softplus(logits)
    strength = sigmoid(logits)
    cums, cum_rows = [], []
    for g in range(group):
        part = log_decay[g * CHUNK : (g + 1) * CHUNK]
        cums.append(mmx(lower, part))
        cum_rows.append(mmx(part, upper, 0, 0))
    mats, scores, rhs, tails, scaled_q, finals = [], [], [], [], [], []
    for g, h in pairs:
        pre = conv_pre(x_ref, taps_ref, h, g * CHUNK)
        mixed = pre * sigmoid(pre)
        q = unit(mixed[:, :DK])[0] * DK ** (-0.5)
        k = unit(mixed[:, DK : 2 * DK])[0]
        v = mixed[:, 2 * DK :]
        cum = cums[g][:, 2 * h : 2 * h + 1]
        cum_row = cum_rows[g][2 * h : 2 * h + 1, :]
        beta = strength[g * CHUNK : (g + 1) * CHUNK, 2 * h + 1 : 2 * h + 2]
        growth = jnp.exp(cum)
        decays = jnp.where(included, jnp.exp(jnp.where(included, cum - cum_row, 0.0)), 0.0)
        grams = mm(jnp.concatenate([q, k], axis=0), k, 1, 1)
        scores.append(grams[:CHUNK] * decays)
        mats.append(jnp.where(strictly, beta * decays * grams[CHUNK:], 0.0))
        rhs.append(jnp.concatenate([beta * v, beta * growth * k], axis=1))
        last = cum[CHUNK - 1 : CHUNK, :]
        tails.append(k * jnp.exp(last - cum))
        scaled_q.append(growth * q)
        finals.append(jnp.exp(last))
    inverses = inverse_parts(mats, ri, ci)
    solved = [b + mm(r, b) for r, b in zip(inverses, rhs)]
    mixes = [mm(p, u) for p, u in zip(scores, solved)]
    adds = [mm(u, t, 0, 0) for u, t in zip(solved, tails)]
    for j, (g, h) in enumerate(pairs):
        inv_ref[h, g] = inverses[j].astype(BF16)
        uw_ref[h, g] = solved[j].astype(BF16)
        qe_ref[h, g] = (scaled_q[j] - mixes[j][:, DV:]).astype(BF16)
        trans_ref[h, g] = (-adds[j][DV:]).astype(BF16)
        olocal_ref[g * CHUNK : (g + 1) * CHUNK, h * DV : (h + 1) * DV] = mixes[j][:, :DV]
    for h in range(heads):
        now = carry_ref[h]
        for g in range(group):
            j = pairs.index((g, h))
            low = now.astype(BF16)
            state_ref[h, g] = low
            moved = finals[j] * now + mm(low, trans_ref[h, g])
            now = jnp.concatenate([moved[:DV] + adds[j][:DV], moved[DV:]], axis=0)
        carry_ref[h] = now
        end_ref[h] = now.astype(BF16)
    for j, (g, h) in enumerate(pairs):
        both = mm(qe_ref[h, g], state_ref[h, g], 1, 1)
        rows = slice(g * CHUNK, (g + 1) * CHUNK)
        olocal_ref[rows, h * DV : (h + 1) * DV] += both[:, :DV]
        qmap_ref[rows, h * DK : (h + 1) * DK] = both[:, DV:].astype(BF16)


def mixer_forward(projected, halo, rates, bias_row, taps, group):
    total = projected.shape[0]
    heads = rates.shape[1] // 2
    rows = CHUNK * group
    steps = total // rows
    chunks = total // CHUNK
    whole = lambda i: (0, 0)
    saved = lambda a, b: (
        jax.ShapeDtypeStruct((heads, chunks, a, b), BF16),
        pl.BlockSpec((heads, group, a, b), lambda i: (0, i, 0, 0)),
    )
    outs = [
        (jax.ShapeDtypeStruct((total, heads * DV), F32), pl.BlockSpec((rows, heads * DV), lambda i: (i, 0))),
        (jax.ShapeDtypeStruct((total, heads * DK), BF16), pl.BlockSpec((rows, heads * DK), lambda i: (i, 0))),
        saved(DV + DK, DK),
        saved(CHUNK, DV + DK),
        saved(CHUNK, CHUNK),
        saved(DK, DK),
        saved(CHUNK, DK),
        (jax.ShapeDtypeStruct((heads, DV + DK, DK), BF16), pl.BlockSpec((heads, DV + DK, DK), lambda i: (0, 0, 0))),
    ]
    return pl.pallas_call(
        functools.partial(forward_kernel, heads, group),
        grid=(steps,),
        in_specs=[
            pl.BlockSpec((rows, heads * PER), lambda i: (i, 0)),
            pl.BlockSpec((HALO, heads * PER), lambda i: (jnp.maximum(i * (rows // HALO) - 1, 0), 0)),
            pl.BlockSpec((HALO, heads * PER), whole),
            pl.BlockSpec((rows, 2 * heads), lambda i: (i, 0)),
            pl.BlockSpec((1, 2 * heads), whole),
            pl.BlockSpec((CONV, heads * MIX), whole),
        ],
        out_shape=[o[0] for o in outs],
        out_specs=[o[1] for o in outs],
        scratch_shapes=[
            pltpu.VMEM((rows + 8, heads * MIX), F32),
            pltpu.VMEM((heads, DV + DK, DK), F32),
        ],
        compiler_params=pltpu.CompilerParams(vmem_limit_bytes=VMEM_LIMIT),
        cost_estimate=LIGHT,
    )(projected, projected, halo, rates, bias_row, taps)


def backward_kernel(
    heads, group, steps, peers, own,
    proj_ref, prev_ref, halo_ref, rates_ref, bias_ref, taps_ref,
    state_ref, uw_ref, inv_ref, trans_ref, qe_ref,
    dout_ref, ggate_ref, value_ref, incoming_ref, place_ref, spots_ref, maps_ref, local_ref,
    gp_ref, grates_ref, sums_ref, tail_ref, lead_ref,
    x_ref, d_ref, carry_ref, next_ref,
):
    step = pl.program_id(0)
    rows_here = CHUNK * group
    conv_scratch(step == steps - 1, proj_ref, prev_ref, halo_ref, x_ref, heads, rows_here)
    ri, ci = iotas(CHUNK)
    included = ri >= ci
    strictly = ri > ci
    lower = jnp.where(included, 1.0, 0.0)
    upper = jnp.where(ri <= ci, 1.0, 0.0)

    @pl.when(step == 0)
    def _():
        for h in range(heads):
            grad = jnp.zeros((DV, DK), F32)
            for turn in range(peers - 1):
                source = peers - 1 - turn
                moved = mm(grad, maps_ref[source, h, DV:, :], 1, 1) + local_ref[source, h].astype(F32)
                grad = jnp.where(source > place_ref[0], moved, grad)
            carry_ref[h] = grad
        d_ref[rows_here : rows_here + 8, :] = jnp.zeros((8, heads * MIX), F32)
        sums_ref[...] = jnp.zeros_like(sums_ref)

    @pl.when(step > 0)
    def _():
        d_ref[rows_here : rows_here + 8, :] = d_ref[0:8, :]

    def near_row(g):
        first = ((steps - 1 - step) * group + g) * CHUNK
        return pl.multiple_of(spots_ref[first // own] * own + first % own, CHUNK)

    pairs = [(g, h) for g in range(group) for h in range(heads)]
    logits = rates_ref[...] + bias_ref[...]
    log_decay = -softplus(logits)
    strength = sigmoid(logits)
    cums, cum_rows = [], []
    for g in range(group):
        part = log_decay[g * CHUNK : (g + 1) * CHUNK]
        cums.append(mmx(lower, part))
        cum_rows.append(mmx(part, upper, 0, 0))
    douts, injections = [], []
    for g, h in pairs:
        do = dout_ref[g * CHUNK : (g + 1) * CHUNK, h * DV : (h + 1) * DV]
        douts.append(do)
        injections.append(mm(do, qe_ref[h, g], 0, 0))
    for h in range(heads):
        now = carry_ref[h]
        for g in reversed(range(group)):
            j = pairs.index((g, h))
            last = cums[g][CHUNK - 1 : CHUNK, 2 * h : 2 * h + 1]
            next_ref[h, g] = now
            now = jnp.exp(last) * now + mm(now, trans_ref[h, g], 1, 1) + injections[j]
        carry_ref[h] = now
    lane = lax.broadcasted_iota(jnp.int32, (CHUNK, 2 * heads), 1)
    row_col = lax.broadcasted_iota(jnp.int32, (CHUNK, 1), 0)
    dcums = [jnp.zeros((CHUNK, 2 * heads), F32) for _ in range(group)]
    dlogits = [jnp.zeros((CHUNK, 2 * heads), F32) for _ in range(group)]
    for j, (g, h) in enumerate(pairs):
        pre = conv_pre(x_ref, taps_ref, h, g * CHUNK)
        sig = sigmoid(pre)
        mixed = pre * sig
        slope = sig * (1.0 + pre * (1.0 - sig))
        uq, rq = unit(mixed[:, :DK])
        q = uq * DK ** (-0.5)
        k, rk = unit(mixed[:, DK : 2 * DK])
        v = mixed[:, 2 * DK :]
        cum = cums[g][:, 2 * h : 2 * h + 1]
        cum_row = cum_rows[g][2 * h : 2 * h + 1, :]
        beta = strength[g * CHUNK : (g + 1) * CHUNK, 2 * h + 1 : 2 * h + 2]
        growth = jnp.exp(cum)
        decays = jnp.where(included, jnp.exp(jnp.where(included, cum - cum_row, 0.0)), 0.0)
        qb, kb = q.astype(BF16), k.astype(BF16)
        grams = mm(jnp.concatenate([qb, kb], axis=0), kb, 1, 1)
        scores = grams[:CHUNK] * decays
        last = cum[CHUNK - 1 : CHUNK, :]
        fade = jnp.exp(last - cum)
        tail = k * fade
        sl = state_ref[h, g]
        state = sl[:DV].astype(F32) + mm(incoming_ref[h], sl[DV:])
        after = next_ref[h, g]
        afterb = after.astype(BF16)
        stateb = state.astype(BF16)
        uw = uw_ref[h, g]
        errors = uw[:, :DV].astype(F32) - mm(uw[:, DV:], stateb, 1, 1)
        eb = errors.astype(BF16)
        do = douts[j]
        de = mm(scores, do, 0, 0) + mm(tail, afterb, 1, 1)
        db = de + mm(inv_ref[h, g], de, 0, 0)
        dbb = db.astype(BF16)
        stacked = jnp.concatenate([do, dbb], axis=0)
        against_e = mm(stacked, eb, 1, 1)
        against_s = mm(stacked, stateb)
        dp = against_e[:CHUNK]
        da = jnp.where(strictly, -against_e[CHUNK:], 0.0)
        dos = against_s[:CHUNK]
        dbs = against_s[CHUNK:]
        dpd = dp * decays
        dg = da * beta * decays
        dtail = mm(eb, afterb)
        dq = mm(dpd, kb) + growth * dos
        sym = dg + dg.T
        dk = (
            mm(jnp.concatenate([dpd.T, sym], axis=1), jnp.concatenate([qb, kb], axis=0))
            - beta * growth * dbs
            + fade * dtail
        )
        dv = beta * db
        dlogit = (1.0 - beta) * jnp.sum(db * errors, axis=1, keepdims=True)
        tdot = jnp.sum(tail * dtail, axis=1, keepdims=True)
        out = value_ref[g * CHUNK : (g + 1) * CHUNK, h * DV : (h + 1) * DV].astype(F32)
        dcum = jnp.sum(do.astype(F32) * out, axis=1, keepdims=True) - beta * jnp.sum(
            v * db, axis=1, keepdims=True
        )
        at_end = jnp.exp(last) * jnp.sum(jnp.sum(after * state, axis=1, keepdims=True), axis=0, keepdims=True) + jnp.sum(
            tdot, axis=0, keepdims=True
        )
        dcum = dcum + jnp.where(row_col == CHUNK - 1, at_end, 0.0)
        dcums[g] = jnp.where(lane == 2 * h, dcum, dcums[g])
        dlogits[g] = jnp.where(lane == 2 * h + 1, dlogit, dlogits[g])
        dq = dq * DK ** (-0.5)
        dmq = rq * (dq - uq * jnp.sum(uq * dq, axis=1, keepdims=True))
        dmk = rk * (dk - k * jnp.sum(k * dk, axis=1, keepdims=True))
        d_ref[g * CHUNK : (g + 1) * CHUNK, h * MIX : (h + 1) * MIX] = (
            jnp.concatenate([dmq, dmk, dv], axis=1) * slope
        )
    for g in range(group):
        rows = slice(g * CHUNK, (g + 1) * CHUNK)
        dld = mmx(upper, dcums[g])
        drate = jnp.where(lane % 2 == 0, -sigmoid(logits[rows]) * dld, dlogits[g])
        grates_ref[pl.ds(near_row(g), CHUNK), :] = drate
        sums_ref[CONV : CONV + 1, : 2 * heads] += jnp.sum(drate, axis=0, keepdims=True)
    for g, h in pairs:
        cols = slice(h * MIX, (h + 1) * MIX)
        row = g * CHUNK
        dpre = d_ref[pl.ds(row, CHUNK), cols]
        total = None
        for i in range(CONV):
            sums_ref[i : i + 1, cols] += jnp.sum(
                dpre * x_ref[pl.ds(row + 8 - (CONV - 1) + i, CHUNK), cols], axis=0, keepdims=True
            )
            part = taps_ref[i : i + 1, cols] * d_ref[pl.ds(row + CONV - 1 - i, CHUNK), cols]
            total = part if total is None else total + part
        gp_ref[pl.ds(near_row(g), CHUNK), h * PER : h * PER + MIX] = total.astype(BF16)
        gp_ref[pl.ds(near_row(g), CHUNK), h * PER + MIX : (h + 1) * PER] = ggate_ref[
            row : row + CHUNK, h * DV : (h + 1) * DV
        ]
        if g == group - 1:
            @pl.when(step == 0)
            def _(total=total, cols=cols):
                tail_ref[:, cols] = total[CHUNK - HALO :]

    @pl.when(step == steps - 1)
    def _():
        lead_ref[...] = d_ref[0:8, :]


def mixer_backward(projected, halo, rates, bias_row, taps, saved, dout, ggate, value, incoming, place, spots, maps, local, group):
    state, uw, inv, trans, qe = saved
    total = projected.shape[0]
    heads = rates.shape[1] // 2
    rows = CHUNK * group
    steps = total // rows
    whole = lambda i: (0, 0)
    flip = lambda i: (steps - 1 - i, 0)
    keep = lambda a, b: pl.BlockSpec((heads, group, a, b), lambda i: (0, steps - 1 - i, 0, 0))
    return pl.pallas_call(
        functools.partial(backward_kernel, heads, group, steps, maps.shape[0], total // spots.shape[0]),
        grid=(steps,),
        in_specs=[
            pl.BlockSpec((rows, heads * PER), flip),
            pl.BlockSpec((HALO, heads * PER), lambda i: (jnp.maximum((steps - 1 - i) * (rows // HALO) - 1, 0), 0)),
            pl.BlockSpec((HALO, heads * PER), whole),
            pl.BlockSpec((rows, 2 * heads), flip),
            pl.BlockSpec((1, 2 * heads), whole),
            pl.BlockSpec((CONV, heads * MIX), whole),
            keep(DV + DK, DK),
            keep(CHUNK, DV + DK),
            keep(CHUNK, CHUNK),
            keep(DK, DK),
            keep(CHUNK, DK),
            pl.BlockSpec((rows, heads * DV), flip),
            pl.BlockSpec((rows, heads * DV), flip),
            pl.BlockSpec((rows, heads * DV), flip),
            pl.BlockSpec(incoming.shape, lambda i: (0, 0, 0)),
            pl.BlockSpec(memory_space=pltpu.SMEM),
            pl.BlockSpec(memory_space=pltpu.SMEM),
            pl.BlockSpec(maps.shape, lambda i: (0, 0, 0, 0)),
            pl.BlockSpec(local.shape, lambda i: (0, 0, 0, 0)),
        ],
        out_shape=[
            jax.ShapeDtypeStruct((total, heads * PER), BF16),
            jax.ShapeDtypeStruct((total, 2 * heads), F32),
            jax.ShapeDtypeStruct((8, heads * MIX), F32),
            jax.ShapeDtypeStruct((HALO, heads * MIX), F32),
            jax.ShapeDtypeStruct((8, heads * MIX), F32),
        ],
        out_specs=[
            pl.BlockSpec((total, heads * PER), whole),
            pl.BlockSpec((total, 2 * heads), whole),
            pl.BlockSpec((8, heads * MIX), whole),
            pl.BlockSpec((HALO, heads * MIX), whole),
            pl.BlockSpec((8, heads * MIX), whole),
        ],
        scratch_shapes=[
            pltpu.VMEM((rows + 8, heads * MIX), F32),
            pltpu.VMEM((rows + 8, heads * MIX), F32),
            pltpu.VMEM((heads, DV, DK), F32),
            pltpu.VMEM((heads, group, DV, DK), F32),
        ],
        compiler_params=pltpu.CompilerParams(vmem_limit_bytes=VMEM_LIMIT),
        cost_estimate=LIGHT,
    )(projected, projected, halo, rates, bias_row, taps, state, uw, inv, trans, qe, dout, ggate, value, incoming, place, spots, maps, local)


def gate_kernel(
    heads, peers,
    ids_ref, place_ref, maps_ref, olocal_ref, qmap_ref, proj_ref, gain_ref, *refs,
):
    *w_refs, value_ref, gated_ref, part_ref, incoming_ref = refs

    @pl.when(pl.program_id(0) == 0)
    def _():
        for h in range(heads):
            state = jnp.zeros((DV, DK), F32)
            for source in range(peers - 1):
                moved = mm(state, maps_ref[source, h, DV:, :]) + maps_ref[source, h, :DV, :].astype(F32)
                state = jnp.where(source < place_ref[0], moved, state)
            incoming_ref[h] = state.astype(BF16)

    for h in range(heads):
        cols = slice(h * DV, (h + 1) * DV)
        out = olocal_ref[:, cols] + mm(qmap_ref[:, h * DK : (h + 1) * DK], incoming_ref[h], 1, 1)
        low = out.astype(BF16)
        value_ref[:, cols] = low
        value = low.astype(F32)
        normed = value * lax.rsqrt(jnp.mean(value * value, axis=-1, keepdims=True) + epsilon)
        gate = proj_ref[:, h * PER + MIX : (h + 1) * PER].astype(F32)
        gated_ref[:, cols] = (normed * gain_ref[...] * (gate * sigmoid(gate))).astype(BF16)
    part_ref[...] = mm(gated_ref[...], w_refs[0][...]).astype(BF16)


def gate_output(ids, place, maps, out_local, query_map, projected, gain, w_out):
    heads = maps.shape[1]
    total = projected.shape[0]
    count = ids.shape[0]
    rows = total // count
    width = sum(w.shape[1] for w in w_out)
    theirs = lambda i, ids, place: (ids[i], 0)
    mine = lambda i, ids, place: (i, 0)
    whole = lambda i, ids, place: (0, 0)
    return pl.pallas_call(
        functools.partial(gate_kernel, heads, maps.shape[0]),
        grid_spec=pltpu.PrefetchScalarGridSpec(
            num_scalar_prefetch=2,
            grid=(count,),
            in_specs=[
                pl.BlockSpec(maps.shape, lambda i, ids, place: (0, 0, 0, 0)),
                pl.BlockSpec((rows, heads * DV), theirs),
                pl.BlockSpec((rows, heads * DK), theirs),
                pl.BlockSpec((rows, heads * PER), theirs),
                pl.BlockSpec((1, DV), whole),
                *[pl.BlockSpec(w.shape, whole) for w in w_out],
            ],
            out_specs=[
                pl.BlockSpec((rows, heads * DV), theirs),
                pl.BlockSpec((rows, heads * DV), mine),
                pl.BlockSpec((rows, width), mine),
                pl.BlockSpec((heads, DV, DK), lambda i, ids, place: (0, 0, 0)),
            ],
        ),
        out_shape=[
            jax.ShapeDtypeStruct((total, heads * DV), BF16),
            jax.ShapeDtypeStruct((total, heads * DV), BF16),
            jax.ShapeDtypeStruct((total, width), BF16),
            jax.ShapeDtypeStruct((heads, DV, DK), BF16),
        ],
        compiler_params=pltpu.CompilerParams(vmem_limit_bytes=VMEM_LIMIT),
        cost_estimate=LIGHT,
    )(ids, place, maps, out_local, query_map, projected, gain, *w_out)


def gate_back_kernel(
    heads,
    ids_ref, branch_ref, value_ref, proj_ref, qmap_ref, gain_ref, *refs,
):
    *w_refs, ggate_ref, dout_ref, gain_grad_ref, local_ref = refs

    @pl.when(pl.program_id(0) == 0)
    def _():
        gain_grad_ref[...] = jnp.zeros_like(gain_grad_ref)
        local_ref[...] = jnp.zeros_like(local_ref)

    grads = mm(branch_ref[...], w_refs[0][...], 1, 1)
    gain = gain_ref[...]
    for h in range(heads):
        cols = slice(h * DV, (h + 1) * DV)
        value = value_ref[:, cols].astype(F32)
        inverse = lax.rsqrt(jnp.mean(value * value, axis=-1, keepdims=True) + epsilon)
        normed = value * inverse
        gate = proj_ref[:, h * PER + MIX : (h + 1) * PER].astype(F32)
        sig = sigmoid(gate)
        grad = grads[:, cols]
        through = grad * (gate * sig)
        ggate_ref[:, cols] = (grad * normed * gain * (sig * (1.0 + gate * (1.0 - sig)))).astype(BF16)
        gain_grad_ref[...] += jnp.sum(through * normed, axis=0, keepdims=True)
        scaled = through * gain
        low = (inverse * (scaled - normed * jnp.mean(scaled * normed, axis=-1, keepdims=True))).astype(BF16)
        dout_ref[:, cols] = low
        local_ref[h] += mm(low, qmap_ref[:, h * DK : (h + 1) * DK], 0, 0)


def gate_backward(ids, branch, w_out, value, projected, query_map, gain, heads):
    total = projected.shape[0]
    count = ids.shape[0]
    rows = total // count
    theirs = lambda i, ids: (ids[i], 0)
    mine = lambda i, ids: (i, 0)
    whole = lambda i, ids: (0, 0)
    return pl.pallas_call(
        functools.partial(gate_back_kernel, heads),
        grid_spec=pltpu.PrefetchScalarGridSpec(
            num_scalar_prefetch=1,
            grid=(count,),
            in_specs=[
                pl.BlockSpec((rows, branch.shape[1]), mine),
                pl.BlockSpec((rows, heads * DV), theirs),
                pl.BlockSpec((rows, heads * PER), theirs),
                pl.BlockSpec((rows, heads * DK), theirs),
                pl.BlockSpec((1, DV), whole),
                *[pl.BlockSpec(w.shape, whole) for w in w_out],
            ],
            out_specs=[
                pl.BlockSpec((rows, heads * DV), theirs),
                pl.BlockSpec((rows, heads * DV), theirs),
                pl.BlockSpec((1, DV), whole),
                pl.BlockSpec((heads, DV, DK), lambda i, ids: (0, 0, 0)),
            ],
        ),
        out_shape=[
            jax.ShapeDtypeStruct((total, heads * DV), BF16),
            jax.ShapeDtypeStruct((total, heads * DV), BF16),
            jax.ShapeDtypeStruct((1, DV), F32),
            jax.ShapeDtypeStruct((heads, DV, DK), F32),
        ],
        compiler_params=pltpu.CompilerParams(vmem_limit_bytes=VMEM_LIMIT),
        cost_estimate=LIGHT,
    )(ids, branch, value, projected, query_map, gain, *w_out)


def project_kernel(layout, pieces, ids_ref, spots_ref, rate_ref, *refs):
    x_refs = refs[: len(layout)]
    w_refs = refs[len(layout) : len(layout) + pieces]
    out_ref, rates_ref = refs[len(layout) + pieces :]
    rows = out_ref.shape[0] // ids_ref.shape[0]
    blocks = {}
    for (k, _), ref in zip(layout, x_refs):
        blocks.setdefault(k, []).append(ref)
    ks = list(blocks)
    for first in range(0, len(ks), 2):
        group = ks[first : first + 2]
        group_refs = [ref for k in group for ref in blocks[k]]
        x = jnp.concatenate([ref[...] for ref in group_refs], axis=0)
        total = None
        for b, w_ref in enumerate(w_refs):
            cols = block_columns(spots_ref, b, w_ref.shape[0])
            share = mm(jnp.concatenate([ref[:, cols] for ref in group_refs], axis=0), w_ref[...])
            total = share if total is None else total + share
        total = total.astype(BF16)
        rates = mm(x, rate_ref[...], 1, 1)
        for i, k in enumerate(group):
            place = pl.ds(pl.multiple_of(ids_ref[k] * rows, rows), rows)
            out_ref[place, :] = total[i * rows : (i + 1) * rows]
            rates_ref[place, :] = rates[i * rows : (i + 1) * rows]


def layout_of(found, total):
    rows = found[0][0].shape[0]
    count = total // rows
    ks = [0] + [k for s in range(1, count // 2) for k in (s, count - s)] + [count // 2]
    layout, arrays = [], []
    for k in ks:
        start = k * rows
        for piece in found.get(k, ()):
            layout.append((k, start))
            arrays.append(piece)
            start += piece.shape[0]
    return layout, arrays


def project(ids, spots, found, w_mix, w_rate):
    total = ids.shape[0] * found[0][0].shape[0]
    layout, arrays = layout_of(found, total)
    cols = w_mix[0].shape[1]
    rates = w_rate.shape[0]
    whole = lambda shape: pl.BlockSpec(shape, lambda i, ids, spots: (0, 0))
    return pl.pallas_call(
        functools.partial(project_kernel, layout, len(w_mix)),
        grid_spec=pltpu.PrefetchScalarGridSpec(
            num_scalar_prefetch=2,
            grid=(1,),
            in_specs=[whole(a.shape) for a in (w_rate, *arrays, *w_mix)],
            out_specs=[whole((total, cols)), whole((total, rates))],
        ),
        out_shape=[
            jax.ShapeDtypeStruct((total, cols), BF16),
            jax.ShapeDtypeStruct((total, rates), F32),
        ],
        compiler_params=pltpu.CompilerParams(vmem_limit_bytes=VMEM_LIMIT),
        cost_estimate=LIGHT,
    )(ids, spots, w_rate, *arrays, *w_mix)


def normed_back_kernel(pieces, blocks, spots_ref, *refs):
    grads, rates, normed = refs[:blocks], refs[blocks : 2 * blocks], refs[2 * blocks : 3 * blocks]
    rate_ref, before_ref = refs[3 * blocks : 3 * blocks + 2]
    w_refs = refs[3 * blocks + 2 : 3 * blocks + 2 + pieces]
    part_ref, sums_ref = refs[3 * blocks + 2 + pieces :]
    left = jnp.concatenate([ref[...] for ref in grads], axis=0)
    rate = jnp.concatenate([ref[...].astype(BF16) for ref in rates], axis=0)
    count = rate.shape[1]
    sums_ref[...] = before_ref[...]
    for b, w_ref in enumerate(w_refs):
        cols = block_columns(spots_ref, b, w_ref.shape[0])
        part = mm(left, w_ref[...], 1, 1) + mm(rate, rate_ref[:, cols])
        part_ref[:, cols] = part.astype(BF16)
        right = jnp.concatenate([ref[:, cols] for ref in normed], axis=0)
        sums_ref[:count, cols] += mm(rate, right, 0, 0)
        sums_ref[4:5, cols] += jnp.sum(part * right.astype(F32), axis=0, keepdims=True)


def normed_back(spots, order, blocks, grad_projected, grad_rates, normed, w_mix, w_rate, before):
    total, width = normed.shape
    rows = total // blocks
    cols = w_mix[0].shape[1]
    rates = w_rate.shape[0]
    count = len(order)
    block = lambda k, wide: pl.BlockSpec((rows, wide), lambda i, spots: (k, 0))
    whole = lambda i, spots: (0, 0)
    return pl.pallas_call(
        functools.partial(normed_back_kernel, len(w_mix), count),
        grid_spec=pltpu.PrefetchScalarGridSpec(
            num_scalar_prefetch=1,
            grid=(1,),
            in_specs=[
                *[block(k, cols) for k in order],
                *[block(k, rates) for k in order],
                *[block(k, width) for k in order],
                pl.BlockSpec((rates, width), whole),
                pl.BlockSpec((8, width), whole),
                *[pl.BlockSpec(w.shape, whole) for w in w_mix],
            ],
            out_specs=[pl.BlockSpec((count * rows, width), whole), pl.BlockSpec((8, width), whole)],
        ),
        out_shape=[
            jax.ShapeDtypeStruct((count * rows, width), BF16),
            jax.ShapeDtypeStruct((8, width), F32),
        ],
        compiler_params=pltpu.CompilerParams(vmem_limit_bytes=VMEM_LIMIT),
        cost_estimate=LIGHT,
    )(
        spots,
        *[grad_projected] * count,
        *[grad_rates] * count,
        *[normed] * count,
        w_rate,
        before,
        *w_mix,
    )


def stack_kernel(layout, *refs):
    out_ref = refs[len(layout)]
    for (_, start), ref in zip(layout, refs):
        out_ref[start : start + ref.shape[0], :] = ref[...]


def stacked(found, total):
    layout, arrays = layout_of(found, total)
    return pl.pallas_call(
        functools.partial(stack_kernel, layout),
        out_shape=jax.ShapeDtypeStruct((total, arrays[0].shape[1]), arrays[0].dtype),
        compiler_params=pltpu.CompilerParams(vmem_limit_bytes=VMEM_LIMIT),
        cost_estimate=LIGHT,
    )(*arrays)


def finish_kernel(first_ref, second_ref, buffer_ref, out_ref):
    half = first_ref.shape[0]
    out_ref[:half, :] = first_ref[...]
    out_ref[half:, :] = second_ref[...]


def finish_stack(buffer, pieces, k):
    half, width = pieces[0].shape
    whole = pl.BlockSpec((half, width), lambda i: (0, 0))
    return pl.pallas_call(
        finish_kernel,
        grid=(1,),
        in_specs=[whole, whole, pl.BlockSpec(memory_space=pl.ANY)],
        out_specs=pl.BlockSpec((2 * half, width), lambda i: (k, 0)),
        out_shape=jax.ShapeDtypeStruct(buffer.shape, buffer.dtype),
        input_output_aliases={2: 0},
        cost_estimate=LIGHT,
    )(*pieces, buffer)


def outer_kernel(pieces, spots_ref, left_ref, right_ref, *outs):
    product = mm(left_ref[...], right_ref[...], 0, 0).astype(BF16)
    for b in range(pieces):

        @pl.when(pl.program_id(0) == b)
        def _(b=b):
            outs[b][...] = product


def outer(spots, left, right, part, parts):
    total, m = left.shape
    pieces = spots.shape[0]
    n = right.shape[1] // parts
    shape = (m // pieces, n)
    return pl.pallas_call(
        functools.partial(outer_kernel, pieces),
        grid_spec=pltpu.PrefetchScalarGridSpec(
            num_scalar_prefetch=1,
            grid=(pieces,),
            in_specs=[
                pl.BlockSpec((total, m // pieces), lambda i, spots: (0, spots[i])),
                pl.BlockSpec((total, n), lambda i, spots: (0, part)),
            ],
            out_specs=[pl.BlockSpec(shape, lambda i, spots: (0, 0))] * pieces,
        ),
        out_shape=[jax.ShapeDtypeStruct(shape, BF16)] * pieces,
        compiler_params=pltpu.CompilerParams(vmem_limit_bytes=VMEM_LIMIT),
        cost_estimate=LIGHT,
    )(spots, left, right)


def add_kernel(sizes, *refs):
    outs = refs[3 * sum(sizes) :]
    at = 0
    for out_ref, size in zip(outs, sizes):
        start = 0
        for _ in range(size):
            one, two, three = refs[at : at + 3]
            cols = slice(start, start + one.shape[1])
            out_ref[:, cols] = one[...].astype(F32) + two[...].astype(F32) + three[...].astype(F32)
            start += one.shape[1]
            at += 3


def add_all(groups):
    steps = 4
    flat = [a for group in groups for triple in group for a in triple]
    spec = lambda rows, wide: pl.BlockSpec((rows // steps, wide), lambda i: (i, 0))
    shapes = [(group[0][0].shape[0], sum(t[0].shape[1] for t in group)) for group in groups]
    return pl.pallas_call(
        functools.partial(add_kernel, [len(group) for group in groups]),
        grid=(steps,),
        in_specs=[spec(*a.shape) for a in flat],
        out_specs=[spec(*shape) for shape in shapes],
        out_shape=[jax.ShapeDtypeStruct(shape, F32) for shape in shapes],
        compiler_params=pltpu.CompilerParams(vmem_limit_bytes=VMEM_LIMIT),
        cost_estimate=LIGHT,
    )(*flat)
def ring_order(count):
    return list(range(0, count, 2)) + list(range(1, count, 2))[::-1]


def ring_step(value, axis, step):
    order = ring_order(lax.axis_size(axis))
    count = len(order)
    return lax.ppermute(value, axis, [(order[i], order[(i + step) % count]) for i in range(count)])


def ring_ids(axis):
    order = ring_order(lax.axis_size(axis))
    count = len(order)
    place = {device: i for i, device in enumerate(order)}
    ahead = [[order[(place[device] + k) % count] for k in range(count)] for device in range(count)]
    back = [[row.index(device) for device in range(count)] for row in ahead]
    row = lax.dynamic_index_in_dim(
        jnp.array([a + b for a, b in zip(ahead, back)], jnp.int32), lax.axis_index(axis), 0, False
    )
    return row[:count], row[count:]


def after(value, *earlier):
    return lax.optimization_barrier((value, *earlier))[0]


def together(*values):
    return lax.optimization_barrier(values)


def window(fillers, hop, gate):
    return fillers[hop](lambda value: after(value, gate)) if hop in fillers else ()


def ring_gather(shard, axis, fillers={}, stack=True):
    count = lax.axis_size(axis)
    far = count // 2
    half = shard.shape[0] // 2
    total = count * shard.shape[0]
    found = {0: [shard]}
    forward = backward = shard
    buffer = None
    for hop in range(1, far + 1):
        gate = forward
        extra = list(window(fillers, hop, gate))
        if hop < far:
            forward = ring_step(forward, axis, 1)
            backward = ring_step(backward, axis, -1)
            found[count - hop] = [forward]
            found[hop] = [backward]
        else:
            if stack:
                buffer = stacked({k: [after(p, gate) for p in ps] for k, ps in found.items()}, total)
                extra.append(buffer)
            forward = ring_step(forward[:half], axis, 1)
            backward = ring_step(backward[half:], axis, -1)
            found[hop] = [forward, backward]
        forward, backward, *_ = together(forward, backward, *extra)
    found[far] = [forward, backward]
    return finish_stack(buffer, found[far], far) if stack else found


def ring_scatter(take, rows, axis, fillers={}):
    count = lax.axis_size(axis)
    far = count // 2
    size = rows // 2
    flows = [[take(far, 0, size), None], [None, take(far, size, size)]]
    gate = take(far, 0, size)
    for hop in range(1, far + 1):
        flows = [
            [flow[way] if flow[way] is None else ring_step(flow[way], axis, 1 - 2 * way) for way in range(2)]
            for flow in flows
        ]
        extra = window(fillers, hop, gate)
        flat = together(*[a for flow in flows for a in flow if a is not None], *extra)
        flat = iter(flat)
        flows = [[None if a is None else next(flat) for a in flow] for flow in flows]
        s = far - hop
        if s:
            for part, flow in enumerate(flows):
                for way, k in enumerate((s, count - s)):
                    piece = take(k, part * size, size)
                    flow[way] = piece if flow[way] is None else flow[way] + piece
            gate = flows[0][0]
    totals = [
        take(0, part * size, size).astype(F32) + flow[0].astype(F32) + flow[1].astype(F32)
        for part, flow in enumerate(flows)
    ]
    return jnp.concatenate(totals, axis=0)


def near_rows(array, rows):
    return lambda k, start, size: lax.slice_in_dim(array, k * rows + start, k * rows + start + size, axis=0)


def swap(value, axis, bit):
    count = lax.axis_size(axis)
    return lax.ppermute(value, axis, [(i, i ^ bit) for i in range(count)])


def pair_spots(axis):
    count = lax.axis_size(axis)
    order = jnp.arange(count, dtype=jnp.int32)
    return lax.axis_index(axis) ^ order if count == 4 else order


def pair_far(shard, axis, *pins):
    if lax.axis_size(axis) != 4:
        return lax.all_gather(shard, axis)
    return swap(after(shard, *pins), axis, 2)


def pair_gather(shard, far, axis, *pins):
    count = lax.axis_size(axis)
    if count != 4:
        return [far[b] for b in range(count)]
    return [shard, swap(after(shard, *pins), axis, 1), far, swap(after(far, *pins), axis, 1)]


def pair_across(pieces, axis):
    if lax.axis_size(axis) != 4:
        return None
    return swap(pieces[3], axis, 1), swap(pieces[1], axis, 1)


def pair_far_sum(pieces, crossed, axis, pin):
    if crossed is None:
        return lax.psum_scatter(jnp.stack(pieces), axis, scatter_dimension=0)
    return swap(pin(pieces[2]) + crossed[0], axis, 2)


def round_sum(value, axis):
    count = lax.axis_size(axis)
    level = [value] + [swap(value, axis, bit) for bit in range(1, count)]
    while len(level) > 1:
        level = [level[i] + level[i + 1] for i in range(0, len(level), 2)]
    return level[0]


def per_device(
    tokens,
    w_qkvg,
    w_rates,
    conv_weight,
    head_bias,
    norm_gain,
    head_gain,
    mlp_gain,
    w_out,
    w_ff_gate,
    w_ff_up,
    w_ff_down,
    cotangent,
):
    heads = head_bias.shape[1]
    own_rows = tokens.shape[0]
    contract = (((1,), (1,)), ((), ()))
    rows_first = (((0,), (0,)), ((), ()))
    dot = lambda a, b, dims: lax.dot_general(a, b, dims, preferred_element_type=F32)
    plain = (((1,), (0,)), ((), ()))
    ids, near_spots = ring_ids("head")
    spots = pair_spots("seq")
    place = lax.axis_index("seq").reshape(1)
    gain_row = head_gain.reshape(1, DV)
    bias_row = head_bias.T.reshape(1, 2 * heads)
    peers = lax.axis_size("seq")
    width = tokens.shape[1]
    keep = {}
    mix_far = pair_far(w_qkvg, "seq")
    inputs = tokens.astype(F32)
    inverse_one = lax.rsqrt(jnp.mean(inputs * inputs, axis=-1, keepdims=True) + epsilon)
    norm_normed = inputs * inverse_one
    hops = lax.axis_size("head") // 2
    last_window = hops

    rate_shard = w_rates.T
    if peers == 4:
        w_rate = jnp.zeros((2 * heads, width), BF16)
        for b in range(4):
            w_rate = lax.dynamic_update_slice_in_dim(
                w_rate,
                swap(rate_shard, "seq", b) if b else rate_shard,
                (place[0] ^ b) * rate_shard.shape[1],
                1,
            )
    else:
        w_rate = lax.all_gather(rate_shard, "seq", axis=1, tiled=True)

    count = 2 * hops
    stages = 4
    cot_found = {0: [cotangent]}
    cot_state = [cotangent, cotangent]

    def cot_hop(hop, *gates):
        forward, backward, *_ = together(*cot_state, *gates)
        if hop < hops:
            forward, backward = ring_step(forward, "head", 1), ring_step(backward, "head", -1)
            cot_found[count - hop], cot_found[hop] = [forward], [backward]
        else:
            half = own_rows // 2
            forward = ring_step(forward[:half], "head", 1)
            backward = ring_step(backward[half:], "head", -1)
            cot_found[hop] = [forward, backward]
        cot_state[:] = [forward, backward]
        return list(cot_state)

    def fetch_mix(pin):
        keep["mix"] = pair_gather(w_qkvg, pin(mix_far), "seq")
        return keep["mix"]

    def cot_window(hop, other=lambda pin: []):
        def filler(pin):
            made = list(other(pin))
            forward, backward = cot_state
            cot_state[:] = [pin(forward), pin(backward)]
            return made + cot_hop(hop)

        return filler

    fillers = {last_window: cot_window(1)} | {last_window - 1: fetch_mix}
    normed_found = ring_gather((norm_normed * norm_gain).astype(BF16), "head", fillers, False)
    w_mix = keep["mix"]
    out_rows = lax.all_gather(after(w_out, mix_far), "seq", axis=1, tiled=True)

    stage_hops = {
        stage: range(2 + (hops - 1) * stage // 3, 2 + (hops - 1) * (stage + 1) // 3) for stage in range(3)
    }

    def cot_stage(stage, gate):
        made = []
        for hop in stage_hops[stage]:
            made = cot_hop(hop, gate)
        return made

    cot_stage(0, normed_found[hops][0])
    projected, rates = project(ids, spots, normed_found, w_mix, w_rate)
    seq_rows = projected.shape[0]
    halo_rows = shifted(projected[seq_rows - HALO :], "seq", 1)
    projected, *_ = together(projected, *cot_state)
    cot_stage(1, projected)
    out_local, query_map, *saved, end_state = mixer_forward(
        projected, halo_rows, rates, bias_row, conv_weight, GROUP
    )
    end_state, *_ = together(end_state, *cot_state)
    maps = lax.all_gather(end_state, "seq")
    cot_stage(2, maps)
    value, gated, branch_part, incoming = gate_output(
        ids, place, maps, out_local, query_map, projected, gain_row, [out_rows]
    )
    branch_part, *_ = together(branch_part, *cot_state)
    fetch = lambda w, *pins: lax.all_gather(after(w, *pins), "seq", axis=1, tiled=True)
    down_w = fetch(w_ff_down, maps)
    gate_w = fetch(w_ff_gate, maps)
    up_w = fetch(w_ff_up, maps)

    def stack_normed(pin):
        keep["normed"] = stacked({k: [pin(p) for p in ps] for k, ps in normed_found.items()}, seq_rows)
        return (keep["normed"],)

    def stack_cotangent(pin):
        keep["cot"] = stacked({k: [pin(p) for p in ps] for k, ps in cot_found.items()}, seq_rows)
        return (keep["cot"],)

    residual = inputs + ring_scatter(
        near_rows(branch_part, own_rows), own_rows, "head", {1: stack_cotangent, 2: stack_normed}
    )
    inverse_two = lax.rsqrt(jnp.mean(residual * residual, axis=-1, keepdims=True) + epsilon)
    mlp_normed = residual * inverse_two

    def hidden_gradient(pin):
        keep["gh"] = dot(pin(keep["cot"]), down_w, contract)
        return (keep["gh"],)

    mlp_near = ring_gather((mlp_normed * mlp_gain).astype(BF16), "head", {2: hidden_gradient})
    normed, cotangent_near, grad_hidden = keep["normed"], keep["cot"], keep["gh"]

    gate_pre = dot(mlp_near, gate_w, contract)
    up_pre = dot(mlp_near, up_w, contract)
    ff_sigmoid = jax.nn.sigmoid(gate_pre)
    ff_silu = gate_pre * ff_sigmoid
    hidden = (ff_silu * up_pre).astype(BF16)
    ff_slope = ff_sigmoid * (1.0 + gate_pre * (1.0 - ff_sigmoid))
    grad_gate_pre = (grad_hidden * up_pre * ff_slope).astype(BF16)
    grad_up_pre = (grad_hidden * ff_silu).astype(BF16)
    grad_mlp_part = (dot(grad_gate_pre, gate_w, plain) + dot(grad_up_pre, up_w, plain)).astype(BF16)

    def weight_product(name, left, right):
        def filler(pin):
            keep[name] = dot(pin(left), right, rows_first).astype(BF16)
            return (keep[name],)

        return filler

    scatter = lambda a: lax.psum_scatter(a, "seq", scatter_dimension=1, tiled=True).astype(F32)

    def output_rows(pin):
        keep["output"] = dot(pin(hidden), down_w, plain).astype(BF16)
        return (keep["output"],)

    grad_mlp_in = ring_scatter(
        near_rows(grad_mlp_part, own_rows),
        own_rows,
        "head",
        {
            1: weight_product("down", hidden, cotangent_near),
            2: weight_product("gate", grad_gate_pre, mlp_near),
            3: weight_product("up", grad_up_pre, mlp_near),
            4: output_rows,
        },
    )

    output_part = keep["output"]
    mlp_gain_part = jnp.sum(grad_mlp_in * mlp_normed, axis=0)
    scaled_two = grad_mlp_in * mlp_gain
    grad_residual = cotangent.astype(F32) + inverse_two * (
        scaled_two - mlp_normed * jnp.mean(scaled_two * mlp_normed, axis=-1, keepdims=True)
    )

    def total_all(groups, pin=lambda value: value):
        if peers == 4:
            sums = add_all(
                [[(keep[n][0], keep[n, "crossed"][1], pin(keep[n, "far"])) for n in group] for group in groups]
            )
        else:
            sums = [
                jnp.concatenate([keep[n, "far"].astype(F32) for n in group], axis=1) for group in groups
            ]
        for group, value in zip(groups, sums):
            keep[group[0], "total"] = value
        return sums

    def far_sums(*names):
        def filler(pin):
            for name in names:
                keep[name, "far"] = pair_far_sum(keep[name], keep[name, "crossed"], "seq", pin)
            return [keep[name, "far"] for name in names]

        return filler

    grad_down_s = scatter(keep["down"])
    grad_gate_s = scatter(keep["gate"])
    grad_up_s = scatter(keep["up"])
    branch_near = ring_gather(grad_residual.astype(BF16), "head")
    take_output = near_rows(output_part, own_rows)
    output_state = [None, None]
    known = lambda: [a for a in output_state if a is not None]

    def output_hops(stage, *gates):
        for hop in range(hops * (stage - 1) // stages, hops * stage // stages):
            here = []
            for way, k in enumerate((hops - hop, count - hops + hop)):
                if hop == 0 and way == 1:
                    here.append(None)
                    continue
                piece = take_output(k, 0, own_rows)
                total = piece if output_state[way] is None else output_state[way] + piece
                here.append(ring_step(after(total, *gates), "head", 1 - 2 * way))
            output_state[:] = here

    output_hops(1, branch_near)
    grad_gate_mix, grad_mixer, head_gain_part, local_grad = gate_backward(
        ids, branch_near, [out_rows], value, projected, query_map, gain_row, heads
    )
    local_low, *_ = together(local_grad.astype(BF16), *known())
    output_hops(2, local_low)
    locals_all = lax.all_gather(local_low, "seq")
    grad_projected, grad_rates, seq_sums, tail_rows, lead_rows = mixer_backward(
        projected, halo_rows, rates, bias_row, conv_weight, saved,
        grad_mixer, grad_gate_mix, value, incoming, place, near_spots, maps, locals_all, GROUP,
    )
    grad_projected, *_ = together(grad_projected, *known())
    later_rows = shifted(lead_rows, "seq", -1)
    output_hops(3, grad_projected)
    grad_out_w = dot(after(gated, lead_rows), branch_near, rows_first).astype(BF16)
    grad_projected, grad_out_w = together(grad_projected, grad_out_w)
    grad_out_s = scatter(grad_out_w)
    padded = jnp.concatenate([jnp.zeros((HALO, heads * MIX), F32), later_rows])
    last_rows = tail_rows + sum(
        conv_weight[i] * padded[CONV - 1 - i : CONV - 1 - i + HALO] for i in range(CONV)
    )
    last_start = near_spots[count - 1] * own_rows + own_rows - HALO
    for h in range(heads):
        grad_projected = lax.dynamic_update_slice(
            grad_projected, last_rows[:, h * MIX : (h + 1) * MIX].astype(BF16), (last_start, h * PER)
        )
    early = [hops] + ([hops - 1, hops + 1] if hops > 1 else [])
    late = [k for s in range(hops - 2, 0, -1) for k in (s, count - s)] + [0]
    place_of = {k: (0, i) for i, k in enumerate(early)} | {k: (1, i) for i, k in enumerate(late)}
    parts = []
    part, sums = normed_back(
        spots, early, count, grad_projected, grad_rates, normed, w_mix, w_rate, jnp.zeros((8, width), F32)
    )
    parts.append(part)

    def take(k, start, size):
        which, i = place_of[k]
        return lax.slice_in_dim(parts[which], i * own_rows + start, i * own_rows + start + size, axis=0)

    def late_rows(pin):
        part, keep["sums"] = normed_back(
            spots, late, count, pin(grad_projected), grad_rates, normed, w_mix, w_rate, sums
        )
        parts.append(part)
        return (part,)

    mixes = [("mix", h) for h in range(heads)]

    def first_window(pin):
        output_hops(4, pin(part))
        return (*late_rows(pin), *known())

    def second_window(pin):
        keep[mixes[0]] = outer(spots, normed, pin(grad_projected), 0, heads)
        keep[mixes[0], "crossed"] = pair_across(keep[mixes[0]], "seq")
        sums = pin(keep["sums"])
        gains = jnp.concatenate([sums[4:5], mlp_gain_part[None], head_gain_part], axis=1)
        keep["gains"] = round_sum(gains, "head")
        keep["small"] = jnp.concatenate([sums, seq_sums], axis=1)
        return (*keep[mixes[0]], keep["gains"], keep["small"])

    def third_window(pin):
        made = []
        for h, name in enumerate(mixes[1:]):
            keep[name] = outer(spots, normed, pin(grad_projected), h + 1, heads)
            keep[name, "crossed"] = pair_across(keep[name], "seq")
            made += keep[name]
        keep["gains"] = round_sum(pin(keep["gains"]), "seq")
        keep["small"] = round_sum(pin(keep["small"]), "seq")
        far_sums(mixes[0])(pin)
        return (*made, keep["gains"], keep["small"])

    def fourth_window(pin):
        far_sums(*mixes[1:])(pin)
        return [keep[mixes[0], "far"]]

    grad_normed = ring_scatter(
        take, own_rows, "head", {1: first_window, 2: second_window, 3: third_window, 4: fourth_window}
    )
    scaled_one = grad_normed * norm_gain
    grad_input = grad_residual + inverse_one * (
        scaled_one - norm_normed * jnp.mean(scaled_one * norm_normed, axis=-1, keepdims=True)
    )
    output = (
        residual + sum(a.astype(F32) for a in known()) + take_output(0, 0, own_rows).astype(F32)
    ).astype(BF16)
    pin = lambda value: after(value, grad_normed)
    total_all([mixes])
    small, gains = keep["small"], keep["gains"]
    per_seq = w_rates.shape[0]
    return (
        output,
        grad_input,
        keep[mixes[0], "total"],
        lax.dynamic_slice_in_dim(small[: 2 * heads], place[0] * per_seq, per_seq, 1).T,
        small[:CONV, width:],
        small[CONV, width : width + 2 * heads].reshape(heads, 2).T,
        gains[0, :width] / norm_gain,
        gains[0, 2 * width :],
        gains[0, width : 2 * width],
        grad_out_s,
        grad_gate_s,
        grad_up_s,
        grad_down_s,
    )


def solution(mesh):
    in_specs = (
        P(("seq", "head"), None),
        P("seq", "head"),
        P("seq", "head"),
        P(None, "head"),
        P(None, "head"),
        P(),
        P(),
        P(),
        P("head", "seq"),
        P("head", "seq"),
        P("head", "seq"),
        P("head", "seq"),
        P(("seq", "head"), None),
    )
    out_specs = (
        P(("seq", "head"), None),
        P(("seq", "head"), None),
        P("seq", "head"),
        P("seq", "head"),
        P(None, "head"),
        P(None, "head"),
        P(),
        P(),
        P(),
        P("head", "seq"),
        P("head", "seq"),
        P("head", "seq"),
        P("head", "seq"),
    )
    return jax.shard_map(
        per_device, mesh=mesh, in_specs=in_specs, out_specs=out_specs, check_vma=False
    )
```

```python
import functools
import jax
import jax.numpy as jnp
from jax import lax
from jax.experimental import pallas as pl
from jax.experimental.pallas import tpu as pltpu
from jax.sharding import PartitionSpec as P

DK = 128
DV = 256
CONV = 4
CHUNK = 128
MIX = 2 * DK + DV
PER = 2 * DK + 2 * DV
GROUP = 4
epsilon = 1e-06
F32 = jnp.float32
BF16 = jnp.bfloat16
HALO = 16
VMEM_LIMIT = 56 * 1024 * 1024
LIGHT = pl.CostEstimate(flops=1, bytes_accessed=1, transcendentals=0)


def shifted(value, axis, steps):
    count = lax.axis_size(axis)
    leading, last = (max(0, -steps), min(count, count - steps))
    return lax.ppermute(value, axis, [(source, source + steps) for source in range(leading, last)])


def mm(a, b, ca=1, cb=0):
    return lax.dot_general(
        a.astype(BF16), b.astype(BF16), (((ca,), (cb,)), ((), ())), preferred_element_type=F32
    )


def mmx(a, b, ca=1, cb=0):
    return lax.dot_general(
        a, b, (((ca,), (cb,)), ((), ())), preferred_element_type=F32, precision=lax.Precision.HIGHEST
    )


def block_columns(spots_ref, b, width):
    return pl.ds(pl.multiple_of(spots_ref[b] * width, 128), width)


def softplus(x):
    return jnp.maximum(x, 0.0) + jnp.log1p(jnp.exp(-jnp.abs(x)))


def sigmoid(x):
    return 1.0 / (1.0 + jnp.exp(-x))


def iotas(n):
    return (
        lax.broadcasted_iota(jnp.int32, (n, n), 0),
        lax.broadcasted_iota(jnp.int32, (n, n), 1),
    )


def inverse_parts(mats, rows, cols):
    base = 16
    near = (rows // base) == (cols // base)
    diag = [jnp.where(near, a, 0.0) for a in mats]
    result = [-d for d in diag]
    power = [mm(d, d) for d in diag]
    span = 2
    while True:
        result = [r + p + mm(r, p) for r, p in zip(result, power)]
        span *= 2
        if span >= base:
            break
        power = [mm(p, p) for p in power]
    size = base
    n = mats[0].shape[0]
    while size < n:
        cross = ((rows // (2 * size)) == (cols // (2 * size))) & ((rows // size) != (cols // size))
        off = [jnp.where(cross, a, 0.0) for a in mats]
        left = [o + mm(r, o) for o, r in zip(off, result)]
        result = [r - x - mm(x, r) for r, x in zip(result, left)]
        size *= 2
    return result


def conv_scratch(first, proj_ref, prev_ref, halo_ref, x_ref, heads, rows):
    for h in range(heads):
        cols = slice(h * PER, h * PER + MIX)
        before = jnp.where(first, halo_ref[:, cols].astype(F32), prev_ref[:, cols].astype(F32))
        x_ref[0:8, h * MIX : (h + 1) * MIX] = before[HALO - 8 :]
        x_ref[8 : 8 + rows, h * MIX : (h + 1) * MIX] = proj_ref[:, cols].astype(F32)


def conv_pre(x_ref, taps_ref, h, row):
    cols = slice(h * MIX, (h + 1) * MIX)
    total = None
    for i in range(CONV):
        part = taps_ref[i : i + 1, cols] * x_ref[pl.ds(row + 8 - (CONV - 1) + i, CHUNK), cols]
        total = part if total is None else total + part
    return total


def unit(a):
    r = lax.rsqrt(jnp.sum(a * a, axis=-1, keepdims=True) + epsilon)
    return a * r, r


def forward_kernel(
    heads, group,
    proj_ref, prev_ref, halo_ref, rates_ref, bias_ref, taps_ref,
    olocal_ref, qmap_ref, state_ref, uw_ref, inv_ref, trans_ref, qe_ref, end_ref,
    x_ref, carry_ref,
):
    step = pl.program_id(0)
    rows_here = CHUNK * group
    conv_scratch(step == 0, proj_ref, prev_ref, halo_ref, x_ref, heads, rows_here)
    ri, ci = iotas(CHUNK)
    included = ri >= ci
    strictly = ri > ci
    lower = jnp.where(included, 1.0, 0.0)
    upper = jnp.where(ri <= ci, 1.0, 0.0)

    @pl.when(step == 0)
    def _():
        for h in range(heads):
            carry_ref[h, :DV, :] = jnp.zeros((DV, DK), F32)
            carry_ref[h, DV:, :] = jnp.where(ri == ci, 1.0, 0.0)

    pairs = [(g, h) for g in range(group) for h in range(heads)]
    logits = rates_ref[...] + bias_ref[...]
    log_decay = -softplus(logits)
    strength = sigmoid(logits)
    cums, cum_rows = [], []
    for g in range(group):
        part = log_decay[g * CHUNK : (g + 1) * CHUNK]
        cums.append(mmx(lower, part))
        cum_rows.append(mmx(part, upper, 0, 0))
    mats, scores, rhs, tails, scaled_q, finals = [], [], [], [], [], []
    for g, h in pairs:
        pre = conv_pre(x_ref, taps_ref, h, g * CHUNK)
        mixed = pre * sigmoid(pre)
        q = unit(mixed[:, :DK])[0] * DK ** (-0.5)
        k = unit(mixed[:, DK : 2 * DK])[0]
        v = mixed[:, 2 * DK :]
        cum = cums[g][:, 2 * h : 2 * h + 1]
        cum_row = cum_rows[g][2 * h : 2 * h + 1, :]
        beta = strength[g * CHUNK : (g + 1) * CHUNK, 2 * h + 1 : 2 * h + 2]
        growth = jnp.exp(cum)
        decays = jnp.where(included, jnp.exp(jnp.where(included, cum - cum_row, 0.0)), 0.0)
        grams = mm(jnp.concatenate([q, k], axis=0), k, 1, 1)
        scores.append(grams[:CHUNK] * decays)
        mats.append(jnp.where(strictly, beta * decays * grams[CHUNK:], 0.0))
        rhs.append(jnp.concatenate([beta * v, beta * growth * k], axis=1))
        last = cum[CHUNK - 1 : CHUNK, :]
        tails.append(k * jnp.exp(last - cum))
        scaled_q.append(growth * q)
        finals.append(jnp.exp(last))
    inverses = inverse_parts(mats, ri, ci)
    solved = [b + mm(r, b) for r, b in zip(inverses, rhs)]
    mixes = [mm(p, u) for p, u in zip(scores, solved)]
    adds = [mm(u, t, 0, 0) for u, t in zip(solved, tails)]
    for j, (g, h) in enumerate(pairs):
        inv_ref[h, g] = inverses[j].astype(BF16)
        uw_ref[h, g] = solved[j].astype(BF16)
        qe_ref[h, g] = (scaled_q[j] - mixes[j][:, DV:]).astype(BF16)
        trans_ref[h, g] = (-adds[j][DV:]).astype(BF16)
        olocal_ref[g * CHUNK : (g + 1) * CHUNK, h * DV : (h + 1) * DV] = mixes[j][:, :DV]
    for h in range(heads):
        now = carry_ref[h]
        for g in range(group):
            j = pairs.index((g, h))
            low = now.astype(BF16)
            state_ref[h, g] = low
            moved = finals[j] * now + mm(low, trans_ref[h, g])
            now = jnp.concatenate([moved[:DV] + adds[j][:DV], moved[DV:]], axis=0)
        carry_ref[h] = now
        end_ref[h] = now.astype(BF16)
    for j, (g, h) in enumerate(pairs):
        both = mm(qe_ref[h, g], state_ref[h, g], 1, 1)
        rows = slice(g * CHUNK, (g + 1) * CHUNK)
        olocal_ref[rows, h * DV : (h + 1) * DV] += both[:, :DV]
        qmap_ref[rows, h * DK : (h + 1) * DK] = both[:, DV:].astype(BF16)


def mixer_forward(projected, halo, rates, bias_row, taps, group):
    total = projected.shape[0]
    heads = rates.shape[1] // 2
    rows = CHUNK * group
    steps = total // rows
    chunks = total // CHUNK
    whole = lambda i: (0, 0)
    saved = lambda a, b: (
        jax.ShapeDtypeStruct((heads, chunks, a, b), BF16),
        pl.BlockSpec((heads, group, a, b), lambda i: (0, i, 0, 0)),
    )
    outs = [
        (jax.ShapeDtypeStruct((total, heads * DV), F32), pl.BlockSpec((rows, heads * DV), lambda i: (i, 0))),
        (jax.ShapeDtypeStruct((total, heads * DK), BF16), pl.BlockSpec((rows, heads * DK), lambda i: (i, 0))),
        saved(DV + DK, DK),
        saved(CHUNK, DV + DK),
        saved(CHUNK, CHUNK),
        saved(DK, DK),
        saved(CHUNK, DK),
        (jax.ShapeDtypeStruct((heads, DV + DK, DK), BF16), pl.BlockSpec((heads, DV + DK, DK), lambda i: (0, 0, 0))),
    ]
    return pl.pallas_call(
        functools.partial(forward_kernel, heads, group),
        grid=(steps,),
        in_specs=[
            pl.BlockSpec((rows, heads * PER), lambda i: (i, 0)),
            pl.BlockSpec((HALO, heads * PER), lambda i: (jnp.maximum(i * (rows // HALO) - 1, 0), 0)),
            pl.BlockSpec((HALO, heads * PER), whole),
            pl.BlockSpec((rows, 2 * heads), lambda i: (i, 0)),
            pl.BlockSpec((1, 2 * heads), whole),
            pl.BlockSpec((CONV, heads * MIX), whole),
        ],
        out_shape=[o[0] for o in outs],
        out_specs=[o[1] for o in outs],
        scratch_shapes=[
            pltpu.VMEM((rows + 8, heads * MIX), F32),
            pltpu.VMEM((heads, DV + DK, DK), F32),
        ],
        compiler_params=pltpu.CompilerParams(vmem_limit_bytes=VMEM_LIMIT),
        cost_estimate=LIGHT,
    )(projected, projected, halo, rates, bias_row, taps)


def backward_kernel(
    heads, group, steps, peers, own,
    proj_ref, prev_ref, halo_ref, rates_ref, bias_ref, taps_ref,
    state_ref, uw_ref, inv_ref, trans_ref, qe_ref,
    dout_ref, value_ref, incoming_ref, place_ref, spots_ref, maps_ref, *refs,
):
    *local_refs, gp_ref, grates_ref, sums_ref, tail_ref, lead_ref, x_ref, d_ref, carry_ref, next_ref = refs
    step = pl.program_id(0)
    rows_here = CHUNK * group
    conv_scratch(step == steps - 1, proj_ref, prev_ref, halo_ref, x_ref, heads, rows_here)
    ri, ci = iotas(CHUNK)
    included = ri >= ci
    strictly = ri > ci
    lower = jnp.where(included, 1.0, 0.0)
    upper = jnp.where(ri <= ci, 1.0, 0.0)

    @pl.when(step == 0)
    def _():
        for h in range(heads):
            grad = jnp.zeros((DV, DK), F32)
            for turn in range(peers - 1):
                source = peers - 1 - turn
                share = jnp.zeros((DV, DK), F32)
                for b, local_ref in enumerate(local_refs):
                    here = (place_ref[0] ^ b) == source if peers == 4 else b == source
                    share = jnp.where(here, local_ref[h].astype(F32), share)
                moved = mm(grad, maps_ref[source, h, DV:, :], 1, 1) + share
                grad = jnp.where(source > place_ref[0], moved, grad)
            carry_ref[h] = grad
        d_ref[rows_here : rows_here + 8, :] = jnp.zeros((8, heads * MIX), F32)
        sums_ref[...] = jnp.zeros_like(sums_ref)

    @pl.when(step > 0)
    def _():
        d_ref[rows_here : rows_here + 8, :] = d_ref[0:8, :]

    def near_row(g):
        first = ((steps - 1 - step) * group + g) * CHUNK
        return pl.multiple_of(spots_ref[first // own] * own + first % own, CHUNK)

    pairs = [(g, h) for g in range(group) for h in range(heads)]
    logits = rates_ref[...] + bias_ref[...]
    log_decay = -softplus(logits)
    strength = sigmoid(logits)
    cums, cum_rows = [], []
    for g in range(group):
        part = log_decay[g * CHUNK : (g + 1) * CHUNK]
        cums.append(mmx(lower, part))
        cum_rows.append(mmx(part, upper, 0, 0))
    douts, injections = [], []
    for g, h in pairs:
        do = dout_ref[g * CHUNK : (g + 1) * CHUNK, h * DV : (h + 1) * DV]
        douts.append(do)
        injections.append(mm(do, qe_ref[h, g], 0, 0))
    for h in range(heads):
        now = carry_ref[h]
        for g in reversed(range(group)):
            j = pairs.index((g, h))
            last = cums[g][CHUNK - 1 : CHUNK, 2 * h : 2 * h + 1]
            next_ref[h, g] = now
            now = jnp.exp(last) * now + mm(now, trans_ref[h, g], 1, 1) + injections[j]
        carry_ref[h] = now
    lane = lax.broadcasted_iota(jnp.int32, (CHUNK, 2 * heads), 1)
    row_col = lax.broadcasted_iota(jnp.int32, (CHUNK, 1), 0)
    dcums = [jnp.zeros((CHUNK, 2 * heads), F32) for _ in range(group)]
    dlogits = [jnp.zeros((CHUNK, 2 * heads), F32) for _ in range(group)]
    for j, (g, h) in enumerate(pairs):
        pre = conv_pre(x_ref, taps_ref, h, g * CHUNK)
        sig = sigmoid(pre)
        mixed = pre * sig
        slope = sig * (1.0 + pre * (1.0 - sig))
        uq, rq = unit(mixed[:, :DK])
        q = uq * DK ** (-0.5)
        k, rk = unit(mixed[:, DK : 2 * DK])
        v = mixed[:, 2 * DK :]
        cum = cums[g][:, 2 * h : 2 * h + 1]
        cum_row = cum_rows[g][2 * h : 2 * h + 1, :]
        beta = strength[g * CHUNK : (g + 1) * CHUNK, 2 * h + 1 : 2 * h + 2]
        growth = jnp.exp(cum)
        decays = jnp.where(included, jnp.exp(jnp.where(included, cum - cum_row, 0.0)), 0.0)
        qb, kb = q.astype(BF16), k.astype(BF16)
        grams = mm(jnp.concatenate([qb, kb], axis=0), kb, 1, 1)
        scores = grams[:CHUNK] * decays
        last = cum[CHUNK - 1 : CHUNK, :]
        fade = jnp.exp(last - cum)
        tail = k * fade
        sl = state_ref[h, g]
        state = sl[:DV].astype(F32) + mm(incoming_ref[h], sl[DV:])
        after = next_ref[h, g]
        afterb = after.astype(BF16)
        stateb = state.astype(BF16)
        uw = uw_ref[h, g]
        errors = uw[:, :DV].astype(F32) - mm(uw[:, DV:], stateb, 1, 1)
        eb = errors.astype(BF16)
        do = douts[j]
        de = mm(scores, do, 0, 0) + mm(tail, afterb, 1, 1)
        db = de + mm(inv_ref[h, g], de, 0, 0)
        dbb = db.astype(BF16)
        stacked = jnp.concatenate([do, dbb], axis=0)
        against_e = mm(stacked, eb, 1, 1)
        against_s = mm(stacked, stateb)
        dp = against_e[:CHUNK]
        da = jnp.where(strictly, -against_e[CHUNK:], 0.0)
        dos = against_s[:CHUNK]
        dbs = against_s[CHUNK:]
        dpd = dp * decays
        dg = da * beta * decays
        dtail = mm(eb, afterb)
        dq = mm(dpd, kb) + growth * dos
        sym = dg + dg.T
        dk = (
            mm(jnp.concatenate([dpd.T, sym], axis=1), jnp.concatenate([qb, kb], axis=0))
            - beta * growth * dbs
            + fade * dtail
        )
        dv = beta * db
        dlogit = (1.0 - beta) * jnp.sum(db * errors, axis=1, keepdims=True)
        tdot = jnp.sum(tail * dtail, axis=1, keepdims=True)
        out = value_ref[g * CHUNK : (g + 1) * CHUNK, h * DV : (h + 1) * DV].astype(F32)
        dcum = jnp.sum(do.astype(F32) * out, axis=1, keepdims=True) - beta * jnp.sum(
            v * db, axis=1, keepdims=True
        )
        at_end = jnp.exp(last) * jnp.sum(jnp.sum(after * state, axis=1, keepdims=True), axis=0, keepdims=True) + jnp.sum(
            tdot, axis=0, keepdims=True
        )
        dcum = dcum + jnp.where(row_col == CHUNK - 1, at_end, 0.0)
        dcums[g] = jnp.where(lane == 2 * h, dcum, dcums[g])
        dlogits[g] = jnp.where(lane == 2 * h + 1, dlogit, dlogits[g])
        dq = dq * DK ** (-0.5)
        dmq = rq * (dq - uq * jnp.sum(uq * dq, axis=1, keepdims=True))
        dmk = rk * (dk - k * jnp.sum(k * dk, axis=1, keepdims=True))
        d_ref[g * CHUNK : (g + 1) * CHUNK, h * MIX : (h + 1) * MIX] = (
            jnp.concatenate([dmq, dmk, dv], axis=1) * slope
        )
    for g in range(group):
        rows = slice(g * CHUNK, (g + 1) * CHUNK)
        dld = mmx(upper, dcums[g])
        drate = jnp.where(lane % 2 == 0, -sigmoid(logits[rows]) * dld, dlogits[g])
        grates_ref[pl.ds(near_row(g), CHUNK), :] = drate
        sums_ref[CONV : CONV + 1, : 2 * heads] += jnp.sum(drate, axis=0, keepdims=True)
    for g, h in pairs:
        cols = slice(h * MIX, (h + 1) * MIX)
        row = g * CHUNK
        dpre = d_ref[pl.ds(row, CHUNK), cols]
        total = None
        for i in range(CONV):
            sums_ref[i : i + 1, cols] += jnp.sum(
                dpre * x_ref[pl.ds(row + 8 - (CONV - 1) + i, CHUNK), cols], axis=0, keepdims=True
            )
            part = taps_ref[i : i + 1, cols] * d_ref[pl.ds(row + CONV - 1 - i, CHUNK), cols]
            total = part if total is None else total + part
        gp_ref[pl.ds(near_row(g), CHUNK), cols] = total.astype(BF16)
        if g == group - 1:
            @pl.when(step == 0)
            def _(total=total, cols=cols):
                tail_ref[:, cols] = total[CHUNK - HALO :]

    @pl.when(step == steps - 1)
    def _():
        lead_ref[...] = d_ref[0:8, :]


def mixer_backward(projected, halo, rates, bias_row, taps, saved, dout, value, incoming, place, spots, maps, local, group):
    state, uw, inv, trans, qe = saved
    total = projected.shape[0]
    heads = rates.shape[1] // 2
    rows = CHUNK * group
    steps = total // rows
    whole = lambda i: (0, 0)
    flip = lambda i: (steps - 1 - i, 0)
    keep = lambda a, b: pl.BlockSpec((heads, group, a, b), lambda i: (0, steps - 1 - i, 0, 0))
    return pl.pallas_call(
        functools.partial(backward_kernel, heads, group, steps, maps.shape[0], total // spots.shape[0]),
        grid=(steps,),
        in_specs=[
            pl.BlockSpec((rows, heads * PER), flip),
            pl.BlockSpec((HALO, heads * PER), lambda i: (jnp.maximum((steps - 1 - i) * (rows // HALO) - 1, 0), 0)),
            pl.BlockSpec((HALO, heads * PER), whole),
            pl.BlockSpec((rows, 2 * heads), flip),
            pl.BlockSpec((1, 2 * heads), whole),
            pl.BlockSpec((CONV, heads * MIX), whole),
            keep(DV + DK, DK),
            keep(CHUNK, DV + DK),
            keep(CHUNK, CHUNK),
            keep(DK, DK),
            keep(CHUNK, DK),
            pl.BlockSpec((rows, heads * DV), flip),
            pl.BlockSpec((rows, heads * DV), flip),
            pl.BlockSpec(incoming.shape, lambda i: (0, 0, 0)),
            pl.BlockSpec(memory_space=pltpu.SMEM),
            pl.BlockSpec(memory_space=pltpu.SMEM),
            pl.BlockSpec(maps.shape, lambda i: (0, 0, 0, 0)),
            *[pl.BlockSpec(part.shape, lambda i: (0, 0, 0)) for part in local],
        ],
        out_shape=[
            jax.ShapeDtypeStruct((total, heads * MIX), BF16),
            jax.ShapeDtypeStruct((total, 2 * heads), F32),
            jax.ShapeDtypeStruct((8, heads * MIX), F32),
            jax.ShapeDtypeStruct((HALO, heads * MIX), F32),
            jax.ShapeDtypeStruct((8, heads * MIX), F32),
        ],
        out_specs=[
            pl.BlockSpec((total, heads * MIX), whole),
            pl.BlockSpec((total, 2 * heads), whole),
            pl.BlockSpec((8, heads * MIX), whole),
            pl.BlockSpec((HALO, heads * MIX), whole),
            pl.BlockSpec((8, heads * MIX), whole),
        ],
        scratch_shapes=[
            pltpu.VMEM((rows + 8, heads * MIX), F32),
            pltpu.VMEM((rows + 8, heads * MIX), F32),
            pltpu.VMEM((heads, DV, DK), F32),
            pltpu.VMEM((heads, group, DV, DK), F32),
        ],
        compiler_params=pltpu.CompilerParams(vmem_limit_bytes=VMEM_LIMIT),
        cost_estimate=LIGHT,
    )(projected, projected, halo, rates, bias_row, taps, state, uw, inv, trans, qe, dout, value, incoming, place, spots, maps, *local)


def pair_rows(ids_ref, step, which, rows):
    return pl.ds(pl.multiple_of(ids_ref[2 * step + which] * rows, rows), rows)


def gate_kernel(heads, peers, ids_ref, place_ref, maps_ref, gain_ref, w_ref, *refs):
    olocal_refs, qmap_refs = refs[0:2], refs[2:4]
    gate_refs = refs[4 : 4 + 2 * heads]
    value_ref, gated_ref, part_ref, incoming_ref = refs[4 + 2 * heads :]
    step = pl.program_id(0)

    @pl.when(step == 0)
    def _():
        for h in range(heads):
            state = jnp.zeros((DV, DK), F32)
            for source in range(peers - 1):
                moved = mm(state, maps_ref[source, h, DV:, :]) + maps_ref[source, h, :DV, :].astype(F32)
                state = jnp.where(source < place_ref[0], moved, state)
            incoming_ref[h] = state.astype(BF16)

    rows = olocal_refs[0].shape[0]
    for h in range(heads):
        cols = slice(h * DV, (h + 1) * DV)
        query_map = jnp.concatenate([ref[:, h * DK : (h + 1) * DK] for ref in qmap_refs], axis=0)
        out_local = jnp.concatenate([ref[:, cols] for ref in olocal_refs], axis=0)
        low = (out_local + mm(query_map, incoming_ref[h], 1, 1)).astype(BF16)
        for which in range(2):
            value_ref[pair_rows(ids_ref, step, which, rows), cols] = low[which * rows : (which + 1) * rows]
        value = low.astype(F32)
        normed = value * lax.rsqrt(jnp.mean(value * value, axis=-1, keepdims=True) + epsilon)
        gate = jnp.concatenate([gate_refs[2 * h + which][...] for which in range(2)], axis=0).astype(F32)
        gated_ref[:, cols] = (normed * gain_ref[...] * (gate * sigmoid(gate))).astype(BF16)
    part_ref[...] = mm(gated_ref[...], w_ref[...]).astype(BF16)


def gate_blocks(heads, rows):
    full = lambda wide: [
        pl.BlockSpec((rows, wide), lambda i, *s, which=which: (s[0][2 * i + which], 0)) for which in range(2)
    ]
    gates = [
        pl.BlockSpec(
            (rows, DV), lambda i, *s, which=which, h=h: (s[0][2 * i + which], (h + 1) * (PER // DV) - 1)
        )
        for h in range(heads)
        for which in range(2)
    ]
    return full, gates


def gate_output(ids, place, maps, out_local, query_map, projected, gain, w_out):
    heads = maps.shape[1]
    total = projected.shape[0]
    count = ids.shape[0]
    rows = total // count
    width = w_out.shape[1]
    mine = lambda i, *s: (i, 0)
    whole = lambda i, *s: (0, 0)
    full, gates = gate_blocks(heads, rows)
    return pl.pallas_call(
        functools.partial(gate_kernel, heads, maps.shape[0]),
        grid_spec=pltpu.PrefetchScalarGridSpec(
            num_scalar_prefetch=2,
            grid=(count // 2,),
            in_specs=[
                pl.BlockSpec(maps.shape, lambda i, *s: (0, 0, 0, 0)),
                pl.BlockSpec((1, DV), whole),
                pl.BlockSpec(w_out.shape, whole),
                *full(heads * DV),
                *full(heads * DK),
                *gates,
            ],
            out_specs=[
                pl.BlockSpec((total, heads * DV), whole),
                pl.BlockSpec((2 * rows, heads * DV), mine),
                pl.BlockSpec((2 * rows, width), mine),
                pl.BlockSpec((heads, DV, DK), lambda i, *s: (0, 0, 0)),
            ],
        ),
        out_shape=[
            jax.ShapeDtypeStruct((total, heads * DV), BF16),
            jax.ShapeDtypeStruct((total, heads * DV), BF16),
            jax.ShapeDtypeStruct((total, width), BF16),
            jax.ShapeDtypeStruct((heads, DV, DK), BF16),
        ],
        compiler_params=pltpu.CompilerParams(vmem_limit_bytes=VMEM_LIMIT),
        cost_estimate=LIGHT,
    )(
        ids, place, maps, gain, w_out, out_local, out_local, query_map, query_map,
        *[projected] * (2 * heads),
    )


def gate_back_kernel(heads, ids_ref, branch_ref, gain_ref, w_ref, *refs):
    value_refs, qmap_refs = refs[0:2], refs[2:4]
    gate_refs = refs[4 : 4 + 2 * heads]
    ggate_ref, dout_ref, gain_grad_ref, local_ref, sum_ref = refs[4 + 2 * heads :]
    step = pl.program_id(0)

    @pl.when(step == 0)
    def _():
        gain_grad_ref[...] = jnp.zeros_like(gain_grad_ref)
        sum_ref[...] = jnp.zeros_like(sum_ref)

    rows = value_refs[0].shape[0]
    grads = mm(branch_ref[...], w_ref[...], 1, 1)
    gain = gain_ref[...]
    for h in range(heads):
        cols = slice(h * DV, (h + 1) * DV)
        value = jnp.concatenate([ref[:, cols] for ref in value_refs], axis=0).astype(F32)
        inverse = lax.rsqrt(jnp.mean(value * value, axis=-1, keepdims=True) + epsilon)
        normed = value * inverse
        gate = jnp.concatenate([gate_refs[2 * h + which][...] for which in range(2)], axis=0).astype(F32)
        sig = sigmoid(gate)
        grad = grads[:, cols]
        through = grad * (gate * sig)
        ggate_ref[:, cols] = (grad * normed * gain * (sig * (1.0 + gate * (1.0 - sig)))).astype(BF16)
        gain_grad_ref[...] += jnp.sum(through * normed, axis=0, keepdims=True)
        scaled = through * gain
        low = (inverse * (scaled - normed * jnp.mean(scaled * normed, axis=-1, keepdims=True))).astype(BF16)
        for which in range(2):
            dout_ref[pair_rows(ids_ref, step, which, rows), cols] = low[which * rows : (which + 1) * rows]
        query_map = jnp.concatenate([ref[:, h * DK : (h + 1) * DK] for ref in qmap_refs], axis=0)
        sum_ref[h] += mm(low, query_map, 0, 0)

    @pl.when(step == pl.num_programs(0) - 1)
    def _():
        local_ref[...] = sum_ref[...].astype(BF16)


def gate_backward(ids, branch, w_out, value, projected, query_map, gain, heads):
    total = projected.shape[0]
    count = ids.shape[0]
    rows = total // count
    mine = lambda i, *s: (i, 0)
    whole = lambda i, *s: (0, 0)
    full, gates = gate_blocks(heads, rows)
    return pl.pallas_call(
        functools.partial(gate_back_kernel, heads),
        grid_spec=pltpu.PrefetchScalarGridSpec(
            num_scalar_prefetch=1,
            grid=(count // 2,),
            in_specs=[
                pl.BlockSpec((2 * rows, branch.shape[1]), mine),
                pl.BlockSpec((1, DV), whole),
                pl.BlockSpec(w_out.shape, whole),
                *full(heads * DV),
                *full(heads * DK),
                *gates,
            ],
            out_specs=[
                pl.BlockSpec((2 * rows, heads * DV), mine),
                pl.BlockSpec((total, heads * DV), whole),
                pl.BlockSpec((1, DV), whole),
                pl.BlockSpec((heads, DV, DK), lambda i, *s: (0, 0, 0)),
            ],
            scratch_shapes=[pltpu.VMEM((heads, DV, DK), F32)],
        ),
        out_shape=[
            jax.ShapeDtypeStruct((total, heads * DV), BF16),
            jax.ShapeDtypeStruct((total, heads * DV), BF16),
            jax.ShapeDtypeStruct((1, DV), F32),
            jax.ShapeDtypeStruct((heads, DV, DK), BF16),
        ],
        compiler_params=pltpu.CompilerParams(vmem_limit_bytes=VMEM_LIMIT),
        cost_estimate=LIGHT,
    )(
        ids, branch, gain, w_out, value, value, query_map, query_map, *[projected] * (2 * heads)
    )


def project_kernel(layout, pieces, ids_ref, spots_ref, rate_ref, *refs):
    x_refs = refs[: len(layout)]
    w_refs = refs[len(layout) : len(layout) + pieces]
    out_ref, rates_ref = refs[len(layout) + pieces :]
    rows = out_ref.shape[0] // ids_ref.shape[0]
    blocks = {}
    for (k, _), ref in zip(layout, x_refs):
        blocks.setdefault(k, []).append(ref)
    ks = list(blocks)
    for first in range(0, len(ks), 2):
        group = ks[first : first + 2]
        group_refs = [ref for k in group for ref in blocks[k]]
        x = jnp.concatenate([ref[...] for ref in group_refs], axis=0)
        total = None
        for b, w_ref in enumerate(w_refs):
            cols = block_columns(spots_ref, b, w_ref.shape[0])
            share = mm(jnp.concatenate([ref[:, cols] for ref in group_refs], axis=0), w_ref[...])
            total = share if total is None else total + share
        total = total.astype(BF16)
        rates = mm(x, rate_ref[...], 1, 1)
        for i, k in enumerate(group):
            place = pl.ds(pl.multiple_of(ids_ref[k] * rows, rows), rows)
            out_ref[place, :] = total[i * rows : (i + 1) * rows]
            rates_ref[place, :] = rates[i * rows : (i + 1) * rows]


def layout_of(found, total):
    rows = found[0][0].shape[0]
    count = total // rows
    ks = [0] + [k for s in range(1, count // 2) for k in (s, count - s)] + [count // 2]
    layout, arrays = [], []
    for k in ks:
        start = k * rows
        for piece in found.get(k, ()):
            layout.append((k, start))
            arrays.append(piece)
            start += piece.shape[0]
    return layout, arrays


def project(ids, spots, found, w_mix, w_rate):
    total = ids.shape[0] * found[0][0].shape[0]
    layout, arrays = layout_of(found, total)
    cols = w_mix[0].shape[1]
    rates = w_rate.shape[0]
    whole = lambda shape: pl.BlockSpec(shape, lambda i, ids, spots: (0, 0))
    return pl.pallas_call(
        functools.partial(project_kernel, layout, len(w_mix)),
        grid_spec=pltpu.PrefetchScalarGridSpec(
            num_scalar_prefetch=2,
            grid=(1,),
            in_specs=[whole(a.shape) for a in (w_rate, *arrays, *w_mix)],
            out_specs=[whole((total, cols)), whole((total, rates))],
        ),
        out_shape=[
            jax.ShapeDtypeStruct((total, cols), BF16),
            jax.ShapeDtypeStruct((total, rates), F32),
        ],
        compiler_params=pltpu.CompilerParams(vmem_limit_bytes=VMEM_LIMIT),
        cost_estimate=LIGHT,
    )(ids, spots, w_rate, *arrays, *w_mix)


def normed_back_kernel(pieces, blocks, spots_ref, *refs):
    mixes, gates, rates, normed = (refs[i * blocks : (i + 1) * blocks] for i in range(4))
    rate_ref, before_ref = refs[4 * blocks : 4 * blocks + 2]
    w_refs = refs[4 * blocks + 2 : 4 * blocks + 2 + pieces]
    part_ref, sums_ref = refs[4 * blocks + 2 + pieces :]
    heads = gates[0].shape[1] // DV
    left = jnp.concatenate(
        [
            jnp.concatenate([ref[:, h * size : (h + 1) * size] for ref in group], axis=0)
            for h in range(heads)
            for group, size in ((mixes, MIX), (gates, DV))
        ],
        axis=1,
    )
    rate = jnp.concatenate([ref[...].astype(BF16) for ref in rates], axis=0)
    count = rate.shape[1]
    sums_ref[...] = before_ref[...]
    for b, w_ref in enumerate(w_refs):
        cols = block_columns(spots_ref, b, w_ref.shape[0])
        part = mm(left, w_ref[...], 1, 1) + mm(rate, rate_ref[:, cols])
        part_ref[:, cols] = part.astype(BF16)
        right = jnp.concatenate([ref[:, cols] for ref in normed], axis=0)
        sums_ref[:count, cols] += mm(rate, right, 0, 0)
        sums_ref[4:5, cols] += jnp.sum(part * right.astype(F32), axis=0, keepdims=True)


def normed_back(spots, order, blocks, grad_mixed, grad_gates, grad_rates, normed, w_mix, w_rate, before):
    total, width = normed.shape
    rows = total // blocks
    rates = w_rate.shape[0]
    count = len(order)
    block = lambda k, wide: pl.BlockSpec((rows, wide), lambda i, spots: (k, 0))
    whole = lambda i, spots: (0, 0)
    return pl.pallas_call(
        functools.partial(normed_back_kernel, len(w_mix), count),
        grid_spec=pltpu.PrefetchScalarGridSpec(
            num_scalar_prefetch=1,
            grid=(1,),
            in_specs=[
                *[block(k, grad_mixed.shape[1]) for k in order],
                *[block(k, grad_gates.shape[1]) for k in order],
                *[block(k, rates) for k in order],
                *[block(k, width) for k in order],
                pl.BlockSpec((rates, width), whole),
                pl.BlockSpec((8, width), whole),
                *[pl.BlockSpec(w.shape, whole) for w in w_mix],
            ],
            out_specs=[pl.BlockSpec((count * rows, width), whole), pl.BlockSpec((8, width), whole)],
        ),
        out_shape=[
            jax.ShapeDtypeStruct((count * rows, width), BF16),
            jax.ShapeDtypeStruct((8, width), F32),
        ],
        compiler_params=pltpu.CompilerParams(vmem_limit_bytes=VMEM_LIMIT),
        cost_estimate=LIGHT,
    )(
        spots,
        *[grad_mixed] * count,
        *[grad_gates] * count,
        *[grad_rates] * count,
        *[normed] * count,
        w_rate,
        before,
        *w_mix,
    )


def stack_kernel(layout, *refs):
    out_ref = refs[len(layout)]
    for (_, start), ref in zip(layout, refs):
        out_ref[start : start + ref.shape[0], :] = ref[...]


def stacked(found, total):
    layout, arrays = layout_of(found, total)
    return pl.pallas_call(
        functools.partial(stack_kernel, layout),
        out_shape=jax.ShapeDtypeStruct((total, arrays[0].shape[1]), arrays[0].dtype),
        compiler_params=pltpu.CompilerParams(vmem_limit_bytes=VMEM_LIMIT),
        cost_estimate=LIGHT,
    )(*arrays)


def finish_kernel(first_ref, second_ref, buffer_ref, out_ref):
    half = first_ref.shape[0]
    out_ref[:half, :] = first_ref[...]
    out_ref[half:, :] = second_ref[...]


def finish_stack(buffer, pieces, k):
    half, width = pieces[0].shape
    whole = pl.BlockSpec((half, width), lambda i: (0, 0))
    return pl.pallas_call(
        finish_kernel,
        grid=(1,),
        in_specs=[whole, whole, pl.BlockSpec(memory_space=pl.ANY)],
        out_specs=pl.BlockSpec((2 * half, width), lambda i: (k, 0)),
        out_shape=jax.ShapeDtypeStruct(buffer.shape, buffer.dtype),
        input_output_aliases={2: 0},
        cost_estimate=LIGHT,
    )(*pieces, buffer)


def outer_kernel(left_ref, right_ref, out_ref):
    out_ref[...] = mm(left_ref[...], right_ref[...], 0, 0).astype(BF16)


def outer(left, right):
    total, m = left.shape
    n = right.shape[1]
    by_rows = m % 512 == 0 and m > 512
    rows = 512 if by_rows else m
    cols = n if by_rows or n % 512 else 512
    return pl.pallas_call(
        outer_kernel,
        grid=(m // rows, n // cols),
        in_specs=[
            pl.BlockSpec((total, rows), lambda i, j: (0, i)),
            pl.BlockSpec((total, cols), lambda i, j: (0, j)),
        ],
        out_specs=pl.BlockSpec((rows, cols), lambda i, j: (i, j)),
        out_shape=jax.ShapeDtypeStruct((m, n), BF16),
        compiler_params=pltpu.CompilerParams(vmem_limit_bytes=VMEM_LIMIT),
        cost_estimate=LIGHT,
    )(left, right)


def turn_kernel(count, *refs):
    for i in range(count):
        refs[count + i][...] = refs[i][...].astype(F32).T.astype(BF16)


def turned(arrays):
    rows, width = arrays[0].shape
    step = 512
    return pl.pallas_call(
        functools.partial(turn_kernel, len(arrays)),
        grid=(width // step,),
        in_specs=[pl.BlockSpec((rows, step), lambda i: (0, i))] * len(arrays),
        out_specs=[pl.BlockSpec((step, rows), lambda i: (i, 0))] * len(arrays),
        out_shape=[jax.ShapeDtypeStruct((width, rows), BF16)] * len(arrays),
        compiler_params=pltpu.CompilerParams(vmem_limit_bytes=VMEM_LIMIT),
        cost_estimate=LIGHT,
    )(*arrays)


def widen_kernel(count, *refs):
    for i in range(count):
        refs[count + i][...] = refs[i][...].astype(F32)


def widen(arrays):
    steps = 4
    specs = [pl.BlockSpec((a.shape[0] // steps, a.shape[1]), lambda i: (i, 0)) for a in arrays]
    return pl.pallas_call(
        functools.partial(widen_kernel, len(arrays)),
        grid=(steps,),
        in_specs=specs,
        out_specs=specs,
        out_shape=[jax.ShapeDtypeStruct(a.shape, F32) for a in arrays],
        compiler_params=pltpu.CompilerParams(vmem_limit_bytes=VMEM_LIMIT),
        cost_estimate=LIGHT,
    )(*arrays)


def join_kernel(heads, mix_ref, gate_ref, out_ref):
    for h in range(heads):
        out_ref[:, h * PER : h * PER + MIX] = mix_ref[:, h * MIX : (h + 1) * MIX].astype(F32)
        out_ref[:, h * PER + MIX : (h + 1) * PER] = gate_ref[:, h * DV : (h + 1) * DV].astype(F32)


def join_heads(mix, gate):
    rows = mix.shape[0]
    heads = gate.shape[1] // DV
    steps = 4
    spec = lambda wide: pl.BlockSpec((rows // steps, wide), lambda i: (i, 0))
    return pl.pallas_call(
        functools.partial(join_kernel, heads),
        grid=(steps,),
        in_specs=[spec(mix.shape[1]), spec(gate.shape[1])],
        out_specs=spec(heads * PER),
        out_shape=jax.ShapeDtypeStruct((rows, heads * PER), F32),
        compiler_params=pltpu.CompilerParams(vmem_limit_bytes=VMEM_LIMIT),
        cost_estimate=LIGHT,
    )(mix, gate)


def times_kernel(left_ref, right_ref, out_ref):
    out_ref[...] = mm(left_ref[...], right_ref[...])


def times(left, right):
    total, depth = left.shape
    n = right.shape[1]
    rows = 256
    return pl.pallas_call(
        times_kernel,
        grid=(total // rows,),
        in_specs=[
            pl.BlockSpec((rows, depth), lambda i: (i, 0)),
            pl.BlockSpec((depth, n), lambda i: (0, 0)),
        ],
        out_specs=pl.BlockSpec((rows, n), lambda i: (i, 0)),
        out_shape=jax.ShapeDtypeStruct((total, n), F32),
        compiler_params=pltpu.CompilerParams(vmem_limit_bytes=VMEM_LIMIT),
        cost_estimate=LIGHT,
    )(left, right)
def ring_order(count):
    return list(range(0, count, 2)) + list(range(1, count, 2))[::-1]


def ring_step(value, axis, step):
    order = ring_order(lax.axis_size(axis))
    count = len(order)
    return lax.ppermute(value, axis, [(order[i], order[(i + step) % count]) for i in range(count)])


def ring_ids(axis):
    order = ring_order(lax.axis_size(axis))
    count = len(order)
    place = {device: i for i, device in enumerate(order)}
    ahead = [[order[(place[device] + k) % count] for k in range(count)] for device in range(count)]
    back = [[row.index(device) for device in range(count)] for row in ahead]
    row = lax.dynamic_index_in_dim(
        jnp.array([a + b for a, b in zip(ahead, back)], jnp.int32), lax.axis_index(axis), 0, False
    )
    return row[:count], row[count:]


def after(value, *earlier):
    return lax.optimization_barrier((value, *earlier))[0]


def together(*values):
    return lax.optimization_barrier(values)


def window(fillers, hop, gate):
    return fillers[hop](lambda value: after(value, gate)) if hop in fillers else ()


def ring_gather(shard, axis, fillers={}, stack=True):
    count = lax.axis_size(axis)
    far = count // 2
    half = shard.shape[0] // 2
    total = count * shard.shape[0]
    found = {0: [shard]}
    forward = backward = shard
    buffer = None
    for hop in range(1, far + 1):
        gate = forward
        extra = list(window(fillers, hop, gate))
        if hop < far:
            forward = ring_step(forward, axis, 1)
            backward = ring_step(backward, axis, -1)
            found[count - hop] = [forward]
            found[hop] = [backward]
        else:
            if stack:
                buffer = stacked({k: [after(p, gate) for p in ps] for k, ps in found.items()}, total)
                extra.append(buffer)
            forward = ring_step(forward[:half], axis, 1)
            backward = ring_step(backward[half:], axis, -1)
            found[hop] = [forward, backward]
        forward, backward, *_ = together(forward, backward, *extra)
    found[far] = [forward, backward]
    return finish_stack(buffer, found[far], far) if stack else found


def ring_scatter(take, rows, axis, fillers={}):
    count = lax.axis_size(axis)
    far = count // 2
    size = rows // 2
    flows = [[take(far, 0, size), None], [None, take(far, size, size)]]
    gate = take(far, 0, size)
    for hop in range(1, far + 1):
        flows = [
            [flow[way] if flow[way] is None else ring_step(flow[way], axis, 1 - 2 * way) for way in range(2)]
            for flow in flows
        ]
        extra = window(fillers, hop, gate)
        flat = together(*[a for flow in flows for a in flow if a is not None], *extra)
        flat = iter(flat)
        flows = [[None if a is None else next(flat) for a in flow] for flow in flows]
        s = far - hop
        if s:
            for part, flow in enumerate(flows):
                for way, k in enumerate((s, count - s)):
                    piece = take(k, part * size, size)
                    flow[way] = piece if flow[way] is None else flow[way] + piece
            gate = flows[0][0]
    totals = [
        take(0, part * size, size).astype(F32) + flow[0].astype(F32) + flow[1].astype(F32)
        for part, flow in enumerate(flows)
    ]
    return jnp.concatenate(totals, axis=0)


def near_rows(array, rows):
    return lambda k, start, size: lax.slice_in_dim(array, k * rows + start, k * rows + start + size, axis=0)


def swap(value, axis, bit):
    count = lax.axis_size(axis)
    return lax.ppermute(value, axis, [(i, i ^ bit) for i in range(count)])


def pair_spots(axis):
    count = lax.axis_size(axis)
    order = jnp.arange(count, dtype=jnp.int32)
    return lax.axis_index(axis) ^ order if count == 4 else order


def pair_far(shard, axis, *pins):
    if lax.axis_size(axis) != 4:
        return lax.all_gather(shard, axis)
    return swap(after(shard, *pins), axis, 2)


def pair_gather(shard, far, axis, *pins):
    count = lax.axis_size(axis)
    if count != 4:
        return [far[b] for b in range(count)]
    return [shard, swap(after(shard, *pins), axis, 1), far, swap(after(far, *pins), axis, 1)]


def seq_shards(value, axis):
    if lax.axis_size(axis) != 4:
        whole = lax.all_gather(value, axis)
        return [whole[b] for b in range(lax.axis_size(axis))]
    return [value] + [swap(value, axis, b) for b in range(1, 4)]


def butterfly(value, axis):
    bit = 1
    while bit < lax.axis_size(axis):
        value = value + swap(value, axis, bit)
        bit *= 2
    return value


def per_device(
    tokens,
    w_qkvg,
    w_rates,
    conv_weight,
    head_bias,
    norm_gain,
    head_gain,
    mlp_gain,
    w_out,
    w_ff_gate,
    w_ff_up,
    w_ff_down,
    cotangent,
):
    heads = head_bias.shape[1]
    own_rows = tokens.shape[0]
    contract = (((1,), (1,)), ((), ()))
    rows_first = (((0,), (0,)), ((), ()))
    dot = lambda a, b, dims: lax.dot_general(a, b, dims, preferred_element_type=F32)
    plain = (((1,), (0,)), ((), ()))
    ids, near_spots = ring_ids("head")
    spots = pair_spots("seq")
    place = lax.axis_index("seq").reshape(1)
    gain_row = head_gain.reshape(1, DV)
    bias_row = head_bias.T.reshape(1, 2 * heads)
    peers = lax.axis_size("seq")
    width = tokens.shape[1]
    keep = {}
    mix_far = pair_far(w_qkvg, "seq")
    inputs = tokens.astype(F32)
    inverse_one = lax.rsqrt(jnp.mean(inputs * inputs, axis=-1, keepdims=True) + epsilon)
    norm_normed = inputs * inverse_one
    hops = lax.axis_size("head") // 2
    last_window = hops

    rate_shard = w_rates.T
    if peers == 4:
        w_rate = jnp.zeros((2 * heads, width), BF16)
        for b in range(4):
            w_rate = lax.dynamic_update_slice_in_dim(
                w_rate,
                swap(rate_shard, "seq", b) if b else rate_shard,
                (place[0] ^ b) * rate_shard.shape[1],
                1,
            )
    else:
        w_rate = lax.all_gather(rate_shard, "seq", axis=1, tiled=True)

    count = 2 * hops
    stages = 4
    cot_found = {0: [cotangent]}
    cot_state = [cotangent, cotangent]

    def cot_hop(hop, *gates):
        forward, backward, *_ = together(*cot_state, *gates)
        if hop < hops:
            forward, backward = ring_step(forward, "head", 1), ring_step(backward, "head", -1)
            cot_found[count - hop], cot_found[hop] = [forward], [backward]
        else:
            half = own_rows // 2
            forward = ring_step(forward[:half], "head", 1)
            backward = ring_step(backward[half:], "head", -1)
            cot_found[hop] = [forward, backward]
        cot_state[:] = [forward, backward]
        return list(cot_state)

    def fetch_mix(pin):
        keep["mix"] = pair_gather(w_qkvg, pin(mix_far), "seq")
        return keep["mix"]

    fillers = {last_window: fetch_mix}
    normed_found = ring_gather((norm_normed * norm_gain).astype(BF16), "head", fillers, False)
    w_mix = keep["mix"]
    out_rows = lax.all_gather(after(w_out, mix_far), "seq", axis=1, tiled=True)

    stage_hops = {
        stage: range(1 + hops * stage // stages, 1 + hops * (stage + 1) // stages) for stage in range(stages)
    }

    def cot_stage(stage, gate):
        made = []
        for hop in stage_hops[stage]:
            made = cot_hop(hop, gate)
        return made

    cot_stage(0, normed_found[hops][0])
    projected, rates = project(ids, spots, normed_found, w_mix, w_rate)
    seq_rows = projected.shape[0]
    halo_rows = shifted(projected[seq_rows - HALO :], "seq", 1)
    projected, *_ = together(projected, *cot_state)
    cot_stage(1, projected)
    out_local, query_map, *saved, end_state = mixer_forward(
        projected, halo_rows, rates, bias_row, conv_weight, GROUP
    )
    end_state, *_ = together(end_state, *cot_state)
    cot_stage(2, end_state)
    maps = lax.all_gather(end_state, "seq")
    maps, *_ = together(maps, *cot_state)
    cot_stage(3, maps)
    value, gated, branch_part, incoming = gate_output(
        ids, place, maps, out_local, query_map, projected, gain_row, out_rows
    )
    branch_part, *_ = together(branch_part, *cot_state)
    fetch = lambda w, *pins: lax.all_gather(after(w, *pins), "seq", axis=1, tiled=True)
    down_w = fetch(w_ff_down, maps)
    gate_w = fetch(w_ff_gate, maps)
    up_w = fetch(w_ff_up, maps)

    def stack_normed(pin):
        keep["normed"] = stacked({k: [pin(p) for p in ps] for k, ps in normed_found.items()}, seq_rows)
        return (keep["normed"],)

    def stack_cotangent(pin):
        keep["cot"] = stacked({k: [pin(p) for p in ps] for k, ps in cot_found.items()}, seq_rows)
        return (keep["cot"],)

    def turn_down(pin):
        keep["down_t"] = turned([pin(down_w)])
        return keep["down_t"]

    def turn_others(pin):
        keep["others_t"] = turned([pin(gate_w), pin(up_w)])
        return keep["others_t"]

    residual = inputs + ring_scatter(
        near_rows(branch_part, own_rows), own_rows, "head", {1: stack_cotangent, 2: stack_normed}
    )
    inverse_two = lax.rsqrt(jnp.mean(residual * residual, axis=-1, keepdims=True) + epsilon)
    mlp_normed = residual * inverse_two

    def hidden_gradient(pin):
        keep["gh"] = times(pin(keep["cot"]), keep["down_t"][0])
        return (keep["gh"],)

    mlp_near = ring_gather((mlp_normed * mlp_gain).astype(BF16), "head", {1: turn_down, 2: hidden_gradient, 3: turn_others})
    normed, cotangent_near, grad_hidden = keep["normed"], keep["cot"], keep["gh"]

    gate_pre, up_pre = (dot(mlp_near, w, plain) for w in keep["others_t"])
    ff_sigmoid = jax.nn.sigmoid(gate_pre)
    ff_silu = gate_pre * ff_sigmoid
    hidden = (ff_silu * up_pre).astype(BF16)
    ff_slope = ff_sigmoid * (1.0 + gate_pre * (1.0 - ff_sigmoid))
    grad_gate_pre = (grad_hidden * up_pre * ff_slope).astype(BF16)
    grad_up_pre = (grad_hidden * ff_silu).astype(BF16)
    grad_mlp_part = (dot(grad_gate_pre, gate_w, plain) + dot(grad_up_pre, up_w, plain)).astype(BF16)

    scatter = lambda a: lax.psum_scatter(a, "seq", scatter_dimension=1, tiled=True)

    def weight_product(name, left, right, before=None):
        def filler(pin):
            made = [outer(pin(left), right)] if left is not None else []
            if before is not None:
                keep[before, "sum"] = scatter(pin(keep[before]))
            if made:
                keep[name] = made[0]
            return made

        return filler

    def output_rows(pin):
        keep["up", "sum"] = scatter(pin(keep["up"]))
        keep["output"] = dot(pin(hidden), down_w, plain).astype(BF16)
        return (keep["output"],)

    grad_mlp_in = ring_scatter(
        near_rows(grad_mlp_part, own_rows),
        own_rows,
        "head",
        {
            1: weight_product("down", hidden, cotangent_near),
            2: weight_product("gate", grad_gate_pre, mlp_near, "down"),
            3: weight_product("up", grad_up_pre, mlp_near, "gate"),
            4: output_rows,
        },
    )

    output_part = keep["output"]
    mlp_gain_part = jnp.sum(grad_mlp_in * mlp_normed, axis=0)
    scaled_two = grad_mlp_in * mlp_gain
    grad_residual = cotangent.astype(F32) + inverse_two * (
        scaled_two - mlp_normed * jnp.mean(scaled_two * mlp_normed, axis=-1, keepdims=True)
    )

    grad_down_s, grad_gate_s, grad_up_s = (keep[name, "sum"] for name in ("down", "gate", "up"))
    branch_near = ring_gather(
        grad_residual.astype(BF16), "head", {2: lambda pin: [grad_down_s], 4: lambda pin: [grad_gate_s]}
    )
    take_output = near_rows(output_part, own_rows)
    output_state = [None, None]
    known = lambda: [a for a in output_state if a is not None]

    def output_hops(stage, *gates):
        for hop in range(hops * (stage - 1) // stages, hops * stage // stages):
            here = []
            for way, k in enumerate((hops - hop, count - hops + hop)):
                if hop == 0 and way == 1:
                    here.append(None)
                    continue
                piece = take_output(k, 0, own_rows)
                total = piece if output_state[way] is None else output_state[way] + piece
                here.append(ring_step(after(total, *gates), "head", 1 - 2 * way))
            output_state[:] = here

    output_hops(1, branch_near)
    grad_gate_mix, grad_mixer, head_gain_part, local_grad = gate_backward(
        ids, branch_near, out_rows, value, projected, query_map, gain_row, heads
    )
    local_low, *_ = together(local_grad, *known())
    shares = seq_shards(local_low, "seq")
    gate_grad_w = outer(keep["normed"], together(grad_gate_mix, *shares[1:])[0])
    first_share, gate_grad_w = together(shares[0], gate_grad_w)
    gate_grad_s = lax.psum_scatter(gate_grad_w, "seq", scatter_dimension=0, tiled=True)
    output_hops(2, gate_grad_w)
    grad_mixed, grad_rates, seq_sums, tail_rows, lead_rows = mixer_backward(
        projected, halo_rows, rates, bias_row, conv_weight, saved,
        grad_mixer, value, incoming, place, near_spots, maps, [first_share, *shares[1:]], GROUP,
    )
    grad_mixed, gate_grad_s, grad_up_s, *_ = together(grad_mixed, gate_grad_s, grad_up_s, *known())
    later_rows = shifted(lead_rows, "seq", -1)
    out_grad_w = outer(gated, after(branch_near, lead_rows))
    output_hops(3, grad_mixed)
    padded = jnp.concatenate([jnp.zeros((HALO, heads * MIX), F32), later_rows])
    last_rows = tail_rows + sum(
        conv_weight[i] * padded[CONV - 1 - i : CONV - 1 - i + HALO] for i in range(CONV)
    )
    last_start = near_spots[count - 1] * own_rows + own_rows - HALO
    grad_mixed = lax.dynamic_update_slice(grad_mixed, last_rows.astype(BF16), (last_start, 0))
    grad_mixed, out_grad_w = together(grad_mixed, out_grad_w)
    mix_grad_w = outer(keep["normed"], grad_mixed)
    mix_grad_w, out_grad_w = together(mix_grad_w, out_grad_w)
    grad_out_s = scatter(out_grad_w)
    grad_mixed, mix_grad_w = together(grad_mixed, mix_grad_w)
    mix_grad_s = lax.psum_scatter(mix_grad_w, "seq", scatter_dimension=0, tiled=True)
    early = [hops] + ([hops - 1, hops + 1] if hops > 1 else [])
    late = [k for s in range(hops - 2, 0, -1) for k in (s, count - s)] + [0]
    place_of = {k: (0, i) for i, k in enumerate(early)} | {k: (1, i) for i, k in enumerate(late)}
    parts = []
    part, sums = normed_back(
        spots, early, count, grad_mixed, grad_gate_mix, grad_rates, normed, w_mix, w_rate, jnp.zeros((8, width), F32)
    )
    parts.append(part)

    def take(k, start, size):
        which, i = place_of[k]
        return lax.slice_in_dim(parts[which], i * own_rows + start, i * own_rows + start + size, axis=0)

    def late_rows(pin):
        part, keep["sums"] = normed_back(
            spots, late, count, pin(grad_mixed), grad_gate_mix, grad_rates, normed, w_mix, w_rate, sums
        )
        parts.append(part)
        return (part,)

    def first_window(pin):
        output_hops(4, pin(part))
        return (*late_rows(pin), *known())

    def second_window(pin):
        sums = pin(keep["sums"])
        gains = jnp.concatenate([mlp_gain_part[None], head_gain_part, jnp.zeros((1, width - DV), F32)], axis=1)
        gains = jnp.pad(gains, ((4, 3), (0, 0)))
        small = jnp.concatenate([sums, gains, seq_sums], axis=1)
        small = small + swap(small, "seq", 1)
        keep["gains"] = butterfly(small[4:5, : 3 * width], "head")
        keep["small"] = small
        return (grad_out_s,)

    def fourth_window(pin):
        keep["joined"] = join_heads(pin(mix_grad_s), gate_grad_s)
        return (keep["joined"],)

    def third_window(pin):
        keep["wide"] = widen([pin(a) for a in (grad_down_s, grad_gate_s, grad_up_s)])
        return keep["wide"]

    grad_normed = ring_scatter(
        take, own_rows, "head", {1: first_window, 2: second_window, 3: third_window, 4: fourth_window}
    )
    scaled_one = grad_normed * norm_gain
    grad_input = grad_residual + inverse_one * (
        scaled_one - norm_normed * jnp.mean(scaled_one * norm_normed, axis=-1, keepdims=True)
    )
    output = (
        residual + sum(a.astype(F32) for a in known()) + take_output(0, 0, own_rows).astype(F32)
    ).astype(BF16)
    row = jnp.pad(keep["gains"], ((0, 7), (0, keep["small"].shape[1] - 3 * width)))
    small = jnp.concatenate([keep["small"], row], axis=0)
    bit = 2
    while bit < peers:
        small = small + swap(small, "seq", bit)
        bit *= 2
    gains = small[8:9]
    (wide_out,) = widen([grad_out_s])
    per_seq = w_rates.shape[0]
    return (
        output,
        grad_input,
        keep["joined"],
        lax.dynamic_slice_in_dim(small[: 2 * heads], place[0] * per_seq, per_seq, 1).T,
        small[:CONV, 3 * width :],
        small[CONV, 3 * width : 3 * width + 2 * heads].reshape(heads, 2).T,
        gains[0, :width] / norm_gain,
        gains[0, 2 * width : 2 * width + DV],
        gains[0, width : 2 * width],
        wide_out,
        keep["wide"][1],
        keep["wide"][2],
        keep["wide"][0],
    )


def solution(mesh):
    in_specs = (
        P(("seq", "head"), None),
        P("seq", "head"),
        P("seq", "head"),
        P(None, "head"),
        P(None, "head"),
        P(),
        P(),
        P(),
        P("head", "seq"),
        P("head", "seq"),
        P("head", "seq"),
        P("head", "seq"),
        P(("seq", "head"), None),
    )
    out_specs = (
        P(("seq", "head"), None),
        P(("seq", "head"), None),
        P("seq", "head"),
        P("seq", "head"),
        P(None, "head"),
        P(None, "head"),
        P(),
        P(),
        P(),
        P("head", "seq"),
        P("head", "seq"),
        P("head", "seq"),
        P("head", "seq"),
    )
    return jax.shard_map(
        per_device, mesh=mesh, in_specs=in_specs, out_specs=out_specs, check_vma=False
    )
```

```python
import functools
import jax
import jax.numpy as jnp
from jax import lax
from jax.experimental import pallas as pl
from jax.experimental.pallas import tpu as pltpu
from jax.sharding import PartitionSpec as P

DK = 128
DV = 256
CONV = 4
CHUNK = 128
MIX = 2 * DK + DV
PER = 2 * DK + 2 * DV
GROUP = 4
epsilon = 1e-06
F32 = jnp.float32
BF16 = jnp.bfloat16
HALO = 16
VMEM_LIMIT = 56 * 1024 * 1024
LIGHT = pl.CostEstimate(flops=1, bytes_accessed=1, transcendentals=0)


def shifted(value, axis, steps):
    count = lax.axis_size(axis)
    leading, last = (max(0, -steps), min(count, count - steps))
    return lax.ppermute(value, axis, [(source, source + steps) for source in range(leading, last)])


def mm(a, b, ca=1, cb=0):
    return lax.dot_general(
        a.astype(BF16), b.astype(BF16), (((ca,), (cb,)), ((), ())), preferred_element_type=F32
    )


def mmx(a, b, ca=1, cb=0):
    return lax.dot_general(
        a, b, (((ca,), (cb,)), ((), ())), preferred_element_type=F32, precision=lax.Precision.HIGHEST
    )


def block_columns(spots_ref, b, width):
    return pl.ds(pl.multiple_of(spots_ref[b] * width, 128), width)


def softplus(x):
    return jnp.maximum(x, 0.0) + jnp.log1p(jnp.exp(-jnp.abs(x)))


def sigmoid(x):
    return 1.0 / (1.0 + jnp.exp(-x))


def iotas(n):
    return (
        lax.broadcasted_iota(jnp.int32, (n, n), 0),
        lax.broadcasted_iota(jnp.int32, (n, n), 1),
    )


def inverse_parts(mats, rows, cols):
    base = 16
    near = (rows // base) == (cols // base)
    diag = [jnp.where(near, a, 0.0) for a in mats]
    result = [-d for d in diag]
    power = [mm(d, d) for d in diag]
    span = 2
    while True:
        result = [r + p + mm(r, p) for r, p in zip(result, power)]
        span *= 2
        if span >= base:
            break
        power = [mm(p, p) for p in power]
    size = base
    n = mats[0].shape[0]
    while size < n:
        cross = ((rows // (2 * size)) == (cols // (2 * size))) & ((rows // size) != (cols // size))
        off = [jnp.where(cross, a, 0.0) for a in mats]
        left = [o + mm(r, o) for o, r in zip(off, result)]
        result = [r - x - mm(x, r) for r, x in zip(result, left)]
        size *= 2
    return result


def conv_scratch(first, proj_ref, prev_ref, halo_ref, x_ref, heads, rows):
    for h in range(heads):
        cols = slice(h * PER, h * PER + MIX)
        before = jnp.where(first, halo_ref[:, cols].astype(F32), prev_ref[:, cols].astype(F32))
        x_ref[0:8, h * MIX : (h + 1) * MIX] = before[HALO - 8 :]
        x_ref[8 : 8 + rows, h * MIX : (h + 1) * MIX] = proj_ref[:, cols].astype(F32)


def conv_pre(x_ref, taps_ref, h, row):
    cols = slice(h * MIX, (h + 1) * MIX)
    total = None
    for i in range(CONV):
        part = taps_ref[i : i + 1, cols] * x_ref[pl.ds(row + 8 - (CONV - 1) + i, CHUNK), cols]
        total = part if total is None else total + part
    return total


def unit(a):
    r = lax.rsqrt(jnp.sum(a * a, axis=-1, keepdims=True) + epsilon)
    return a * r, r


def forward_kernel(
    heads, group,
    proj_ref, prev_ref, halo_ref, rates_ref, bias_ref, taps_ref,
    olocal_ref, qmap_ref, state_ref, uw_ref, inv_ref, trans_ref, qe_ref, end_ref,
    x_ref, carry_ref,
):
    step = pl.program_id(0)
    rows_here = CHUNK * group
    conv_scratch(step == 0, proj_ref, prev_ref, halo_ref, x_ref, heads, rows_here)
    ri, ci = iotas(CHUNK)
    included = ri >= ci
    strictly = ri > ci
    lower = jnp.where(included, 1.0, 0.0)
    upper = jnp.where(ri <= ci, 1.0, 0.0)

    @pl.when(step == 0)
    def _():
        for h in range(heads):
            carry_ref[h, :DV, :] = jnp.zeros((DV, DK), F32)
            carry_ref[h, DV:, :] = jnp.where(ri == ci, 1.0, 0.0)

    pairs = [(g, h) for g in range(group) for h in range(heads)]
    logits = rates_ref[...] + bias_ref[...]
    log_decay = -softplus(logits)
    strength = sigmoid(logits)
    cums, cum_rows = [], []
    for g in range(group):
        part = log_decay[g * CHUNK : (g + 1) * CHUNK]
        cums.append(mmx(lower, part))
        cum_rows.append(mmx(part, upper, 0, 0))
    mats, scores, rhs, tails, scaled_q, finals = [], [], [], [], [], []
    for g, h in pairs:
        pre = conv_pre(x_ref, taps_ref, h, g * CHUNK)
        mixed = pre * sigmoid(pre)
        q = unit(mixed[:, :DK])[0] * DK ** (-0.5)
        k = unit(mixed[:, DK : 2 * DK])[0]
        v = mixed[:, 2 * DK :]
        cum = cums[g][:, 2 * h : 2 * h + 1]
        cum_row = cum_rows[g][2 * h : 2 * h + 1, :]
        beta = strength[g * CHUNK : (g + 1) * CHUNK, 2 * h + 1 : 2 * h + 2]
        growth = jnp.exp(cum)
        decays = jnp.where(included, jnp.exp(jnp.where(included, cum - cum_row, 0.0)), 0.0)
        grams = mm(jnp.concatenate([q, k], axis=0), k, 1, 1)
        scores.append(grams[:CHUNK] * decays)
        mats.append(jnp.where(strictly, beta * decays * grams[CHUNK:], 0.0))
        rhs.append(jnp.concatenate([beta * v, beta * growth * k], axis=1))
        last = cum[CHUNK - 1 : CHUNK, :]
        tails.append(k * jnp.exp(last - cum))
        scaled_q.append(growth * q)
        finals.append(jnp.exp(last))
    inverses = inverse_parts(mats, ri, ci)
    solved = [b + mm(r, b) for r, b in zip(inverses, rhs)]
    mixes = [mm(p, u) for p, u in zip(scores, solved)]
    adds = [mm(u, t, 0, 0) for u, t in zip(solved, tails)]
    for j, (g, h) in enumerate(pairs):
        inv_ref[h, g] = inverses[j].astype(BF16)
        uw_ref[h, g] = solved[j].astype(BF16)
        qe_ref[h, g] = (scaled_q[j] - mixes[j][:, DV:]).astype(BF16)
        trans_ref[h, g] = (-adds[j][DV:]).astype(BF16)
        olocal_ref[g * CHUNK : (g + 1) * CHUNK, h * DV : (h + 1) * DV] = mixes[j][:, :DV]
    for h in range(heads):
        now = carry_ref[h]
        for g in range(group):
            j = pairs.index((g, h))
            low = now.astype(BF16)
            state_ref[h, g] = low
            moved = finals[j] * now + mm(low, trans_ref[h, g])
            now = jnp.concatenate([moved[:DV] + adds[j][:DV], moved[DV:]], axis=0)
        carry_ref[h] = now
        end_ref[h] = now.astype(BF16)
    for j, (g, h) in enumerate(pairs):
        both = mm(qe_ref[h, g], state_ref[h, g], 1, 1)
        rows = slice(g * CHUNK, (g + 1) * CHUNK)
        olocal_ref[rows, h * DV : (h + 1) * DV] += both[:, :DV]
        qmap_ref[rows, h * DK : (h + 1) * DK] = both[:, DV:].astype(BF16)


def mixer_forward(projected, halo, rates, bias_row, taps, group):
    total = projected.shape[0]
    heads = rates.shape[1] // 2
    rows = CHUNK * group
    steps = total // rows
    chunks = total // CHUNK
    whole = lambda i: (0, 0)
    saved = lambda a, b: (
        jax.ShapeDtypeStruct((heads, chunks, a, b), BF16),
        pl.BlockSpec((heads, group, a, b), lambda i: (0, i, 0, 0)),
    )
    outs = [
        (jax.ShapeDtypeStruct((total, heads * DV), F32), pl.BlockSpec((rows, heads * DV), lambda i: (i, 0))),
        (jax.ShapeDtypeStruct((total, heads * DK), BF16), pl.BlockSpec((rows, heads * DK), lambda i: (i, 0))),
        saved(DV + DK, DK),
        saved(CHUNK, DV + DK),
        saved(CHUNK, CHUNK),
        saved(DK, DK),
        saved(CHUNK, DK),
        (jax.ShapeDtypeStruct((heads, DV + DK, DK), BF16), pl.BlockSpec((heads, DV + DK, DK), lambda i: (0, 0, 0))),
    ]
    return pl.pallas_call(
        functools.partial(forward_kernel, heads, group),
        grid=(steps,),
        in_specs=[
            pl.BlockSpec((rows, heads * PER), lambda i: (i, 0)),
            pl.BlockSpec((HALO, heads * PER), lambda i: (jnp.maximum(i * (rows // HALO) - 1, 0), 0)),
            pl.BlockSpec((HALO, heads * PER), whole),
            pl.BlockSpec((rows, 2 * heads), lambda i: (i, 0)),
            pl.BlockSpec((1, 2 * heads), whole),
            pl.BlockSpec((CONV, heads * MIX), whole),
        ],
        out_shape=[o[0] for o in outs],
        out_specs=[o[1] for o in outs],
        scratch_shapes=[
            pltpu.VMEM((rows + 8, heads * MIX), F32),
            pltpu.VMEM((heads, DV + DK, DK), F32),
        ],
        compiler_params=pltpu.CompilerParams(vmem_limit_bytes=VMEM_LIMIT),
        cost_estimate=LIGHT,
    )(projected, projected, halo, rates, bias_row, taps)


def backward_kernel(
    heads, group, steps, peers, own,
    proj_ref, prev_ref, halo_ref, rates_ref, bias_ref, taps_ref,
    state_ref, uw_ref, inv_ref, trans_ref, qe_ref,
    dout_ref, value_ref, incoming_ref, place_ref, spots_ref, maps_ref, *refs,
):
    *local_refs, gp_ref, grates_ref, sums_ref, tail_ref, lead_ref, x_ref, d_ref, carry_ref, next_ref = refs
    step = pl.program_id(0)
    rows_here = CHUNK * group
    conv_scratch(step == steps - 1, proj_ref, prev_ref, halo_ref, x_ref, heads, rows_here)
    ri, ci = iotas(CHUNK)
    included = ri >= ci
    strictly = ri > ci
    lower = jnp.where(included, 1.0, 0.0)
    upper = jnp.where(ri <= ci, 1.0, 0.0)

    @pl.when(step == 0)
    def _():
        for h in range(heads):
            grad = jnp.zeros((DV, DK), F32)
            for turn in range(peers - 1):
                source = peers - 1 - turn
                share = jnp.zeros((DV, DK), F32)
                for b, local_ref in enumerate(local_refs):
                    here = (place_ref[0] ^ b) == source if peers == 4 else b == source
                    share = jnp.where(here, local_ref[h].astype(F32), share)
                moved = mm(grad, maps_ref[source, h, DV:, :], 1, 1) + share
                grad = jnp.where(source > place_ref[0], moved, grad)
            carry_ref[h] = grad
        d_ref[rows_here : rows_here + 8, :] = jnp.zeros((8, heads * MIX), F32)
        sums_ref[...] = jnp.zeros_like(sums_ref)

    @pl.when(step > 0)
    def _():
        d_ref[rows_here : rows_here + 8, :] = d_ref[0:8, :]

    def near_row(g):
        first = ((steps - 1 - step) * group + g) * CHUNK
        return pl.multiple_of(spots_ref[first // own] * own + first % own, CHUNK)

    pairs = [(g, h) for g in range(group) for h in range(heads)]
    logits = rates_ref[...] + bias_ref[...]
    log_decay = -softplus(logits)
    strength = sigmoid(logits)
    cums, cum_rows = [], []
    for g in range(group):
        part = log_decay[g * CHUNK : (g + 1) * CHUNK]
        cums.append(mmx(lower, part))
        cum_rows.append(mmx(part, upper, 0, 0))
    douts, injections = [], []
    for g, h in pairs:
        do = dout_ref[g * CHUNK : (g + 1) * CHUNK, h * DV : (h + 1) * DV]
        douts.append(do)
        injections.append(mm(do, qe_ref[h, g], 0, 0))
    for h in range(heads):
        now = carry_ref[h]
        for g in reversed(range(group)):
            j = pairs.index((g, h))
            last = cums[g][CHUNK - 1 : CHUNK, 2 * h : 2 * h + 1]
            next_ref[h, g] = now
            now = jnp.exp(last) * now + mm(now, trans_ref[h, g], 1, 1) + injections[j]
        carry_ref[h] = now
    lane = lax.broadcasted_iota(jnp.int32, (CHUNK, 2 * heads), 1)
    row_col = lax.broadcasted_iota(jnp.int32, (CHUNK, 1), 0)
    dcums = [jnp.zeros((CHUNK, 2 * heads), F32) for _ in range(group)]
    dlogits = [jnp.zeros((CHUNK, 2 * heads), F32) for _ in range(group)]
    for j, (g, h) in enumerate(pairs):
        pre = conv_pre(x_ref, taps_ref, h, g * CHUNK)
        sig = sigmoid(pre)
        mixed = pre * sig
        slope = sig * (1.0 + pre * (1.0 - sig))
        uq, rq = unit(mixed[:, :DK])
        q = uq * DK ** (-0.5)
        k, rk = unit(mixed[:, DK : 2 * DK])
        v = mixed[:, 2 * DK :]
        cum = cums[g][:, 2 * h : 2 * h + 1]
        cum_row = cum_rows[g][2 * h : 2 * h + 1, :]
        beta = strength[g * CHUNK : (g + 1) * CHUNK, 2 * h + 1 : 2 * h + 2]
        growth = jnp.exp(cum)
        decays = jnp.where(included, jnp.exp(jnp.where(included, cum - cum_row, 0.0)), 0.0)
        qb, kb = q.astype(BF16), k.astype(BF16)
        grams = mm(jnp.concatenate([qb, kb], axis=0), kb, 1, 1)
        scores = grams[:CHUNK] * decays
        last = cum[CHUNK - 1 : CHUNK, :]
        fade = jnp.exp(last - cum)
        tail = k * fade
        sl = state_ref[h, g]
        state = sl[:DV].astype(F32) + mm(incoming_ref[h], sl[DV:])
        after = next_ref[h, g]
        afterb = after.astype(BF16)
        stateb = state.astype(BF16)
        uw = uw_ref[h, g]
        errors = uw[:, :DV].astype(F32) - mm(uw[:, DV:], stateb, 1, 1)
        eb = errors.astype(BF16)
        do = douts[j]
        de = mm(scores, do, 0, 0) + mm(tail, afterb, 1, 1)
        db = de + mm(inv_ref[h, g], de, 0, 0)
        dbb = db.astype(BF16)
        stacked = jnp.concatenate([do, dbb], axis=0)
        against_e = mm(stacked, eb, 1, 1)
        against_s = mm(stacked, stateb)
        dp = against_e[:CHUNK]
        da = jnp.where(strictly, -against_e[CHUNK:], 0.0)
        dos = against_s[:CHUNK]
        dbs = against_s[CHUNK:]
        dpd = dp * decays
        dg = da * beta * decays
        dtail = mm(eb, afterb)
        dq = mm(dpd, kb) + growth * dos
        sym = dg + dg.T
        dk = (
            mm(jnp.concatenate([dpd.T, sym], axis=1), jnp.concatenate([qb, kb], axis=0))
            - beta * growth * dbs
            + fade * dtail
        )
        dv = beta * db
        dlogit = (1.0 - beta) * jnp.sum(db * errors, axis=1, keepdims=True)
        tdot = jnp.sum(tail * dtail, axis=1, keepdims=True)
        out = value_ref[g * CHUNK : (g + 1) * CHUNK, h * DV : (h + 1) * DV].astype(F32)
        dcum = jnp.sum(do.astype(F32) * out, axis=1, keepdims=True) - beta * jnp.sum(
            v * db, axis=1, keepdims=True
        )
        at_end = jnp.exp(last) * jnp.sum(jnp.sum(after * state, axis=1, keepdims=True), axis=0, keepdims=True) + jnp.sum(
            tdot, axis=0, keepdims=True
        )
        dcum = dcum + jnp.where(row_col == CHUNK - 1, at_end, 0.0)
        dcums[g] = jnp.where(lane == 2 * h, dcum, dcums[g])
        dlogits[g] = jnp.where(lane == 2 * h + 1, dlogit, dlogits[g])
        dq = dq * DK ** (-0.5)
        dmq = rq * (dq - uq * jnp.sum(uq * dq, axis=1, keepdims=True))
        dmk = rk * (dk - k * jnp.sum(k * dk, axis=1, keepdims=True))
        d_ref[g * CHUNK : (g + 1) * CHUNK, h * MIX : (h + 1) * MIX] = (
            jnp.concatenate([dmq, dmk, dv], axis=1) * slope
        )
    for g in range(group):
        rows = slice(g * CHUNK, (g + 1) * CHUNK)
        dld = mmx(upper, dcums[g])
        drate = jnp.where(lane % 2 == 0, -sigmoid(logits[rows]) * dld, dlogits[g])
        grates_ref[pl.ds(near_row(g), CHUNK), :] = drate
        sums_ref[CONV : CONV + 1, : 2 * heads] += jnp.sum(drate, axis=0, keepdims=True)
    for g, h in pairs:
        cols = slice(h * MIX, (h + 1) * MIX)
        row = g * CHUNK
        dpre = d_ref[pl.ds(row, CHUNK), cols]
        total = None
        for i in range(CONV):
            sums_ref[i : i + 1, cols] += jnp.sum(
                dpre * x_ref[pl.ds(row + 8 - (CONV - 1) + i, CHUNK), cols], axis=0, keepdims=True
            )
            part = taps_ref[i : i + 1, cols] * d_ref[pl.ds(row + CONV - 1 - i, CHUNK), cols]
            total = part if total is None else total + part
        gp_ref[pl.ds(near_row(g), CHUNK), cols] = total.astype(BF16)
        if g == group - 1:
            @pl.when(step == 0)
            def _(total=total, cols=cols):
                tail_ref[:, cols] = total[CHUNK - HALO :]

    @pl.when(step == steps - 1)
    def _():
        lead_ref[...] = d_ref[0:8, :]


def mixer_backward(projected, halo, rates, bias_row, taps, saved, dout, value, incoming, place, spots, maps, local, group):
    state, uw, inv, trans, qe = saved
    total = projected.shape[0]
    heads = rates.shape[1] // 2
    rows = CHUNK * group
    steps = total // rows
    whole = lambda i: (0, 0)
    flip = lambda i: (steps - 1 - i, 0)
    keep = lambda a, b: pl.BlockSpec((heads, group, a, b), lambda i: (0, steps - 1 - i, 0, 0))
    return pl.pallas_call(
        functools.partial(backward_kernel, heads, group, steps, maps.shape[0], total // spots.shape[0]),
        grid=(steps,),
        in_specs=[
            pl.BlockSpec((rows, heads * PER), flip),
            pl.BlockSpec((HALO, heads * PER), lambda i: (jnp.maximum((steps - 1 - i) * (rows // HALO) - 1, 0), 0)),
            pl.BlockSpec((HALO, heads * PER), whole),
            pl.BlockSpec((rows, 2 * heads), flip),
            pl.BlockSpec((1, 2 * heads), whole),
            pl.BlockSpec((CONV, heads * MIX), whole),
            keep(DV + DK, DK),
            keep(CHUNK, DV + DK),
            keep(CHUNK, CHUNK),
            keep(DK, DK),
            keep(CHUNK, DK),
            pl.BlockSpec((rows, heads * DV), flip),
            pl.BlockSpec((rows, heads * DV), flip),
            pl.BlockSpec(incoming.shape, lambda i: (0, 0, 0)),
            pl.BlockSpec(memory_space=pltpu.SMEM),
            pl.BlockSpec(memory_space=pltpu.SMEM),
            pl.BlockSpec(maps.shape, lambda i: (0, 0, 0, 0)),
            *[pl.BlockSpec(part.shape, lambda i: (0, 0, 0)) for part in local],
        ],
        out_shape=[
            jax.ShapeDtypeStruct((total, heads * MIX), BF16),
            jax.ShapeDtypeStruct((total, 2 * heads), F32),
            jax.ShapeDtypeStruct((8, heads * MIX), F32),
            jax.ShapeDtypeStruct((HALO, heads * MIX), F32),
            jax.ShapeDtypeStruct((8, heads * MIX), F32),
        ],
        out_specs=[
            pl.BlockSpec((total, heads * MIX), whole),
            pl.BlockSpec((total, 2 * heads), whole),
            pl.BlockSpec((8, heads * MIX), whole),
            pl.BlockSpec((HALO, heads * MIX), whole),
            pl.BlockSpec((8, heads * MIX), whole),
        ],
        scratch_shapes=[
            pltpu.VMEM((rows + 8, heads * MIX), F32),
            pltpu.VMEM((rows + 8, heads * MIX), F32),
            pltpu.VMEM((heads, DV, DK), F32),
            pltpu.VMEM((heads, group, DV, DK), F32),
        ],
        compiler_params=pltpu.CompilerParams(vmem_limit_bytes=VMEM_LIMIT),
        cost_estimate=LIGHT,
    )(projected, projected, halo, rates, bias_row, taps, state, uw, inv, trans, qe, dout, value, incoming, place, spots, maps, *local)


def pair_rows(ids_ref, step, which, rows):
    return pl.ds(pl.multiple_of(ids_ref[2 * step + which] * rows, rows), rows)


def gate_kernel(heads, peers, ids_ref, place_ref, maps_ref, gain_ref, w_ref, *refs):
    olocal_refs, qmap_refs = refs[0:2], refs[2:4]
    gate_refs = refs[4 : 4 + 2 * heads]
    value_ref, gated_ref, part_ref, incoming_ref = refs[4 + 2 * heads :]
    step = pl.program_id(0)

    @pl.when(step == 0)
    def _():
        for h in range(heads):
            state = jnp.zeros((DV, DK), F32)
            for source in range(peers - 1):
                moved = mm(state, maps_ref[source, h, DV:, :]) + maps_ref[source, h, :DV, :].astype(F32)
                state = jnp.where(source < place_ref[0], moved, state)
            incoming_ref[h] = state.astype(BF16)

    rows = olocal_refs[0].shape[0]
    for h in range(heads):
        cols = slice(h * DV, (h + 1) * DV)
        query_map = jnp.concatenate([ref[:, h * DK : (h + 1) * DK] for ref in qmap_refs], axis=0)
        out_local = jnp.concatenate([ref[:, cols] for ref in olocal_refs], axis=0)
        low = (out_local + mm(query_map, incoming_ref[h], 1, 1)).astype(BF16)
        for which in range(2):
            value_ref[pair_rows(ids_ref, step, which, rows), cols] = low[which * rows : (which + 1) * rows]
        value = low.astype(F32)
        normed = value * lax.rsqrt(jnp.mean(value * value, axis=-1, keepdims=True) + epsilon)
        gate = jnp.concatenate([gate_refs[2 * h + which][...] for which in range(2)], axis=0).astype(F32)
        gated_ref[:, cols] = (normed * gain_ref[...] * (gate * sigmoid(gate))).astype(BF16)
    part_ref[...] = mm(gated_ref[...], w_ref[...]).astype(BF16)


def gate_blocks(heads, rows):
    full = lambda wide: [
        pl.BlockSpec((rows, wide), lambda i, *s, which=which: (s[0][2 * i + which], 0)) for which in range(2)
    ]
    gates = [
        pl.BlockSpec(
            (rows, DV), lambda i, *s, which=which, h=h: (s[0][2 * i + which], (h + 1) * (PER // DV) - 1)
        )
        for h in range(heads)
        for which in range(2)
    ]
    return full, gates


def gate_output(ids, place, maps, out_local, query_map, projected, gain, w_out):
    heads = maps.shape[1]
    total = projected.shape[0]
    count = ids.shape[0]
    rows = total // count
    width = w_out.shape[1]
    mine = lambda i, *s: (i, 0)
    whole = lambda i, *s: (0, 0)
    full, gates = gate_blocks(heads, rows)
    return pl.pallas_call(
        functools.partial(gate_kernel, heads, maps.shape[0]),
        grid_spec=pltpu.PrefetchScalarGridSpec(
            num_scalar_prefetch=2,
            grid=(count // 2,),
            in_specs=[
                pl.BlockSpec(maps.shape, lambda i, *s: (0, 0, 0, 0)),
                pl.BlockSpec((1, DV), whole),
                pl.BlockSpec(w_out.shape, whole),
                *full(heads * DV),
                *full(heads * DK),
                *gates,
            ],
            out_specs=[
                pl.BlockSpec((total, heads * DV), whole),
                pl.BlockSpec((2 * rows, heads * DV), mine),
                pl.BlockSpec((2 * rows, width), mine),
                pl.BlockSpec((heads, DV, DK), lambda i, *s: (0, 0, 0)),
            ],
        ),
        out_shape=[
            jax.ShapeDtypeStruct((total, heads * DV), BF16),
            jax.ShapeDtypeStruct((total, heads * DV), BF16),
            jax.ShapeDtypeStruct((total, width), BF16),
            jax.ShapeDtypeStruct((heads, DV, DK), BF16),
        ],
        compiler_params=pltpu.CompilerParams(vmem_limit_bytes=VMEM_LIMIT),
        cost_estimate=LIGHT,
    )(
        ids, place, maps, gain, w_out, out_local, out_local, query_map, query_map,
        *[projected] * (2 * heads),
    )


def gate_back_kernel(heads, ids_ref, branch_ref, gain_ref, w_ref, *refs):
    value_refs, qmap_refs = refs[0:2], refs[2:4]
    gate_refs = refs[4 : 4 + 2 * heads]
    ggate_ref, dout_ref, gain_grad_ref, local_ref, sum_ref = refs[4 + 2 * heads :]
    step = pl.program_id(0)

    @pl.when(step == 0)
    def _():
        gain_grad_ref[...] = jnp.zeros_like(gain_grad_ref)
        sum_ref[...] = jnp.zeros_like(sum_ref)

    rows = value_refs[0].shape[0]
    grads = mm(branch_ref[...], w_ref[...], 1, 1)
    gain = gain_ref[...]
    for h in range(heads):
        cols = slice(h * DV, (h + 1) * DV)
        value = jnp.concatenate([ref[:, cols] for ref in value_refs], axis=0).astype(F32)
        inverse = lax.rsqrt(jnp.mean(value * value, axis=-1, keepdims=True) + epsilon)
        normed = value * inverse
        gate = jnp.concatenate([gate_refs[2 * h + which][...] for which in range(2)], axis=0).astype(F32)
        sig = sigmoid(gate)
        grad = grads[:, cols]
        through = grad * (gate * sig)
        ggate_ref[:, cols] = (grad * normed * gain * (sig * (1.0 + gate * (1.0 - sig)))).astype(BF16)
        gain_grad_ref[...] += jnp.sum(through * normed, axis=0, keepdims=True)
        scaled = through * gain
        low = (inverse * (scaled - normed * jnp.mean(scaled * normed, axis=-1, keepdims=True))).astype(BF16)
        for which in range(2):
            dout_ref[pair_rows(ids_ref, step, which, rows), cols] = low[which * rows : (which + 1) * rows]
        query_map = jnp.concatenate([ref[:, h * DK : (h + 1) * DK] for ref in qmap_refs], axis=0)
        sum_ref[h] += mm(low, query_map, 0, 0)

    @pl.when(step == pl.num_programs(0) - 1)
    def _():
        local_ref[...] = sum_ref[...].astype(BF16)


def gate_backward(ids, branch, w_out, value, projected, query_map, gain, heads):
    total = projected.shape[0]
    count = ids.shape[0]
    rows = total // count
    mine = lambda i, *s: (i, 0)
    whole = lambda i, *s: (0, 0)
    full, gates = gate_blocks(heads, rows)
    return pl.pallas_call(
        functools.partial(gate_back_kernel, heads),
        grid_spec=pltpu.PrefetchScalarGridSpec(
            num_scalar_prefetch=1,
            grid=(count // 2,),
            in_specs=[
                pl.BlockSpec((2 * rows, branch.shape[1]), mine),
                pl.BlockSpec((1, DV), whole),
                pl.BlockSpec(w_out.shape, whole),
                *full(heads * DV),
                *full(heads * DK),
                *gates,
            ],
            out_specs=[
                pl.BlockSpec((2 * rows, heads * DV), mine),
                pl.BlockSpec((total, heads * DV), whole),
                pl.BlockSpec((1, DV), whole),
                pl.BlockSpec((heads, DV, DK), lambda i, *s: (0, 0, 0)),
            ],
            scratch_shapes=[pltpu.VMEM((heads, DV, DK), F32)],
        ),
        out_shape=[
            jax.ShapeDtypeStruct((total, heads * DV), BF16),
            jax.ShapeDtypeStruct((total, heads * DV), BF16),
            jax.ShapeDtypeStruct((1, DV), F32),
            jax.ShapeDtypeStruct((heads, DV, DK), BF16),
        ],
        compiler_params=pltpu.CompilerParams(vmem_limit_bytes=VMEM_LIMIT),
        cost_estimate=LIGHT,
    )(
        ids, branch, gain, w_out, value, value, query_map, query_map, *[projected] * (2 * heads)
    )


def project_kernel(layout, pieces, ids_ref, spots_ref, rate_ref, *refs):
    x_refs = refs[: len(layout)]
    w_refs = refs[len(layout) : len(layout) + pieces]
    out_ref, rates_ref = refs[len(layout) + pieces :]
    rows = out_ref.shape[0] // ids_ref.shape[0]
    blocks = {}
    for (k, _), ref in zip(layout, x_refs):
        blocks.setdefault(k, []).append(ref)
    ks = list(blocks)
    for first in range(0, len(ks), 2):
        group = ks[first : first + 2]
        group_refs = [ref for k in group for ref in blocks[k]]
        x = jnp.concatenate([ref[...] for ref in group_refs], axis=0)
        total = None
        for b, w_ref in enumerate(w_refs):
            cols = block_columns(spots_ref, b, w_ref.shape[0])
            share = mm(jnp.concatenate([ref[:, cols] for ref in group_refs], axis=0), w_ref[...])
            total = share if total is None else total + share
        total = total.astype(BF16)
        rates = mm(x, rate_ref[...], 1, 1)
        for i, k in enumerate(group):
            place = pl.ds(pl.multiple_of(ids_ref[k] * rows, rows), rows)
            out_ref[place, :] = total[i * rows : (i + 1) * rows]
            rates_ref[place, :] = rates[i * rows : (i + 1) * rows]


def layout_of(found, total):
    rows = found[0][0].shape[0]
    count = total // rows
    ks = [0] + [k for s in range(1, count // 2) for k in (s, count - s)] + [count // 2]
    layout, arrays = [], []
    for k in ks:
        start = k * rows
        for piece in found.get(k, ()):
            layout.append((k, start))
            arrays.append(piece)
            start += piece.shape[0]
    return layout, arrays


def project(ids, spots, found, w_mix, w_rate):
    total = ids.shape[0] * found[0][0].shape[0]
    layout, arrays = layout_of(found, total)
    cols = w_mix[0].shape[1]
    rates = w_rate.shape[0]
    whole = lambda shape: pl.BlockSpec(shape, lambda i, ids, spots: (0, 0))
    return pl.pallas_call(
        functools.partial(project_kernel, layout, len(w_mix)),
        grid_spec=pltpu.PrefetchScalarGridSpec(
            num_scalar_prefetch=2,
            grid=(1,),
            in_specs=[whole(a.shape) for a in (w_rate, *arrays, *w_mix)],
            out_specs=[whole((total, cols)), whole((total, rates))],
        ),
        out_shape=[
            jax.ShapeDtypeStruct((total, cols), BF16),
            jax.ShapeDtypeStruct((total, rates), F32),
        ],
        compiler_params=pltpu.CompilerParams(vmem_limit_bytes=VMEM_LIMIT),
        cost_estimate=LIGHT,
    )(ids, spots, w_rate, *arrays, *w_mix)


def normed_back_kernel(pieces, blocks, spots_ref, *refs):
    mixes, gates, rates, normed = (refs[i * blocks : (i + 1) * blocks] for i in range(4))
    rate_ref, before_ref = refs[4 * blocks : 4 * blocks + 2]
    w_refs = refs[4 * blocks + 2 : 4 * blocks + 2 + pieces]
    part_ref, sums_ref = refs[4 * blocks + 2 + pieces :]
    heads = gates[0].shape[1] // DV
    left = jnp.concatenate(
        [
            jnp.concatenate([ref[:, h * size : (h + 1) * size] for ref in group], axis=0)
            for h in range(heads)
            for group, size in ((mixes, MIX), (gates, DV))
        ],
        axis=1,
    )
    rate = jnp.concatenate([ref[...].astype(BF16) for ref in rates], axis=0)
    count = rate.shape[1]
    sums_ref[...] = before_ref[...]
    for b, w_ref in enumerate(w_refs):
        cols = block_columns(spots_ref, b, w_ref.shape[0])
        part = mm(left, w_ref[...], 1, 1) + mm(rate, rate_ref[:, cols])
        part_ref[:, cols] = part.astype(BF16)
        right = jnp.concatenate([ref[:, cols] for ref in normed], axis=0)
        sums_ref[:count, cols] += mm(rate, right, 0, 0)
        sums_ref[4:5, cols] += jnp.sum(part * right.astype(F32), axis=0, keepdims=True)


def normed_back(spots, order, blocks, grad_mixed, grad_gates, grad_rates, normed, w_mix, w_rate, before):
    total, width = normed.shape
    rows = total // blocks
    rates = w_rate.shape[0]
    count = len(order)
    block = lambda k, wide: pl.BlockSpec((rows, wide), lambda i, spots: (k, 0))
    whole = lambda i, spots: (0, 0)
    return pl.pallas_call(
        functools.partial(normed_back_kernel, len(w_mix), count),
        grid_spec=pltpu.PrefetchScalarGridSpec(
            num_scalar_prefetch=1,
            grid=(1,),
            in_specs=[
                *[block(k, grad_mixed.shape[1]) for k in order],
                *[block(k, grad_gates.shape[1]) for k in order],
                *[block(k, rates) for k in order],
                *[block(k, width) for k in order],
                pl.BlockSpec((rates, width), whole),
                pl.BlockSpec((8, width), whole),
                *[pl.BlockSpec(w.shape, whole) for w in w_mix],
            ],
            out_specs=[pl.BlockSpec((count * rows, width), whole), pl.BlockSpec((8, width), whole)],
        ),
        out_shape=[
            jax.ShapeDtypeStruct((count * rows, width), BF16),
            jax.ShapeDtypeStruct((8, width), F32),
        ],
        compiler_params=pltpu.CompilerParams(vmem_limit_bytes=VMEM_LIMIT),
        cost_estimate=LIGHT,
    )(
        spots,
        *[grad_mixed] * count,
        *[grad_gates] * count,
        *[grad_rates] * count,
        *[normed] * count,
        w_rate,
        before,
        *w_mix,
    )


def stack_kernel(layout, *refs):
    out_ref = refs[len(layout)]
    for (_, start), ref in zip(layout, refs):
        out_ref[start : start + ref.shape[0], :] = ref[...]


def stacked(found, total):
    layout, arrays = layout_of(found, total)
    return pl.pallas_call(
        functools.partial(stack_kernel, layout),
        out_shape=jax.ShapeDtypeStruct((total, arrays[0].shape[1]), arrays[0].dtype),
        compiler_params=pltpu.CompilerParams(vmem_limit_bytes=VMEM_LIMIT),
        cost_estimate=LIGHT,
    )(*arrays)


def finish_kernel(first_ref, second_ref, buffer_ref, out_ref):
    half = first_ref.shape[0]
    out_ref[:half, :] = first_ref[...]
    out_ref[half:, :] = second_ref[...]


def finish_stack(buffer, pieces, k):
    half, width = pieces[0].shape
    whole = pl.BlockSpec((half, width), lambda i: (0, 0))
    return pl.pallas_call(
        finish_kernel,
        grid=(1,),
        in_specs=[whole, whole, pl.BlockSpec(memory_space=pl.ANY)],
        out_specs=pl.BlockSpec((2 * half, width), lambda i: (k, 0)),
        out_shape=jax.ShapeDtypeStruct(buffer.shape, buffer.dtype),
        input_output_aliases={2: 0},
        cost_estimate=LIGHT,
    )(*pieces, buffer)


def outer_kernel(left_ref, right_ref, out_ref):
    out_ref[...] = mm(left_ref[...], right_ref[...], 0, 0).astype(BF16)


def outer(left, right):
    total, m = left.shape
    n = right.shape[1]
    by_rows = m % 512 == 0 and m > 512
    rows = 512 if by_rows else m
    cols = n if by_rows or n % 512 else 512
    return pl.pallas_call(
        outer_kernel,
        grid=(m // rows, n // cols),
        in_specs=[
            pl.BlockSpec((total, rows), lambda i, j: (0, i)),
            pl.BlockSpec((total, cols), lambda i, j: (0, j)),
        ],
        out_specs=pl.BlockSpec((rows, cols), lambda i, j: (i, j)),
        out_shape=jax.ShapeDtypeStruct((m, n), BF16),
        compiler_params=pltpu.CompilerParams(vmem_limit_bytes=VMEM_LIMIT),
        cost_estimate=LIGHT,
    )(left, right)


def turn_kernel(count, *refs):
    for i in range(count):
        refs[count + i][...] = refs[i][...].astype(F32).T.astype(BF16)


def turned(arrays):
    rows, width = arrays[0].shape
    step = 512
    return pl.pallas_call(
        functools.partial(turn_kernel, len(arrays)),
        grid=(width // step,),
        in_specs=[pl.BlockSpec((rows, step), lambda i: (0, i))] * len(arrays),
        out_specs=[pl.BlockSpec((step, rows), lambda i: (i, 0))] * len(arrays),
        out_shape=[jax.ShapeDtypeStruct((width, rows), BF16)] * len(arrays),
        compiler_params=pltpu.CompilerParams(vmem_limit_bytes=VMEM_LIMIT),
        cost_estimate=LIGHT,
    )(*arrays)


def widen_kernel(count, *refs):
    for i in range(count):
        refs[count + i][...] = refs[i][...].astype(F32)


def widen(arrays):
    steps = 4
    specs = [pl.BlockSpec((a.shape[0] // steps, a.shape[1]), lambda i: (i, 0)) for a in arrays]
    return pl.pallas_call(
        functools.partial(widen_kernel, len(arrays)),
        grid=(steps,),
        in_specs=specs,
        out_specs=specs,
        out_shape=[jax.ShapeDtypeStruct(a.shape, F32) for a in arrays],
        compiler_params=pltpu.CompilerParams(vmem_limit_bytes=VMEM_LIMIT),
        cost_estimate=LIGHT,
    )(*arrays)


def join_kernel(heads, mix_ref, gate_ref, out_ref):
    for h in range(heads):
        out_ref[:, h * PER : h * PER + MIX] = mix_ref[:, h * MIX : (h + 1) * MIX].astype(F32)
        out_ref[:, h * PER + MIX : (h + 1) * PER] = gate_ref[:, h * DV : (h + 1) * DV].astype(F32)


def join_heads(mix, gate):
    rows = mix.shape[0]
    heads = gate.shape[1] // DV
    steps = 4
    spec = lambda wide: pl.BlockSpec((rows // steps, wide), lambda i: (i, 0))
    return pl.pallas_call(
        functools.partial(join_kernel, heads),
        grid=(steps,),
        in_specs=[spec(mix.shape[1]), spec(gate.shape[1])],
        out_specs=spec(heads * PER),
        out_shape=jax.ShapeDtypeStruct((rows, heads * PER), F32),
        compiler_params=pltpu.CompilerParams(vmem_limit_bytes=VMEM_LIMIT),
        cost_estimate=LIGHT,
    )(mix, gate)


def times_kernel(left_ref, right_ref, out_ref):
    out_ref[...] = mm(left_ref[...], right_ref[...])


def times(left, right):
    total, depth = left.shape
    n = right.shape[1]
    rows = 256
    return pl.pallas_call(
        times_kernel,
        grid=(total // rows,),
        in_specs=[
            pl.BlockSpec((rows, depth), lambda i: (i, 0)),
            pl.BlockSpec((depth, n), lambda i: (0, 0)),
        ],
        out_specs=pl.BlockSpec((rows, n), lambda i: (i, 0)),
        out_shape=jax.ShapeDtypeStruct((total, n), F32),
        compiler_params=pltpu.CompilerParams(vmem_limit_bytes=VMEM_LIMIT),
        cost_estimate=LIGHT,
    )(left, right)


def finish_all_kernel(heads, count, mix_ref, gate_ref, *refs):
    join_kernel(heads, mix_ref, gate_ref, refs[count])
    for i in range(count):
        refs[count + 1 + i][...] = refs[i][...].astype(F32)


def finish_all(mix, gate, others):
    heads = gate.shape[1] // DV
    steps = 4
    spec = lambda a, wide: pl.BlockSpec((a.shape[0] // steps, wide), lambda i: (i, 0))
    plain = [spec(a, a.shape[1]) for a in others]
    return pl.pallas_call(
        functools.partial(finish_all_kernel, heads, len(others)),
        grid=(steps,),
        in_specs=[spec(mix, mix.shape[1]), spec(gate, gate.shape[1]), *plain],
        out_specs=[spec(mix, heads * PER), *plain],
        out_shape=[
            jax.ShapeDtypeStruct((mix.shape[0], heads * PER), F32),
            *[jax.ShapeDtypeStruct(a.shape, F32) for a in others],
        ],
        compiler_params=pltpu.CompilerParams(vmem_limit_bytes=VMEM_LIMIT),
        cost_estimate=LIGHT,
    )(mix, gate, *others)
def ring_order(count):
    return list(range(0, count, 2)) + list(range(1, count, 2))[::-1]


def ring_step(value, axis, step):
    order = ring_order(lax.axis_size(axis))
    count = len(order)
    return lax.ppermute(value, axis, [(order[i], order[(i + step) % count]) for i in range(count)])


def ring_ids(axis):
    order = ring_order(lax.axis_size(axis))
    count = len(order)
    place = {device: i for i, device in enumerate(order)}
    ahead = [[order[(place[device] + k) % count] for k in range(count)] for device in range(count)]
    back = [[row.index(device) for device in range(count)] for row in ahead]
    row = lax.dynamic_index_in_dim(
        jnp.array([a + b for a, b in zip(ahead, back)], jnp.int32), lax.axis_index(axis), 0, False
    )
    return row[:count], row[count:]


def after(value, *earlier):
    return lax.optimization_barrier((value, *earlier))[0]


def together(*values):
    return lax.optimization_barrier(values)


def window(fillers, hop, gate):
    return fillers[hop](lambda value: after(value, gate)) if hop in fillers else ()


def ring_gather(shard, axis, fillers={}, stack=True):
    count = lax.axis_size(axis)
    far = count // 2
    half = shard.shape[0] // 2
    total = count * shard.shape[0]
    found = {0: [shard]}
    forward = backward = shard
    buffer = None
    for hop in range(1, far + 1):
        gate = forward
        extra = list(window(fillers, hop, gate))
        if hop < far:
            forward = ring_step(forward, axis, 1)
            backward = ring_step(backward, axis, -1)
            found[count - hop] = [forward]
            found[hop] = [backward]
        else:
            if stack:
                buffer = stacked({k: [after(p, gate) for p in ps] for k, ps in found.items()}, total)
                extra.append(buffer)
            forward = ring_step(forward[:half], axis, 1)
            backward = ring_step(backward[half:], axis, -1)
            found[hop] = [forward, backward]
        forward, backward, *_ = together(forward, backward, *extra)
    found[far] = [forward, backward]
    return finish_stack(buffer, found[far], far) if stack else found


def ring_scatter(take, rows, axis, fillers={}):
    count = lax.axis_size(axis)
    far = count // 2
    size = rows // 2
    flows = [[take(far, 0, size), None], [None, take(far, size, size)]]
    gate = take(far, 0, size)
    for hop in range(1, far + 1):
        flows = [
            [flow[way] if flow[way] is None else ring_step(flow[way], axis, 1 - 2 * way) for way in range(2)]
            for flow in flows
        ]
        extra = window(fillers, hop, gate)
        flat = together(*[a for flow in flows for a in flow if a is not None], *extra)
        flat = iter(flat)
        flows = [[None if a is None else next(flat) for a in flow] for flow in flows]
        s = far - hop
        if s:
            for part, flow in enumerate(flows):
                for way, k in enumerate((s, count - s)):
                    piece = take(k, part * size, size)
                    flow[way] = piece if flow[way] is None else flow[way] + piece
            gate = flows[0][0]
    totals = [
        take(0, part * size, size).astype(F32) + flow[0].astype(F32) + flow[1].astype(F32)
        for part, flow in enumerate(flows)
    ]
    return jnp.concatenate(totals, axis=0)


def near_rows(array, rows):
    return lambda k, start, size: lax.slice_in_dim(array, k * rows + start, k * rows + start + size, axis=0)


def swap(value, axis, bit):
    count = lax.axis_size(axis)
    return lax.ppermute(value, axis, [(i, i ^ bit) for i in range(count)])


def pair_spots(axis):
    count = lax.axis_size(axis)
    order = jnp.arange(count, dtype=jnp.int32)
    return lax.axis_index(axis) ^ order if count == 4 else order


def pair_far(shard, axis, *pins):
    if lax.axis_size(axis) != 4:
        return lax.all_gather(shard, axis)
    return swap(after(shard, *pins), axis, 2)


def pair_gather(shard, far, axis, *pins):
    count = lax.axis_size(axis)
    if count != 4:
        return [far[b] for b in range(count)]
    return [shard, swap(after(shard, *pins), axis, 1), far, swap(after(far, *pins), axis, 1)]


def seq_shards(value, axis):
    if lax.axis_size(axis) != 4:
        whole = lax.all_gather(value, axis)
        return [whole[b] for b in range(lax.axis_size(axis))]
    return [value] + [swap(value, axis, b) for b in range(1, 4)]


def butterfly(value, axis):
    bit = 1
    while bit < lax.axis_size(axis):
        value = value + swap(value, axis, bit)
        bit *= 2
    return value


def per_device(
    tokens,
    w_qkvg,
    w_rates,
    conv_weight,
    head_bias,
    norm_gain,
    head_gain,
    mlp_gain,
    w_out,
    w_ff_gate,
    w_ff_up,
    w_ff_down,
    cotangent,
):
    heads = head_bias.shape[1]
    own_rows = tokens.shape[0]
    contract = (((1,), (1,)), ((), ()))
    rows_first = (((0,), (0,)), ((), ()))
    dot = lambda a, b, dims: lax.dot_general(a, b, dims, preferred_element_type=F32)
    plain = (((1,), (0,)), ((), ()))
    ids, near_spots = ring_ids("head")
    spots = pair_spots("seq")
    place = lax.axis_index("seq").reshape(1)
    gain_row = head_gain.reshape(1, DV)
    bias_row = head_bias.T.reshape(1, 2 * heads)
    peers = lax.axis_size("seq")
    width = tokens.shape[1]
    keep = {}
    mix_far = pair_far(w_qkvg, "seq")
    inputs = tokens.astype(F32)
    inverse_one = lax.rsqrt(jnp.mean(inputs * inputs, axis=-1, keepdims=True) + epsilon)
    norm_normed = inputs * inverse_one
    hops = lax.axis_size("head") // 2
    last_window = hops

    rate_shard = w_rates.T
    if peers == 4:
        w_rate = jnp.zeros((2 * heads, width), BF16)
        for b in range(4):
            w_rate = lax.dynamic_update_slice_in_dim(
                w_rate,
                swap(rate_shard, "seq", b) if b else rate_shard,
                (place[0] ^ b) * rate_shard.shape[1],
                1,
            )
    else:
        w_rate = lax.all_gather(rate_shard, "seq", axis=1, tiled=True)

    count = 2 * hops
    stages = 4
    cot_found = {0: [cotangent]}
    cot_state = [cotangent, cotangent]

    def cot_hop(hop, *gates):
        forward, backward, *_ = together(*cot_state, *gates)
        if hop < hops:
            forward, backward = ring_step(forward, "head", 1), ring_step(backward, "head", -1)
            cot_found[count - hop], cot_found[hop] = [forward], [backward]
        else:
            half = own_rows // 2
            forward = ring_step(forward[:half], "head", 1)
            backward = ring_step(backward[half:], "head", -1)
            cot_found[hop] = [forward, backward]
        cot_state[:] = [forward, backward]
        return list(cot_state)

    def fetch_mix(pin):
        keep["mix"] = pair_gather(w_qkvg, pin(mix_far), "seq")
        return keep["mix"]

    fillers = {last_window: fetch_mix}
    normed_found = ring_gather((norm_normed * norm_gain).astype(BF16), "head", fillers, False)
    w_mix = keep["mix"]
    out_rows = lax.all_gather(after(w_out, mix_far), "seq", axis=1, tiled=True)

    stage_hops = {
        stage: range(1 + hops * stage // stages, 1 + hops * (stage + 1) // stages) for stage in range(stages)
    }

    def cot_stage(stage, gate):
        made = []
        for hop in stage_hops[stage]:
            made = cot_hop(hop, gate)
        return made

    cot_stage(0, normed_found[hops][0])
    projected, rates = project(ids, spots, normed_found, w_mix, w_rate)
    seq_rows = projected.shape[0]
    halo_rows = shifted(projected[seq_rows - HALO :], "seq", 1)
    projected, *_ = together(projected, *cot_state)
    cot_stage(1, projected)
    out_local, query_map, *saved, end_state = mixer_forward(
        projected, halo_rows, rates, bias_row, conv_weight, GROUP
    )
    end_state, *_ = together(end_state, *cot_state)
    cot_stage(2, end_state)
    maps = lax.all_gather(end_state, "seq")
    maps, *_ = together(maps, *cot_state)
    cot_stage(3, maps)
    value, gated, branch_part, incoming = gate_output(
        ids, place, maps, out_local, query_map, projected, gain_row, out_rows
    )
    branch_part, *_ = together(branch_part, *cot_state)
    fetch = lambda w, *pins: lax.all_gather(after(w, *pins), "seq", axis=1, tiled=True)
    down_w = fetch(w_ff_down, maps)
    gate_w = fetch(w_ff_gate, maps)
    up_w = fetch(w_ff_up, maps)

    def stack_normed(pin):
        keep["normed"] = stacked({k: [pin(p) for p in ps] for k, ps in normed_found.items()}, seq_rows)
        return (keep["normed"],)

    def stack_cotangent(pin):
        keep["cot"] = stacked({k: [pin(p) for p in ps] for k, ps in cot_found.items()}, seq_rows)
        return (keep["cot"],)

    def turn_down(pin):
        keep["down_t"] = turned([pin(down_w)])
        return keep["down_t"]

    def turn_others(pin):
        keep["others_t"] = turned([pin(gate_w), pin(up_w)])
        return keep["others_t"]

    residual = inputs + ring_scatter(
        near_rows(branch_part, own_rows), own_rows, "head", {1: stack_cotangent, 2: stack_normed}
    )
    inverse_two = lax.rsqrt(jnp.mean(residual * residual, axis=-1, keepdims=True) + epsilon)
    mlp_normed = residual * inverse_two

    def hidden_gradient(pin):
        keep["gh"] = times(pin(keep["cot"]), keep["down_t"][0])
        return (keep["gh"],)

    mlp_near = ring_gather((mlp_normed * mlp_gain).astype(BF16), "head", {1: turn_down, 2: hidden_gradient, 3: turn_others})
    normed, cotangent_near, grad_hidden = keep["normed"], keep["cot"], keep["gh"]

    gate_pre, up_pre = (dot(mlp_near, w, plain) for w in keep["others_t"])
    ff_sigmoid = jax.nn.sigmoid(gate_pre)
    ff_silu = gate_pre * ff_sigmoid
    hidden = (ff_silu * up_pre).astype(BF16)
    ff_slope = ff_sigmoid * (1.0 + gate_pre * (1.0 - ff_sigmoid))
    grad_gate_pre = (grad_hidden * up_pre * ff_slope).astype(BF16)
    grad_up_pre = (grad_hidden * ff_silu).astype(BF16)
    grad_mlp_part = (dot(grad_gate_pre, gate_w, plain) + dot(grad_up_pre, up_w, plain)).astype(BF16)

    scatter = lambda a: lax.psum_scatter(a, "seq", scatter_dimension=1, tiled=True)

    def weight_product(name, left, right, before=None):
        def filler(pin):
            made = [outer(pin(left), right)] if left is not None else []
            if before is not None:
                keep[before, "sum"] = scatter(pin(keep[before]))
            if made:
                keep[name] = made[0]
            return made

        return filler

    def output_rows(pin):
        keep["up", "sum"] = scatter(pin(keep["up"]))
        keep["output"] = dot(pin(hidden), down_w, plain).astype(BF16)
        return (keep["output"],)

    grad_mlp_in = ring_scatter(
        near_rows(grad_mlp_part, own_rows),
        own_rows,
        "head",
        {
            1: weight_product("down", hidden, cotangent_near),
            2: weight_product("gate", grad_gate_pre, mlp_near, "down"),
            3: weight_product("up", grad_up_pre, mlp_near, "gate"),
            4: output_rows,
        },
    )

    output_part = keep["output"]
    mlp_gain_part = jnp.sum(grad_mlp_in * mlp_normed, axis=0)
    scaled_two = grad_mlp_in * mlp_gain
    grad_residual = cotangent.astype(F32) + inverse_two * (
        scaled_two - mlp_normed * jnp.mean(scaled_two * mlp_normed, axis=-1, keepdims=True)
    )

    grad_down_s, grad_gate_s, grad_up_s = (keep[name, "sum"] for name in ("down", "gate", "up"))
    branch_near = ring_gather(
        grad_residual.astype(BF16), "head", {2: lambda pin: [grad_down_s], 4: lambda pin: [grad_gate_s]}
    )
    take_output = near_rows(output_part, own_rows)
    output_state = [None, None]
    known = lambda: [a for a in output_state if a is not None]

    def output_hops(stage, *gates):
        for hop in range(hops * (stage - 1) // stages, hops * stage // stages):
            here = []
            for way, k in enumerate((hops - hop, count - hops + hop)):
                if hop == 0 and way == 1:
                    here.append(None)
                    continue
                piece = take_output(k, 0, own_rows)
                total = piece if output_state[way] is None else output_state[way] + piece
                here.append(ring_step(after(total, *gates), "head", 1 - 2 * way))
            output_state[:] = here

    output_hops(1, branch_near)
    grad_gate_mix, grad_mixer, head_gain_part, local_grad = gate_backward(
        ids, branch_near, out_rows, value, projected, query_map, gain_row, heads
    )
    local_low, *_ = together(local_grad, *known())
    shares = seq_shards(local_low, "seq")
    gate_grad_w = outer(keep["normed"], together(grad_gate_mix, *shares[1:])[0])
    output_hops(2, shares[1])
    first_share, gate_grad_w, *_ = together(shares[0], gate_grad_w, *known())
    gate_grad_s = lax.psum_scatter(gate_grad_w, "seq", scatter_dimension=0, tiled=True)
    output_hops(3, gate_grad_w)
    grad_mixed, grad_rates, seq_sums, tail_rows, lead_rows = mixer_backward(
        projected, halo_rows, rates, bias_row, conv_weight, saved,
        grad_mixer, value, incoming, place, near_spots, maps, [first_share, *shares[1:]], GROUP,
    )
    grad_mixed, gate_grad_s, grad_up_s, *_ = together(grad_mixed, gate_grad_s, grad_up_s, *known())
    later_rows = shifted(lead_rows, "seq", -1)
    out_grad_w = outer(gated, after(branch_near, lead_rows))
    output_hops(4, grad_mixed)
    padded = jnp.concatenate([jnp.zeros((HALO, heads * MIX), F32), later_rows])
    last_rows = tail_rows + sum(
        conv_weight[i] * padded[CONV - 1 - i : CONV - 1 - i + HALO] for i in range(CONV)
    )
    last_start = near_spots[count - 1] * own_rows + own_rows - HALO
    grad_mixed = lax.dynamic_update_slice(grad_mixed, last_rows.astype(BF16), (last_start, 0))
    grad_mixed, out_grad_w = together(grad_mixed, out_grad_w)
    mix_grad_w = outer(keep["normed"], grad_mixed)
    mix_grad_w, out_grad_w = together(mix_grad_w, out_grad_w)
    grad_out_s = scatter(out_grad_w)
    grad_mixed, mix_grad_w = together(grad_mixed, mix_grad_w)
    mix_grad_s = lax.psum_scatter(mix_grad_w, "seq", scatter_dimension=0, tiled=True)
    early = [hops] + ([hops - 1, hops + 1] if hops > 1 else [])
    late = [k for s in range(hops - 2, 0, -1) for k in (s, count - s)] + [0]
    place_of = {k: (0, i) for i, k in enumerate(early)} | {k: (1, i) for i, k in enumerate(late)}
    parts = []
    part, sums = normed_back(
        spots, early, count, grad_mixed, grad_gate_mix, grad_rates, normed, w_mix, w_rate, jnp.zeros((8, width), F32)
    )
    part, *_ = together(part, *known())
    parts.append(part)

    def take(k, start, size):
        which, i = place_of[k]
        return lax.slice_in_dim(parts[which], i * own_rows + start, i * own_rows + start + size, axis=0)

    def late_rows(pin):
        part, keep["sums"] = normed_back(
            spots, late, count, pin(grad_mixed), grad_gate_mix, grad_rates, normed, w_mix, w_rate, sums
        )
        parts.append(part)
        return (part,)

    def first_window(pin):
        return late_rows(pin)

    def second_window(pin):
        sums = pin(keep["sums"])
        gains = jnp.concatenate([mlp_gain_part[None], head_gain_part, jnp.zeros((1, width - DV), F32)], axis=1)
        gains = jnp.pad(gains, ((4, 3), (0, 0)))
        small = jnp.concatenate([sums, gains, seq_sums], axis=1)
        keep["small"] = butterfly(small, "seq")
        keep["gains"] = keep["small"][4:5, : 3 * width]
        return (keep["gains"],)

    def third_window(pin):
        gains = pin(keep["gains"])
        keep["gains"] = gains + swap(gains, "head", 1)
        return (keep["gains"], mix_grad_s)

    grad_normed = ring_scatter(
        take, own_rows, "head", {1: first_window, 2: second_window, 3: third_window}
    )
    scaled_one = grad_normed * norm_gain
    grad_input = grad_residual + inverse_one * (
        scaled_one - norm_normed * jnp.mean(scaled_one * norm_normed, axis=-1, keepdims=True)
    )
    output = (
        residual + sum(a.astype(F32) for a in known()) + take_output(0, 0, own_rows).astype(F32)
    ).astype(BF16)
    small, gains = keep["small"], after(keep["gains"], grad_normed)
    bit = 2
    while bit < count:
        gains = gains + swap(gains, "head", bit)
        bit *= 2
    joined, *wide = finish_all(mix_grad_s, gate_grad_s, [grad_out_s, grad_gate_s, grad_up_s, grad_down_s])
    per_seq = w_rates.shape[0]
    return (
        output,
        grad_input,
        joined,
        lax.dynamic_slice_in_dim(small[: 2 * heads], place[0] * per_seq, per_seq, 1).T,
        small[:CONV, 3 * width :],
        small[CONV, 3 * width : 3 * width + 2 * heads].reshape(heads, 2).T,
        gains[0, :width] / norm_gain,
        gains[0, 2 * width : 2 * width + DV],
        gains[0, width : 2 * width],
        *wide,
    )


def solution(mesh):
    in_specs = (
        P(("seq", "head"), None),
        P("seq", "head"),
        P("seq", "head"),
        P(None, "head"),
        P(None, "head"),
        P(),
        P(),
        P(),
        P("head", "seq"),
        P("head", "seq"),
        P("head", "seq"),
        P("head", "seq"),
        P(("seq", "head"), None),
    )
    out_specs = (
        P(("seq", "head"), None),
        P(("seq", "head"), None),
        P("seq", "head"),
        P("seq", "head"),
        P(None, "head"),
        P(None, "head"),
        P(),
        P(),
        P(),
        P("head", "seq"),
        P("head", "seq"),
        P("head", "seq"),
        P("head", "seq"),
    )
    return jax.shard_map(
        per_device, mesh=mesh, in_specs=in_specs, out_specs=out_specs, check_vma=False
    )
```

```python
import functools
import jax
import jax.numpy as jnp
from jax import lax
from jax.experimental import pallas as pl
from jax.experimental.pallas import tpu as pltpu
from jax.sharding import PartitionSpec as P

DK = 128
DV = 256
CONV = 4
CHUNK = 128
MIX = 2 * DK + DV
PER = 2 * DK + 2 * DV
GROUP = 4
epsilon = 1e-06
F32 = jnp.float32
BF16 = jnp.bfloat16
HALO = 16
VMEM_LIMIT = 56 * 1024 * 1024
LIGHT = pl.CostEstimate(flops=1, bytes_accessed=1, transcendentals=0)


def shifted(value, axis, steps):
    count = lax.axis_size(axis)
    leading, last = (max(0, -steps), min(count, count - steps))
    return lax.ppermute(value, axis, [(source, source + steps) for source in range(leading, last)])


def mm(a, b, ca=1, cb=0):
    return lax.dot_general(
        a.astype(BF16), b.astype(BF16), (((ca,), (cb,)), ((), ())), preferred_element_type=F32
    )


def mmx(a, b, ca=1, cb=0):
    return lax.dot_general(
        a, b, (((ca,), (cb,)), ((), ())), preferred_element_type=F32, precision=lax.Precision.HIGHEST
    )


def block_columns(spots_ref, b, width):
    return pl.ds(pl.multiple_of(spots_ref[b] * width, 128), width)


def chosen(refs, place_ref, source, h, rows):
    value = refs[0][h, rows, :]
    for b in range(1, len(refs)):
        here = (place_ref[0] ^ b) == source if len(refs) == 4 else b == source
        value = jnp.where(here, refs[b][h, rows, :], value)
    return value


def softplus(x):
    return jnp.maximum(x, 0.0) + jnp.log1p(jnp.exp(-jnp.abs(x)))


def sigmoid(x):
    return 1.0 / (1.0 + jnp.exp(-x))


def iotas(n):
    return (
        lax.broadcasted_iota(jnp.int32, (n, n), 0),
        lax.broadcasted_iota(jnp.int32, (n, n), 1),
    )


def inverse_parts(mats, rows, cols):
    base = 16
    near = (rows // base) == (cols // base)
    diag = [jnp.where(near, a, 0.0) for a in mats]
    result = [-d for d in diag]
    power = [mm(d, d) for d in diag]
    span = 2
    while True:
        result = [r + p + mm(r, p) for r, p in zip(result, power)]
        span *= 2
        if span >= base:
            break
        power = [mm(p, p) for p in power]
    size = base
    n = mats[0].shape[0]
    while size < n:
        cross = ((rows // (2 * size)) == (cols // (2 * size))) & ((rows // size) != (cols // size))
        off = [jnp.where(cross, a, 0.0) for a in mats]
        left = [o + mm(r, o) for o, r in zip(off, result)]
        result = [r - x - mm(x, r) for r, x in zip(result, left)]
        size *= 2
    return result


def conv_scratch(first, proj_ref, prev_ref, halo_ref, x_ref, heads, rows):
    for h in range(heads):
        cols = slice(h * PER, h * PER + MIX)
        before = jnp.where(first, halo_ref[:, cols].astype(F32), prev_ref[:, cols].astype(F32))
        x_ref[0:8, h * MIX : (h + 1) * MIX] = before[HALO - 8 :]
        x_ref[8 : 8 + rows, h * MIX : (h + 1) * MIX] = proj_ref[:, cols].astype(F32)


def conv_pre(x_ref, taps_ref, h, row):
    cols = slice(h * MIX, (h + 1) * MIX)
    total = None
    for i in range(CONV):
        part = taps_ref[i : i + 1, cols] * x_ref[pl.ds(row + 8 - (CONV - 1) + i, CHUNK), cols]
        total = part if total is None else total + part
    return total


def unit(a):
    r = lax.rsqrt(jnp.sum(a * a, axis=-1, keepdims=True) + epsilon)
    return a * r, r


def forward_kernel(
    heads, group,
    proj_ref, prev_ref, halo_ref, rates_ref, bias_ref, taps_ref,
    olocal_ref, qmap_ref, state_ref, uw_ref, inv_ref, trans_ref, qe_ref, end_ref,
    x_ref, carry_ref,
):
    step = pl.program_id(0)
    rows_here = CHUNK * group
    conv_scratch(step == 0, proj_ref, prev_ref, halo_ref, x_ref, heads, rows_here)
    ri, ci = iotas(CHUNK)
    included = ri >= ci
    strictly = ri > ci
    lower = jnp.where(included, 1.0, 0.0)
    upper = jnp.where(ri <= ci, 1.0, 0.0)

    @pl.when(step == 0)
    def _():
        for h in range(heads):
            carry_ref[h, :DV, :] = jnp.zeros((DV, DK), F32)
            carry_ref[h, DV:, :] = jnp.where(ri == ci, 1.0, 0.0)

    pairs = [(g, h) for g in range(group) for h in range(heads)]
    logits = rates_ref[...] + bias_ref[...]
    log_decay = -softplus(logits)
    strength = sigmoid(logits)
    cums, cum_rows = [], []
    for g in range(group):
        part = log_decay[g * CHUNK : (g + 1) * CHUNK]
        cums.append(mmx(lower, part))
        cum_rows.append(mmx(part, upper, 0, 0))
    mats, scores, rhs, tails, scaled_q, finals = [], [], [], [], [], []
    for g, h in pairs:
        pre = conv_pre(x_ref, taps_ref, h, g * CHUNK)
        mixed = pre * sigmoid(pre)
        q = unit(mixed[:, :DK])[0] * DK ** (-0.5)
        k = unit(mixed[:, DK : 2 * DK])[0]
        v = mixed[:, 2 * DK :]
        cum = cums[g][:, 2 * h : 2 * h + 1]
        cum_row = cum_rows[g][2 * h : 2 * h + 1, :]
        beta = strength[g * CHUNK : (g + 1) * CHUNK, 2 * h + 1 : 2 * h + 2]
        growth = jnp.exp(cum)
        decays = jnp.where(included, jnp.exp(jnp.where(included, cum - cum_row, 0.0)), 0.0)
        grams = mm(jnp.concatenate([q, k], axis=0), k, 1, 1)
        scores.append(grams[:CHUNK] * decays)
        mats.append(jnp.where(strictly, beta * decays * grams[CHUNK:], 0.0))
        rhs.append(jnp.concatenate([beta * v, beta * growth * k], axis=1))
        last = cum[CHUNK - 1 : CHUNK, :]
        tails.append(k * jnp.exp(last - cum))
        scaled_q.append(growth * q)
        finals.append(jnp.exp(last))
    inverses = inverse_parts(mats, ri, ci)
    solved = [b + mm(r, b) for r, b in zip(inverses, rhs)]
    mixes = [mm(p, u) for p, u in zip(scores, solved)]
    adds = [mm(u, t, 0, 0) for u, t in zip(solved, tails)]
    for j, (g, h) in enumerate(pairs):
        inv_ref[h, g] = inverses[j].astype(BF16)
        uw_ref[h, g] = solved[j].astype(BF16)
        qe_ref[h, g] = (scaled_q[j] - mixes[j][:, DV:]).astype(BF16)
        trans_ref[h, g] = (-adds[j][DV:]).astype(BF16)
        olocal_ref[g * CHUNK : (g + 1) * CHUNK, h * DV : (h + 1) * DV] = mixes[j][:, :DV]
    for h in range(heads):
        now = carry_ref[h]
        for g in range(group):
            j = pairs.index((g, h))
            low = now.astype(BF16)
            state_ref[h, g] = low
            moved = finals[j] * now + mm(low, trans_ref[h, g])
            now = jnp.concatenate([moved[:DV] + adds[j][:DV], moved[DV:]], axis=0)
        carry_ref[h] = now
        end_ref[h] = now.astype(BF16)
    for j, (g, h) in enumerate(pairs):
        both = mm(qe_ref[h, g], state_ref[h, g], 1, 1)
        rows = slice(g * CHUNK, (g + 1) * CHUNK)
        olocal_ref[rows, h * DV : (h + 1) * DV] += both[:, :DV]
        qmap_ref[rows, h * DK : (h + 1) * DK] = both[:, DV:].astype(BF16)


def mixer_forward(projected, halo, rates, bias_row, taps, group):
    total = projected.shape[0]
    heads = rates.shape[1] // 2
    rows = CHUNK * group
    steps = total // rows
    chunks = total // CHUNK
    whole = lambda i: (0, 0)
    saved = lambda a, b: (
        jax.ShapeDtypeStruct((heads, chunks, a, b), BF16),
        pl.BlockSpec((heads, group, a, b), lambda i: (0, i, 0, 0)),
    )
    outs = [
        (jax.ShapeDtypeStruct((total, heads * DV), F32), pl.BlockSpec((rows, heads * DV), lambda i: (i, 0))),
        (jax.ShapeDtypeStruct((total, heads * DK), BF16), pl.BlockSpec((rows, heads * DK), lambda i: (i, 0))),
        saved(DV + DK, DK),
        saved(CHUNK, DV + DK),
        saved(CHUNK, CHUNK),
        saved(DK, DK),
        saved(CHUNK, DK),
        (jax.ShapeDtypeStruct((heads, DV + DK, DK), BF16), pl.BlockSpec((heads, DV + DK, DK), lambda i: (0, 0, 0))),
    ]
    return pl.pallas_call(
        functools.partial(forward_kernel, heads, group),
        grid=(steps,),
        in_specs=[
            pl.BlockSpec((rows, heads * PER), lambda i: (i, 0)),
            pl.BlockSpec((HALO, heads * PER), lambda i: (jnp.maximum(i * (rows // HALO) - 1, 0), 0)),
            pl.BlockSpec((HALO, heads * PER), whole),
            pl.BlockSpec((rows, 2 * heads), lambda i: (i, 0)),
            pl.BlockSpec((1, 2 * heads), whole),
            pl.BlockSpec((CONV, heads * MIX), whole),
        ],
        out_shape=[o[0] for o in outs],
        out_specs=[o[1] for o in outs],
        scratch_shapes=[
            pltpu.VMEM((rows + 8, heads * MIX), F32),
            pltpu.VMEM((heads, DV + DK, DK), F32),
        ],
        compiler_params=pltpu.CompilerParams(vmem_limit_bytes=VMEM_LIMIT),
        cost_estimate=LIGHT,
    )(projected, projected, halo, rates, bias_row, taps)


def backward_kernel(
    heads, group, steps, peers, own,
    proj_ref, prev_ref, halo_ref, rates_ref, bias_ref, taps_ref,
    state_ref, uw_ref, inv_ref, trans_ref, qe_ref,
    dout_ref, value_ref, incoming_ref, place_ref, spots_ref, *refs,
):
    maps_refs, refs = refs[:peers], refs[peers:]
    *local_refs, gp_ref, grates_ref, sums_ref, tail_ref, lead_ref, x_ref, d_ref, carry_ref, next_ref = refs
    step = pl.program_id(0)
    rows_here = CHUNK * group
    conv_scratch(step == steps - 1, proj_ref, prev_ref, halo_ref, x_ref, heads, rows_here)
    ri, ci = iotas(CHUNK)
    included = ri >= ci
    strictly = ri > ci
    lower = jnp.where(included, 1.0, 0.0)
    upper = jnp.where(ri <= ci, 1.0, 0.0)

    @pl.when(step == 0)
    def _():
        for h in range(heads):
            grad = jnp.zeros((DV, DK), F32)
            for turn in range(peers - 1):
                source = peers - 1 - turn
                share = jnp.zeros((DV, DK), F32)
                for b, local_ref in enumerate(local_refs):
                    here = (place_ref[0] ^ b) == source if peers == 4 else b == source
                    share = jnp.where(here, local_ref[h].astype(F32), share)
                moved = mm(grad, chosen(maps_refs, place_ref, source, h, slice(DV, DV + DK)), 1, 1) + share
                grad = jnp.where(source > place_ref[0], moved, grad)
            carry_ref[h] = grad
        d_ref[rows_here : rows_here + 8, :] = jnp.zeros((8, heads * MIX), F32)
        sums_ref[...] = jnp.zeros_like(sums_ref)

    @pl.when(step > 0)
    def _():
        d_ref[rows_here : rows_here + 8, :] = d_ref[0:8, :]

    def near_row(g):
        first = ((steps - 1 - step) * group + g) * CHUNK
        return pl.multiple_of(spots_ref[first // own] * own + first % own, CHUNK)

    pairs = [(g, h) for g in range(group) for h in range(heads)]
    logits = rates_ref[...] + bias_ref[...]
    log_decay = -softplus(logits)
    strength = sigmoid(logits)
    cums, cum_rows = [], []
    for g in range(group):
        part = log_decay[g * CHUNK : (g + 1) * CHUNK]
        cums.append(mmx(lower, part))
        cum_rows.append(mmx(part, upper, 0, 0))
    douts, injections = [], []
    for g, h in pairs:
        do = dout_ref[g * CHUNK : (g + 1) * CHUNK, h * DV : (h + 1) * DV]
        douts.append(do)
        injections.append(mm(do, qe_ref[h, g], 0, 0))
    for h in range(heads):
        now = carry_ref[h]
        for g in reversed(range(group)):
            j = pairs.index((g, h))
            last = cums[g][CHUNK - 1 : CHUNK, 2 * h : 2 * h + 1]
            next_ref[h, g] = now
            now = jnp.exp(last) * now + mm(now, trans_ref[h, g], 1, 1) + injections[j]
        carry_ref[h] = now
    lane = lax.broadcasted_iota(jnp.int32, (CHUNK, 2 * heads), 1)
    row_col = lax.broadcasted_iota(jnp.int32, (CHUNK, 1), 0)
    dcums = [jnp.zeros((CHUNK, 2 * heads), F32) for _ in range(group)]
    dlogits = [jnp.zeros((CHUNK, 2 * heads), F32) for _ in range(group)]
    for j, (g, h) in enumerate(pairs):
        pre = conv_pre(x_ref, taps_ref, h, g * CHUNK)
        sig = sigmoid(pre)
        mixed = pre * sig
        slope = sig * (1.0 + pre * (1.0 - sig))
        uq, rq = unit(mixed[:, :DK])
        q = uq * DK ** (-0.5)
        k, rk = unit(mixed[:, DK : 2 * DK])
        v = mixed[:, 2 * DK :]
        cum = cums[g][:, 2 * h : 2 * h + 1]
        cum_row = cum_rows[g][2 * h : 2 * h + 1, :]
        beta = strength[g * CHUNK : (g + 1) * CHUNK, 2 * h + 1 : 2 * h + 2]
        growth = jnp.exp(cum)
        decays = jnp.where(included, jnp.exp(jnp.where(included, cum - cum_row, 0.0)), 0.0)
        qb, kb = q.astype(BF16), k.astype(BF16)
        grams = mm(jnp.concatenate([qb, kb], axis=0), kb, 1, 1)
        scores = grams[:CHUNK] * decays
        last = cum[CHUNK - 1 : CHUNK, :]
        fade = jnp.exp(last - cum)
        tail = k * fade
        sl = state_ref[h, g]
        state = sl[:DV].astype(F32) + mm(incoming_ref[h], sl[DV:])
        after = next_ref[h, g]
        afterb = after.astype(BF16)
        stateb = state.astype(BF16)
        uw = uw_ref[h, g]
        errors = uw[:, :DV].astype(F32) - mm(uw[:, DV:], stateb, 1, 1)
        eb = errors.astype(BF16)
        do = douts[j]
        de = mm(scores, do, 0, 0) + mm(tail, afterb, 1, 1)
        db = de + mm(inv_ref[h, g], de, 0, 0)
        dbb = db.astype(BF16)
        stacked = jnp.concatenate([do, dbb], axis=0)
        against_e = mm(stacked, eb, 1, 1)
        against_s = mm(stacked, stateb)
        dp = against_e[:CHUNK]
        da = jnp.where(strictly, -against_e[CHUNK:], 0.0)
        dos = against_s[:CHUNK]
        dbs = against_s[CHUNK:]
        dpd = dp * decays
        dg = da * beta * decays
        dtail = mm(eb, afterb)
        dq = mm(dpd, kb) + growth * dos
        sym = dg + dg.T
        dk = (
            mm(jnp.concatenate([dpd.T, sym], axis=1), jnp.concatenate([qb, kb], axis=0))
            - beta * growth * dbs
            + fade * dtail
        )
        dv = beta * db
        dlogit = (1.0 - beta) * jnp.sum(db * errors, axis=1, keepdims=True)
        tdot = jnp.sum(tail * dtail, axis=1, keepdims=True)
        out = value_ref[g * CHUNK : (g + 1) * CHUNK, h * DV : (h + 1) * DV].astype(F32)
        dcum = jnp.sum(do.astype(F32) * out, axis=1, keepdims=True) - beta * jnp.sum(
            v * db, axis=1, keepdims=True
        )
        at_end = jnp.exp(last) * jnp.sum(jnp.sum(after * state, axis=1, keepdims=True), axis=0, keepdims=True) + jnp.sum(
            tdot, axis=0, keepdims=True
        )
        dcum = dcum + jnp.where(row_col == CHUNK - 1, at_end, 0.0)
        dcums[g] = jnp.where(lane == 2 * h, dcum, dcums[g])
        dlogits[g] = jnp.where(lane == 2 * h + 1, dlogit, dlogits[g])
        dq = dq * DK ** (-0.5)
        dmq = rq * (dq - uq * jnp.sum(uq * dq, axis=1, keepdims=True))
        dmk = rk * (dk - k * jnp.sum(k * dk, axis=1, keepdims=True))
        d_ref[g * CHUNK : (g + 1) * CHUNK, h * MIX : (h + 1) * MIX] = (
            jnp.concatenate([dmq, dmk, dv], axis=1) * slope
        )
    for g in range(group):
        rows = slice(g * CHUNK, (g + 1) * CHUNK)
        dld = mmx(upper, dcums[g])
        drate = jnp.where(lane % 2 == 0, -sigmoid(logits[rows]) * dld, dlogits[g])
        grates_ref[pl.ds(near_row(g), CHUNK), :] = drate
        sums_ref[CONV : CONV + 1, : 2 * heads] += jnp.sum(drate, axis=0, keepdims=True)
    for g, h in pairs:
        cols = slice(h * MIX, (h + 1) * MIX)
        row = g * CHUNK
        dpre = d_ref[pl.ds(row, CHUNK), cols]
        total = None
        for i in range(CONV):
            sums_ref[i : i + 1, cols] += jnp.sum(
                dpre * x_ref[pl.ds(row + 8 - (CONV - 1) + i, CHUNK), cols], axis=0, keepdims=True
            )
            part = taps_ref[i : i + 1, cols] * d_ref[pl.ds(row + CONV - 1 - i, CHUNK), cols]
            total = part if total is None else total + part
        gp_ref[pl.ds(near_row(g), CHUNK), cols] = total.astype(BF16)
        if g == group - 1:
            @pl.when(step == 0)
            def _(total=total, cols=cols):
                tail_ref[:, cols] = total[CHUNK - HALO :]

    @pl.when(step == steps - 1)
    def _():
        lead_ref[...] = d_ref[0:8, :]


def mixer_backward(projected, halo, rates, bias_row, taps, saved, dout, value, incoming, place, spots, maps, local, group):
    state, uw, inv, trans, qe = saved
    total = projected.shape[0]
    heads = rates.shape[1] // 2
    rows = CHUNK * group
    steps = total // rows
    whole = lambda i: (0, 0)
    flip = lambda i: (steps - 1 - i, 0)
    keep = lambda a, b: pl.BlockSpec((heads, group, a, b), lambda i: (0, steps - 1 - i, 0, 0))
    return pl.pallas_call(
        functools.partial(backward_kernel, heads, group, steps, len(maps), total // spots.shape[0]),
        grid=(steps,),
        in_specs=[
            pl.BlockSpec((rows, heads * PER), flip),
            pl.BlockSpec((HALO, heads * PER), lambda i: (jnp.maximum((steps - 1 - i) * (rows // HALO) - 1, 0), 0)),
            pl.BlockSpec((HALO, heads * PER), whole),
            pl.BlockSpec((rows, 2 * heads), flip),
            pl.BlockSpec((1, 2 * heads), whole),
            pl.BlockSpec((CONV, heads * MIX), whole),
            keep(DV + DK, DK),
            keep(CHUNK, DV + DK),
            keep(CHUNK, CHUNK),
            keep(DK, DK),
            keep(CHUNK, DK),
            pl.BlockSpec((rows, heads * DV), flip),
            pl.BlockSpec((rows, heads * DV), flip),
            pl.BlockSpec(incoming.shape, lambda i: (0, 0, 0)),
            pl.BlockSpec(memory_space=pltpu.SMEM),
            pl.BlockSpec(memory_space=pltpu.SMEM),
            *[pl.BlockSpec(part.shape, lambda i: (0, 0, 0)) for part in maps],
            *[pl.BlockSpec(part.shape, lambda i: (0, 0, 0)) for part in local],
        ],
        out_shape=[
            jax.ShapeDtypeStruct((total, heads * MIX), BF16),
            jax.ShapeDtypeStruct((total, 2 * heads), F32),
            jax.ShapeDtypeStruct((8, heads * MIX), F32),
            jax.ShapeDtypeStruct((HALO, heads * MIX), F32),
            jax.ShapeDtypeStruct((8, heads * MIX), F32),
        ],
        out_specs=[
            pl.BlockSpec((total, heads * MIX), whole),
            pl.BlockSpec((total, 2 * heads), whole),
            pl.BlockSpec((8, heads * MIX), whole),
            pl.BlockSpec((HALO, heads * MIX), whole),
            pl.BlockSpec((8, heads * MIX), whole),
        ],
        scratch_shapes=[
            pltpu.VMEM((rows + 8, heads * MIX), F32),
            pltpu.VMEM((rows + 8, heads * MIX), F32),
            pltpu.VMEM((heads, DV, DK), F32),
            pltpu.VMEM((heads, group, DV, DK), F32),
        ],
        compiler_params=pltpu.CompilerParams(vmem_limit_bytes=VMEM_LIMIT),
        cost_estimate=LIGHT,
    )(projected, projected, halo, rates, bias_row, taps, state, uw, inv, trans, qe, dout, value, incoming, place, spots, *maps, *local)


def pair_rows(ids_ref, step, which, rows):
    return pl.ds(pl.multiple_of(ids_ref[2 * step + which] * rows, rows), rows)


def gate_kernel(heads, peers, ids_ref, place_ref, gain_ref, w_ref, *refs):
    maps_refs, refs = refs[:peers], refs[peers:]
    olocal_refs, qmap_refs = refs[0:2], refs[2:4]
    gate_refs = refs[4 : 4 + 2 * heads]
    value_ref, gated_ref, part_ref, incoming_ref = refs[4 + 2 * heads :]
    step = pl.program_id(0)

    @pl.when(step == 0)
    def _():
        for h in range(heads):
            state = jnp.zeros((DV, DK), F32)
            for source in range(peers - 1):
                entry = chosen(maps_refs, place_ref, source, h, slice(None))
                moved = mm(state, entry[DV:]) + entry[:DV].astype(F32)
                state = jnp.where(source < place_ref[0], moved, state)
            incoming_ref[h] = state.astype(BF16)

    rows = olocal_refs[0].shape[0]
    for h in range(heads):
        cols = slice(h * DV, (h + 1) * DV)
        query_map = jnp.concatenate([ref[:, h * DK : (h + 1) * DK] for ref in qmap_refs], axis=0)
        out_local = jnp.concatenate([ref[:, cols] for ref in olocal_refs], axis=0)
        low = (out_local + mm(query_map, incoming_ref[h], 1, 1)).astype(BF16)
        for which in range(2):
            value_ref[pair_rows(ids_ref, step, which, rows), cols] = low[which * rows : (which + 1) * rows]
        value = low.astype(F32)
        normed = value * lax.rsqrt(jnp.mean(value * value, axis=-1, keepdims=True) + epsilon)
        gate = jnp.concatenate([gate_refs[2 * h + which][...] for which in range(2)], axis=0).astype(F32)
        gated_ref[:, cols] = (normed * gain_ref[...] * (gate * sigmoid(gate))).astype(BF16)
    part_ref[...] = mm(gated_ref[...], w_ref[...]).astype(BF16)


def gate_blocks(heads, rows):
    full = lambda wide: [
        pl.BlockSpec((rows, wide), lambda i, *s, which=which: (s[0][2 * i + which], 0)) for which in range(2)
    ]
    gates = [
        pl.BlockSpec(
            (rows, DV), lambda i, *s, which=which, h=h: (s[0][2 * i + which], (h + 1) * (PER // DV) - 1)
        )
        for h in range(heads)
        for which in range(2)
    ]
    return full, gates


def gate_output(ids, place, maps, out_local, query_map, projected, gain, w_out):
    heads = maps[0].shape[0]
    total = projected.shape[0]
    count = ids.shape[0]
    rows = total // count
    width = w_out.shape[1]
    mine = lambda i, *s: (i, 0)
    whole = lambda i, *s: (0, 0)
    full, gates = gate_blocks(heads, rows)
    return pl.pallas_call(
        functools.partial(gate_kernel, heads, len(maps)),
        grid_spec=pltpu.PrefetchScalarGridSpec(
            num_scalar_prefetch=2,
            grid=(count // 2,),
            in_specs=[
                pl.BlockSpec((1, DV), whole),
                pl.BlockSpec(w_out.shape, whole),
                *[pl.BlockSpec(part.shape, lambda i, *s: (0, 0, 0)) for part in maps],
                *full(heads * DV),
                *full(heads * DK),
                *gates,
            ],
            out_specs=[
                pl.BlockSpec((total, heads * DV), whole),
                pl.BlockSpec((2 * rows, heads * DV), mine),
                pl.BlockSpec((2 * rows, width), mine),
                pl.BlockSpec((heads, DV, DK), lambda i, *s: (0, 0, 0)),
            ],
        ),
        out_shape=[
            jax.ShapeDtypeStruct((total, heads * DV), BF16),
            jax.ShapeDtypeStruct((total, heads * DV), BF16),
            jax.ShapeDtypeStruct((total, width), BF16),
            jax.ShapeDtypeStruct((heads, DV, DK), BF16),
        ],
        compiler_params=pltpu.CompilerParams(vmem_limit_bytes=VMEM_LIMIT),
        cost_estimate=LIGHT,
    )(
        ids, place, gain, w_out, *maps, out_local, out_local, query_map, query_map,
        *[projected] * (2 * heads),
    )


def gate_back_kernel(heads, ids_ref, branch_ref, gain_ref, w_ref, *refs):
    value_refs, qmap_refs = refs[0:2], refs[2:4]
    gate_refs = refs[4 : 4 + 2 * heads]
    ggate_ref, dout_ref, gain_grad_ref, local_ref, sum_ref = refs[4 + 2 * heads :]
    step = pl.program_id(0)

    @pl.when(step == 0)
    def _():
        gain_grad_ref[...] = jnp.zeros_like(gain_grad_ref)
        sum_ref[...] = jnp.zeros_like(sum_ref)

    rows = value_refs[0].shape[0]
    grads = mm(branch_ref[...], w_ref[...], 1, 1)
    gain = gain_ref[...]
    for h in range(heads):
        cols = slice(h * DV, (h + 1) * DV)
        value = jnp.concatenate([ref[:, cols] for ref in value_refs], axis=0).astype(F32)
        inverse = lax.rsqrt(jnp.mean(value * value, axis=-1, keepdims=True) + epsilon)
        normed = value * inverse
        gate = jnp.concatenate([gate_refs[2 * h + which][...] for which in range(2)], axis=0).astype(F32)
        sig = sigmoid(gate)
        grad = grads[:, cols]
        through = grad * (gate * sig)
        ggate_ref[:, cols] = (grad * normed * gain * (sig * (1.0 + gate * (1.0 - sig)))).astype(BF16)
        gain_grad_ref[...] += jnp.sum(through * normed, axis=0, keepdims=True)
        scaled = through * gain
        low = (inverse * (scaled - normed * jnp.mean(scaled * normed, axis=-1, keepdims=True))).astype(BF16)
        for which in range(2):
            dout_ref[pair_rows(ids_ref, step, which, rows), cols] = low[which * rows : (which + 1) * rows]
        query_map = jnp.concatenate([ref[:, h * DK : (h + 1) * DK] for ref in qmap_refs], axis=0)
        sum_ref[h] += mm(low, query_map, 0, 0)

    @pl.when(step == pl.num_programs(0) - 1)
    def _():
        local_ref[...] = sum_ref[...].astype(BF16)


def gate_backward(ids, branch, w_out, value, projected, query_map, gain, heads):
    total = projected.shape[0]
    count = ids.shape[0]
    rows = total // count
    mine = lambda i, *s: (i, 0)
    whole = lambda i, *s: (0, 0)
    full, gates = gate_blocks(heads, rows)
    return pl.pallas_call(
        functools.partial(gate_back_kernel, heads),
        grid_spec=pltpu.PrefetchScalarGridSpec(
            num_scalar_prefetch=1,
            grid=(count // 2,),
            in_specs=[
                pl.BlockSpec((2 * rows, branch.shape[1]), mine),
                pl.BlockSpec((1, DV), whole),
                pl.BlockSpec(w_out.shape, whole),
                *full(heads * DV),
                *full(heads * DK),
                *gates,
            ],
            out_specs=[
                pl.BlockSpec((2 * rows, heads * DV), mine),
                pl.BlockSpec((total, heads * DV), whole),
                pl.BlockSpec((1, DV), whole),
                pl.BlockSpec((heads, DV, DK), lambda i, *s: (0, 0, 0)),
            ],
            scratch_shapes=[pltpu.VMEM((heads, DV, DK), F32)],
        ),
        out_shape=[
            jax.ShapeDtypeStruct((total, heads * DV), BF16),
            jax.ShapeDtypeStruct((total, heads * DV), BF16),
            jax.ShapeDtypeStruct((1, DV), F32),
            jax.ShapeDtypeStruct((heads, DV, DK), BF16),
        ],
        compiler_params=pltpu.CompilerParams(vmem_limit_bytes=VMEM_LIMIT),
        cost_estimate=LIGHT,
    )(
        ids, branch, gain, w_out, value, value, query_map, query_map, *[projected] * (2 * heads)
    )


def project_kernel(layout, pieces, ids_ref, spots_ref, rate_ref, *refs):
    x_refs = refs[: len(layout)]
    w_refs = refs[len(layout) : len(layout) + pieces]
    out_ref, rates_ref = refs[len(layout) + pieces :]
    rows = out_ref.shape[0] // ids_ref.shape[0]
    blocks = {}
    for (k, _), ref in zip(layout, x_refs):
        blocks.setdefault(k, []).append(ref)
    ks = list(blocks)
    for first in range(0, len(ks), 2):
        group = ks[first : first + 2]
        group_refs = [ref for k in group for ref in blocks[k]]
        x = jnp.concatenate([ref[...] for ref in group_refs], axis=0)
        total = None
        for b, w_ref in enumerate(w_refs):
            cols = block_columns(spots_ref, b, w_ref.shape[0])
            share = mm(jnp.concatenate([ref[:, cols] for ref in group_refs], axis=0), w_ref[...])
            total = share if total is None else total + share
        total = total.astype(BF16)
        rates = mm(x, rate_ref[...], 1, 1)
        for i, k in enumerate(group):
            place = pl.ds(pl.multiple_of(ids_ref[k] * rows, rows), rows)
            out_ref[place, :] = total[i * rows : (i + 1) * rows]
            rates_ref[place, :] = rates[i * rows : (i + 1) * rows]


def layout_of(found, total):
    rows = found[0][0].shape[0]
    count = total // rows
    ks = [0] + [k for s in range(1, count // 2) for k in (s, count - s)] + [count // 2]
    layout, arrays = [], []
    for k in ks:
        start = k * rows
        for piece in found.get(k, ()):
            layout.append((k, start))
            arrays.append(piece)
            start += piece.shape[0]
    return layout, arrays


def project(ids, spots, found, w_mix, w_rate):
    total = ids.shape[0] * found[0][0].shape[0]
    layout, arrays = layout_of(found, total)
    cols = w_mix[0].shape[1]
    rates = w_rate.shape[0]
    whole = lambda shape: pl.BlockSpec(shape, lambda i, ids, spots: (0, 0))
    return pl.pallas_call(
        functools.partial(project_kernel, layout, len(w_mix)),
        grid_spec=pltpu.PrefetchScalarGridSpec(
            num_scalar_prefetch=2,
            grid=(1,),
            in_specs=[whole(a.shape) for a in (w_rate, *arrays, *w_mix)],
            out_specs=[whole((total, cols)), whole((total, rates))],
        ),
        out_shape=[
            jax.ShapeDtypeStruct((total, cols), BF16),
            jax.ShapeDtypeStruct((total, rates), F32),
        ],
        compiler_params=pltpu.CompilerParams(vmem_limit_bytes=VMEM_LIMIT),
        cost_estimate=LIGHT,
    )(ids, spots, w_rate, *arrays, *w_mix)


def normed_back_kernel(pieces, blocks, spots_ref, *refs):
    mixes, gates, rates, normed = (refs[i * blocks : (i + 1) * blocks] for i in range(4))
    rate_ref, before_ref = refs[4 * blocks : 4 * blocks + 2]
    w_refs = refs[4 * blocks + 2 : 4 * blocks + 2 + pieces]
    part_ref, sums_ref = refs[4 * blocks + 2 + pieces :]
    heads = gates[0].shape[1] // DV
    left = jnp.concatenate(
        [
            jnp.concatenate([ref[:, h * size : (h + 1) * size] for ref in group], axis=0)
            for h in range(heads)
            for group, size in ((mixes, MIX), (gates, DV))
        ],
        axis=1,
    )
    rate = jnp.concatenate([ref[...].astype(BF16) for ref in rates], axis=0)
    count = rate.shape[1]
    sums_ref[...] = before_ref[...]
    for b, w_ref in enumerate(w_refs):
        cols = block_columns(spots_ref, b, w_ref.shape[0])
        part = mm(left, w_ref[...], 1, 1) + mm(rate, rate_ref[:, cols])
        part_ref[:, cols] = part.astype(BF16)
        right = jnp.concatenate([ref[:, cols] for ref in normed], axis=0)
        sums_ref[:count, cols] += mm(rate, right, 0, 0)
        sums_ref[4:5, cols] += jnp.sum(part * right.astype(F32), axis=0, keepdims=True)


def normed_back(spots, order, blocks, grad_mixed, grad_gates, grad_rates, normed, w_mix, w_rate, before):
    total, width = normed.shape
    rows = total // blocks
    rates = w_rate.shape[0]
    count = len(order)
    block = lambda k, wide: pl.BlockSpec((rows, wide), lambda i, spots: (k, 0))
    whole = lambda i, spots: (0, 0)
    return pl.pallas_call(
        functools.partial(normed_back_kernel, len(w_mix), count),
        grid_spec=pltpu.PrefetchScalarGridSpec(
            num_scalar_prefetch=1,
            grid=(1,),
            in_specs=[
                *[block(k, grad_mixed.shape[1]) for k in order],
                *[block(k, grad_gates.shape[1]) for k in order],
                *[block(k, rates) for k in order],
                *[block(k, width) for k in order],
                pl.BlockSpec((rates, width), whole),
                pl.BlockSpec((8, width), whole),
                *[pl.BlockSpec(w.shape, whole) for w in w_mix],
            ],
            out_specs=[pl.BlockSpec((count * rows, width), whole), pl.BlockSpec((8, width), whole)],
        ),
        out_shape=[
            jax.ShapeDtypeStruct((count * rows, width), BF16),
            jax.ShapeDtypeStruct((8, width), F32),
        ],
        compiler_params=pltpu.CompilerParams(vmem_limit_bytes=VMEM_LIMIT),
        cost_estimate=LIGHT,
    )(
        spots,
        *[grad_mixed] * count,
        *[grad_gates] * count,
        *[grad_rates] * count,
        *[normed] * count,
        w_rate,
        before,
        *w_mix,
    )


def stack_kernel(layout, *refs):
    out_ref = refs[len(layout)]
    for (_, start), ref in zip(layout, refs):
        out_ref[start : start + ref.shape[0], :] = ref[...]


def stacked(found, total):
    layout, arrays = layout_of(found, total)
    return pl.pallas_call(
        functools.partial(stack_kernel, layout),
        out_shape=jax.ShapeDtypeStruct((total, arrays[0].shape[1]), arrays[0].dtype),
        compiler_params=pltpu.CompilerParams(vmem_limit_bytes=VMEM_LIMIT),
        cost_estimate=LIGHT,
    )(*arrays)


def finish_kernel(first_ref, second_ref, buffer_ref, out_ref):
    half = first_ref.shape[0]
    out_ref[:half, :] = first_ref[...]
    out_ref[half:, :] = second_ref[...]


def finish_stack(buffer, pieces, k):
    half, width = pieces[0].shape
    whole = pl.BlockSpec((half, width), lambda i: (0, 0))
    return pl.pallas_call(
        finish_kernel,
        grid=(1,),
        in_specs=[whole, whole, pl.BlockSpec(memory_space=pl.ANY)],
        out_specs=pl.BlockSpec((2 * half, width), lambda i: (k, 0)),
        out_shape=jax.ShapeDtypeStruct(buffer.shape, buffer.dtype),
        input_output_aliases={2: 0},
        cost_estimate=LIGHT,
    )(*pieces, buffer)


def outer_kernel(left_ref, right_ref, out_ref):
    out_ref[...] = mm(left_ref[...], right_ref[...], 0, 0).astype(BF16)


def outer(left, right):
    total, m = left.shape
    n = right.shape[1]
    by_rows = m % 512 == 0 and m > 512
    rows = 512 if by_rows else m
    cols = n if by_rows or n % 512 else 512
    return pl.pallas_call(
        outer_kernel,
        grid=(m // rows, n // cols),
        in_specs=[
            pl.BlockSpec((total, rows), lambda i, j: (0, i)),
            pl.BlockSpec((total, cols), lambda i, j: (0, j)),
        ],
        out_specs=pl.BlockSpec((rows, cols), lambda i, j: (i, j)),
        out_shape=jax.ShapeDtypeStruct((m, n), BF16),
        compiler_params=pltpu.CompilerParams(vmem_limit_bytes=VMEM_LIMIT),
        cost_estimate=LIGHT,
    )(left, right)


def turn_kernel(count, *refs):
    for i in range(count):
        refs[count + i][...] = refs[i][...].astype(F32).T.astype(BF16)


def turned(arrays):
    rows, width = arrays[0].shape
    step = 512
    return pl.pallas_call(
        functools.partial(turn_kernel, len(arrays)),
        grid=(width // step,),
        in_specs=[pl.BlockSpec((rows, step), lambda i: (0, i))] * len(arrays),
        out_specs=[pl.BlockSpec((step, rows), lambda i: (i, 0))] * len(arrays),
        out_shape=[jax.ShapeDtypeStruct((width, rows), BF16)] * len(arrays),
        compiler_params=pltpu.CompilerParams(vmem_limit_bytes=VMEM_LIMIT),
        cost_estimate=LIGHT,
    )(*arrays)


def widen_kernel(count, *refs):
    for i in range(count):
        refs[count + i][...] = refs[i][...].astype(F32)


def widen(arrays):
    steps = 4
    specs = [pl.BlockSpec((a.shape[0] // steps, a.shape[1]), lambda i: (i, 0)) for a in arrays]
    return pl.pallas_call(
        functools.partial(widen_kernel, len(arrays)),
        grid=(steps,),
        in_specs=specs,
        out_specs=specs,
        out_shape=[jax.ShapeDtypeStruct(a.shape, F32) for a in arrays],
        compiler_params=pltpu.CompilerParams(vmem_limit_bytes=VMEM_LIMIT),
        cost_estimate=LIGHT,
    )(*arrays)


def join_kernel(heads, mix_ref, gate_ref, out_ref):
    for h in range(heads):
        out_ref[:, h * PER : h * PER + MIX] = mix_ref[:, h * MIX : (h + 1) * MIX].astype(F32)
        out_ref[:, h * PER + MIX : (h + 1) * PER] = gate_ref[:, h * DV : (h + 1) * DV].astype(F32)


def join_heads(mix, gate):
    rows = mix.shape[0]
    heads = gate.shape[1] // DV
    steps = 4
    spec = lambda wide: pl.BlockSpec((rows // steps, wide), lambda i: (i, 0))
    return pl.pallas_call(
        functools.partial(join_kernel, heads),
        grid=(steps,),
        in_specs=[spec(mix.shape[1]), spec(gate.shape[1])],
        out_specs=spec(heads * PER),
        out_shape=jax.ShapeDtypeStruct((rows, heads * PER), F32),
        compiler_params=pltpu.CompilerParams(vmem_limit_bytes=VMEM_LIMIT),
        cost_estimate=LIGHT,
    )(mix, gate)


def times_kernel(left_ref, right_ref, out_ref):
    out_ref[...] = mm(left_ref[...], right_ref[...])


def times(left, right):
    total, depth = left.shape
    n = right.shape[1]
    rows = 256
    return pl.pallas_call(
        times_kernel,
        grid=(total // rows,),
        in_specs=[
            pl.BlockSpec((rows, depth), lambda i: (i, 0)),
            pl.BlockSpec((depth, n), lambda i: (0, 0)),
        ],
        out_specs=pl.BlockSpec((rows, n), lambda i: (i, 0)),
        out_shape=jax.ShapeDtypeStruct((total, n), F32),
        compiler_params=pltpu.CompilerParams(vmem_limit_bytes=VMEM_LIMIT),
        cost_estimate=LIGHT,
    )(left, right)


def finish_all_kernel(heads, count, mix_ref, gate_ref, *refs):
    join_kernel(heads, mix_ref, gate_ref, refs[count])
    for i in range(count):
        refs[count + 1 + i][...] = refs[i][...].astype(F32)


def finish_all(mix, gate, others):
    heads = gate.shape[1] // DV
    steps = 4
    spec = lambda a, wide: pl.BlockSpec((a.shape[0] // steps, wide), lambda i: (i, 0))
    plain = [spec(a, a.shape[1]) for a in others]
    return pl.pallas_call(
        functools.partial(finish_all_kernel, heads, len(others)),
        grid=(steps,),
        in_specs=[spec(mix, mix.shape[1]), spec(gate, gate.shape[1]), *plain],
        out_specs=[spec(mix, heads * PER), *plain],
        out_shape=[
            jax.ShapeDtypeStruct((mix.shape[0], heads * PER), F32),
            *[jax.ShapeDtypeStruct(a.shape, F32) for a in others],
        ],
        compiler_params=pltpu.CompilerParams(vmem_limit_bytes=VMEM_LIMIT),
        cost_estimate=LIGHT,
    )(mix, gate, *others)
def ring_order(count):
    return list(range(0, count, 2)) + list(range(1, count, 2))[::-1]


def ring_step(value, axis, step):
    order = ring_order(lax.axis_size(axis))
    count = len(order)
    return lax.ppermute(value, axis, [(order[i], order[(i + step) % count]) for i in range(count)])


def ring_ids(axis):
    order = ring_order(lax.axis_size(axis))
    count = len(order)
    place = {device: i for i, device in enumerate(order)}
    ahead = [[order[(place[device] + k) % count] for k in range(count)] for device in range(count)]
    back = [[row.index(device) for device in range(count)] for row in ahead]
    row = lax.dynamic_index_in_dim(
        jnp.array([a + b for a, b in zip(ahead, back)], jnp.int32), lax.axis_index(axis), 0, False
    )
    return row[:count], row[count:]


def after(value, *earlier):
    return lax.optimization_barrier((value, *earlier))[0]


def together(*values):
    return lax.optimization_barrier(values)


def window(fillers, hop, gate):
    return fillers[hop](lambda value: after(value, gate)) if hop in fillers else ()


def ring_gather(shard, axis, fillers={}, stack=True):
    count = lax.axis_size(axis)
    far = count // 2
    half = shard.shape[0] // 2
    total = count * shard.shape[0]
    found = {0: [shard]}
    forward = backward = shard
    buffer = None
    for hop in range(1, far + 1):
        gate = forward
        extra = list(window(fillers, hop, gate))
        if hop < far:
            forward = ring_step(forward, axis, 1)
            backward = ring_step(backward, axis, -1)
            found[count - hop] = [forward]
            found[hop] = [backward]
        else:
            if stack:
                buffer = stacked({k: [after(p, gate) for p in ps] for k, ps in found.items()}, total)
                extra.append(buffer)
            forward = ring_step(forward[:half], axis, 1)
            backward = ring_step(backward[half:], axis, -1)
            found[hop] = [forward, backward]
        forward, backward, *_ = together(forward, backward, *extra)
    found[far] = [forward, backward]
    return finish_stack(buffer, found[far], far) if stack else found


def ring_scatter(take, rows, axis, fillers={}):
    count = lax.axis_size(axis)
    far = count // 2
    size = rows // 2
    flows = [[take(far, 0, size), None], [None, take(far, size, size)]]
    gate = take(far, 0, size)
    for hop in range(1, far + 1):
        flows = [
            [flow[way] if flow[way] is None else ring_step(flow[way], axis, 1 - 2 * way) for way in range(2)]
            for flow in flows
        ]
        extra = window(fillers, hop, gate)
        flat = together(*[a for flow in flows for a in flow if a is not None], *extra)
        flat = iter(flat)
        flows = [[None if a is None else next(flat) for a in flow] for flow in flows]
        s = far - hop
        if s:
            for part, flow in enumerate(flows):
                for way, k in enumerate((s, count - s)):
                    piece = take(k, part * size, size)
                    flow[way] = piece if flow[way] is None else flow[way] + piece
            gate = flows[0][0]
    totals = [
        take(0, part * size, size).astype(F32) + flow[0].astype(F32) + flow[1].astype(F32)
        for part, flow in enumerate(flows)
    ]
    return jnp.concatenate(totals, axis=0)


def near_rows(array, rows):
    return lambda k, start, size: lax.slice_in_dim(array, k * rows + start, k * rows + start + size, axis=0)


def swap(value, axis, bit):
    count = lax.axis_size(axis)
    return lax.ppermute(value, axis, [(i, i ^ bit) for i in range(count)])


def pair_spots(axis):
    count = lax.axis_size(axis)
    order = jnp.arange(count, dtype=jnp.int32)
    return lax.axis_index(axis) ^ order if count == 4 else order


def pair_far(shard, axis, *pins):
    if lax.axis_size(axis) != 4:
        return lax.all_gather(shard, axis)
    return swap(after(shard, *pins), axis, 2)


def pair_gather(shard, far, axis, *pins):
    count = lax.axis_size(axis)
    if count != 4:
        return [far[b] for b in range(count)]
    return [shard, swap(after(shard, *pins), axis, 1), far, swap(after(far, *pins), axis, 1)]


def seq_shards(value, axis):
    if lax.axis_size(axis) != 4:
        whole = lax.all_gather(value, axis)
        return [whole[b] for b in range(lax.axis_size(axis))]
    return [value] + [swap(value, axis, b) for b in range(1, 4)]


def butterfly(value, axis):
    bit = 1
    while bit < lax.axis_size(axis):
        value = value + swap(value, axis, bit)
        bit *= 2
    return value


def per_device(
    tokens,
    w_qkvg,
    w_rates,
    conv_weight,
    head_bias,
    norm_gain,
    head_gain,
    mlp_gain,
    w_out,
    w_ff_gate,
    w_ff_up,
    w_ff_down,
    cotangent,
):
    heads = head_bias.shape[1]
    own_rows = tokens.shape[0]
    contract = (((1,), (1,)), ((), ()))
    rows_first = (((0,), (0,)), ((), ()))
    dot = lambda a, b, dims: lax.dot_general(a, b, dims, preferred_element_type=F32)
    plain = (((1,), (0,)), ((), ()))
    ids, near_spots = ring_ids("head")
    spots = pair_spots("seq")
    place = lax.axis_index("seq").reshape(1)
    gain_row = head_gain.reshape(1, DV)
    bias_row = head_bias.T.reshape(1, 2 * heads)
    peers = lax.axis_size("seq")
    width = tokens.shape[1]
    keep = {}
    mix_far = pair_far(w_qkvg, "seq")
    inputs = tokens.astype(F32)
    inverse_one = lax.rsqrt(jnp.mean(inputs * inputs, axis=-1, keepdims=True) + epsilon)
    norm_normed = inputs * inverse_one
    hops = lax.axis_size("head") // 2
    last_window = hops

    rate_shard = w_rates.T
    if peers == 4:
        w_rate = jnp.zeros((2 * heads, width), BF16)
        for b in range(4):
            w_rate = lax.dynamic_update_slice_in_dim(
                w_rate,
                swap(rate_shard, "seq", b) if b else rate_shard,
                (place[0] ^ b) * rate_shard.shape[1],
                1,
            )
    else:
        w_rate = lax.all_gather(rate_shard, "seq", axis=1, tiled=True)

    count = 2 * hops
    stages = 4
    cot_found = {0: [cotangent]}
    cot_state = [cotangent, cotangent]

    def cot_hop(hop, *gates):
        forward, backward, *_ = together(*cot_state, *gates)
        if hop < hops:
            forward, backward = ring_step(forward, "head", 1), ring_step(backward, "head", -1)
            cot_found[count - hop], cot_found[hop] = [forward], [backward]
        else:
            half = own_rows // 2
            forward = ring_step(forward[:half], "head", 1)
            backward = ring_step(backward[half:], "head", -1)
            cot_found[hop] = [forward, backward]
        cot_state[:] = [forward, backward]
        return list(cot_state)

    def fetch_mix(pin):
        keep["mix"] = pair_gather(w_qkvg, pin(mix_far), "seq")
        return keep["mix"]

    fillers = {last_window: fetch_mix}
    normed_found = ring_gather((norm_normed * norm_gain).astype(BF16), "head", fillers, False)
    w_mix = keep["mix"]
    out_rows = lax.all_gather(after(w_out, mix_far), "seq", axis=1, tiled=True)

    stage_hops = {
        stage: range(1 + hops * stage // stages, 1 + hops * (stage + 1) // stages) for stage in range(stages)
    }

    def cot_stage(stage, gate):
        made = []
        for hop in stage_hops[stage]:
            made = cot_hop(hop, gate)
        return made

    cot_stage(0, normed_found[hops][0])
    projected, rates = project(ids, spots, normed_found, w_mix, w_rate)
    seq_rows = projected.shape[0]
    halo_rows = shifted(projected[seq_rows - HALO :], "seq", 1)
    projected, *_ = together(projected, *cot_state)
    cot_stage(1, projected)
    out_local, query_map, *saved, end_state = mixer_forward(
        projected, halo_rows, rates, bias_row, conv_weight, GROUP
    )
    end_state, *_ = together(end_state, *cot_state)
    cot_stage(2, end_state)
    maps = seq_shards(end_state, "seq")
    maps = list(together(*maps, *cot_state))[:peers]
    cot_stage(3, maps[1])
    value, gated, branch_part, incoming = gate_output(
        ids, place, maps, out_local, query_map, projected, gain_row, out_rows
    )
    branch_part, *_ = together(branch_part, *cot_state)
    fetch = lambda w, *pins: lax.all_gather(after(w, *pins), "seq", axis=1, tiled=True)
    down_w = fetch(w_ff_down, *maps)
    gate_w = fetch(w_ff_gate, *maps)
    up_w = fetch(w_ff_up, *maps)

    def stack_normed(pin):
        keep["normed"] = stacked({k: [pin(p) for p in ps] for k, ps in normed_found.items()}, seq_rows)
        return (keep["normed"],)

    def stack_cotangent(pin):
        keep["cot"] = stacked({k: [pin(p) for p in ps] for k, ps in cot_found.items()}, seq_rows)
        return (keep["cot"],)

    def turn_down(pin):
        keep["down_t"] = turned([pin(down_w)])
        return keep["down_t"]

    def turn_others(pin):
        keep["others_t"] = turned([pin(gate_w), pin(up_w)])
        return keep["others_t"]

    residual = inputs + ring_scatter(
        near_rows(branch_part, own_rows), own_rows, "head", {1: stack_cotangent, 2: stack_normed}
    )
    inverse_two = lax.rsqrt(jnp.mean(residual * residual, axis=-1, keepdims=True) + epsilon)
    mlp_normed = residual * inverse_two

    def hidden_gradient(pin):
        keep["gh"] = times(pin(keep["cot"]), keep["down_t"][0])
        return (keep["gh"],)

    mlp_near = ring_gather((mlp_normed * mlp_gain).astype(BF16), "head", {1: turn_down, 2: hidden_gradient, 3: turn_others})
    normed, cotangent_near, grad_hidden = keep["normed"], keep["cot"], keep["gh"]

    gate_pre, up_pre = (dot(mlp_near, w, plain) for w in keep["others_t"])
    ff_sigmoid = jax.nn.sigmoid(gate_pre)
    ff_silu = gate_pre * ff_sigmoid
    hidden = (ff_silu * up_pre).astype(BF16)
    ff_slope = ff_sigmoid * (1.0 + gate_pre * (1.0 - ff_sigmoid))
    grad_gate_pre = (grad_hidden * up_pre * ff_slope).astype(BF16)
    grad_up_pre = (grad_hidden * ff_silu).astype(BF16)
    grad_mlp_part = (dot(grad_gate_pre, gate_w, plain) + dot(grad_up_pre, up_w, plain)).astype(BF16)

    scatter = lambda a: lax.psum_scatter(a, "seq", scatter_dimension=1, tiled=True)

    def weight_product(name, left, right, before=None):
        def filler(pin):
            made = [outer(pin(left), right)] if left is not None else []
            if before is not None:
                keep[before, "sum"] = scatter(pin(keep[before]))
            if made:
                keep[name] = made[0]
            return made

        return filler

    def output_rows(pin):
        keep["up", "sum"] = scatter(pin(keep["up"]))
        keep["output"] = dot(pin(hidden), down_w, plain).astype(BF16)
        return (keep["output"],)

    grad_mlp_in = ring_scatter(
        near_rows(grad_mlp_part, own_rows),
        own_rows,
        "head",
        {
            1: weight_product("down", hidden, cotangent_near),
            2: weight_product("gate", grad_gate_pre, mlp_near, "down"),
            3: weight_product("up", grad_up_pre, mlp_near, "gate"),
            4: output_rows,
        },
    )

    output_part = keep["output"]
    mlp_gain_part = jnp.sum(grad_mlp_in * mlp_normed, axis=0)
    scaled_two = grad_mlp_in * mlp_gain
    grad_residual = cotangent.astype(F32) + inverse_two * (
        scaled_two - mlp_normed * jnp.mean(scaled_two * mlp_normed, axis=-1, keepdims=True)
    )

    grad_down_s, grad_gate_s, grad_up_s = (keep[name, "sum"] for name in ("down", "gate", "up"))
    branch_near = ring_gather(
        grad_residual.astype(BF16), "head", {2: lambda pin: [grad_down_s], 4: lambda pin: [grad_gate_s]}
    )
    take_output = near_rows(output_part, own_rows)
    output_state = [None, None]
    known = lambda: [a for a in output_state if a is not None]

    def output_hops(stage, *gates):
        for hop in range(hops * (stage - 1) // stages, hops * stage // stages):
            here = []
            for way, k in enumerate((hops - hop, count - hops + hop)):
                if hop == 0 and way == 1:
                    here.append(None)
                    continue
                piece = take_output(k, 0, own_rows)
                total = piece if output_state[way] is None else output_state[way] + piece
                here.append(ring_step(after(total, *gates), "head", 1 - 2 * way))
            output_state[:] = here

    output_hops(1, branch_near)
    grad_gate_mix, grad_mixer, head_gain_part, local_grad = gate_backward(
        ids, branch_near, out_rows, value, projected, query_map, gain_row, heads
    )
    local_low, *_ = together(local_grad, *known())
    shares = seq_shards(local_low, "seq")
    gate_grad_w = outer(keep["normed"], together(grad_gate_mix, *shares[1:])[0])
    output_hops(2, shares[1])
    first_share, gate_grad_w, *_ = together(shares[0], gate_grad_w, *known())
    gate_grad_s = lax.psum_scatter(gate_grad_w, "seq", scatter_dimension=0, tiled=True)
    output_hops(3, gate_grad_w)
    grad_mixed, grad_rates, seq_sums, tail_rows, lead_rows = mixer_backward(
        projected, halo_rows, rates, bias_row, conv_weight, saved,
        grad_mixer, value, incoming, place, near_spots, maps, [first_share, *shares[1:]], GROUP,
    )
    grad_mixed, gate_grad_s, grad_up_s, *_ = together(grad_mixed, gate_grad_s, grad_up_s, *known())
    later_rows = shifted(lead_rows, "seq", -1)
    output_hops(4, grad_mixed)
    padded = jnp.concatenate([jnp.zeros((HALO, heads * MIX), F32), later_rows])
    last_rows = tail_rows + sum(
        conv_weight[i] * padded[CONV - 1 - i : CONV - 1 - i + HALO] for i in range(CONV)
    )
    last_start = near_spots[count - 1] * own_rows + own_rows - HALO
    grad_mixed = lax.dynamic_update_slice(grad_mixed, last_rows.astype(BF16), (last_start, 0))
    mix_grad_w = outer(keep["normed"], grad_mixed)
    grad_mixed, mix_grad_w = together(grad_mixed, mix_grad_w)
    mix_grad_s = lax.psum_scatter(mix_grad_w, "seq", scatter_dimension=0, tiled=True)
    early = [hops] + ([hops - 1, hops + 1] if hops > 1 else [])
    late = [k for s in range(hops - 2, 0, -1) for k in (s, count - s)] + [0]
    place_of = {k: (0, i) for i, k in enumerate(early)} | {k: (1, i) for i, k in enumerate(late)}
    parts = []
    part, sums = normed_back(
        spots, early, count, grad_mixed, grad_gate_mix, grad_rates, normed, w_mix, w_rate, jnp.zeros((8, width), F32)
    )
    part, *_ = together(part, *known())
    parts.append(part)

    def take(k, start, size):
        which, i = place_of[k]
        return lax.slice_in_dim(parts[which], i * own_rows + start, i * own_rows + start + size, axis=0)

    def late_rows(pin):
        part, keep["sums"] = normed_back(
            spots, late, count, pin(grad_mixed), grad_gate_mix, grad_rates, normed, w_mix, w_rate, sums
        )
        parts.append(part)
        return (part,)

    def first_window(pin):
        return late_rows(pin)

    def second_window(pin):
        sums = pin(keep["sums"])
        gains = jnp.concatenate([mlp_gain_part[None], head_gain_part, jnp.zeros((1, width - DV), F32)], axis=1)
        gains = jnp.pad(gains, ((4, 3), (0, 0)))
        small = jnp.concatenate([sums, gains, seq_sums], axis=1)
        keep["small"] = small + swap(small, "seq", 1)
        out_grad_w = outer(gated, pin(branch_near))
        keep["out"] = scatter(out_grad_w)
        return (keep["small"], out_grad_w)

    def third_window(pin):
        small = pin(keep["small"])
        bit = 2
        while bit < peers:
            small = small + swap(small, "seq", bit)
            bit *= 2
        keep["small"] = small
        keep["gains"] = small[4:5, : 3 * width]
        return (small, mix_grad_s)

    grad_normed = ring_scatter(
        take, own_rows, "head", {1: first_window, 2: second_window, 3: third_window}
    )
    scaled_one = grad_normed * norm_gain
    grad_input = grad_residual + inverse_one * (
        scaled_one - norm_normed * jnp.mean(scaled_one * norm_normed, axis=-1, keepdims=True)
    )
    output = (
        residual + sum(a.astype(F32) for a in known()) + take_output(0, 0, own_rows).astype(F32)
    ).astype(BF16)
    small, gains = keep["small"], after(keep["gains"], grad_normed)
    bit = 1
    while bit < count:
        gains = gains + swap(gains, "head", bit)
        bit *= 2
    joined, *wide = finish_all(mix_grad_s, gate_grad_s, [keep["out"], grad_gate_s, grad_up_s, grad_down_s])
    per_seq = w_rates.shape[0]
    return (
        output,
        grad_input,
        joined,
        lax.dynamic_slice_in_dim(small[: 2 * heads], place[0] * per_seq, per_seq, 1).T,
        small[:CONV, 3 * width :],
        small[CONV, 3 * width : 3 * width + 2 * heads].reshape(heads, 2).T,
        gains[0, :width] / norm_gain,
        gains[0, 2 * width : 2 * width + DV],
        gains[0, width : 2 * width],
        *wide,
    )


def solution(mesh):
    in_specs = (
        P(("seq", "head"), None),
        P("seq", "head"),
        P("seq", "head"),
        P(None, "head"),
        P(None, "head"),
        P(),
        P(),
        P(),
        P("head", "seq"),
        P("head", "seq"),
        P("head", "seq"),
        P("head", "seq"),
        P(("seq", "head"), None),
    )
    out_specs = (
        P(("seq", "head"), None),
        P(("seq", "head"), None),
        P("seq", "head"),
        P("seq", "head"),
        P(None, "head"),
        P(None, "head"),
        P(),
        P(),
        P(),
        P("head", "seq"),
        P("head", "seq"),
        P("head", "seq"),
        P("head", "seq"),
    )
    return jax.shard_map(
        per_device, mesh=mesh, in_specs=in_specs, out_specs=out_specs, check_vma=False
    )
```

```python
import functools
import jax
import jax.numpy as jnp
from jax import lax
from jax.experimental import pallas as pl
from jax.experimental.pallas import tpu as pltpu
from jax.sharding import PartitionSpec as P

DK = 128
DV = 256
CONV = 4
CHUNK = 128
MIX = 2 * DK + DV
PER = 2 * DK + 2 * DV
GROUP = 4
epsilon = 1e-06
F32 = jnp.float32
BF16 = jnp.bfloat16
HALO = 16
VMEM_LIMIT = 56 * 1024 * 1024
LIGHT = pl.CostEstimate(flops=1, bytes_accessed=1, transcendentals=0)


def shifted(value, axis, steps):
    count = lax.axis_size(axis)
    leading, last = (max(0, -steps), min(count, count - steps))
    return lax.ppermute(value, axis, [(source, source + steps) for source in range(leading, last)])


def mm(a, b, ca=1, cb=0):
    return lax.dot_general(
        a.astype(BF16), b.astype(BF16), (((ca,), (cb,)), ((), ())), preferred_element_type=F32
    )


def mmx(a, b, ca=1, cb=0):
    return lax.dot_general(
        a, b, (((ca,), (cb,)), ((), ())), preferred_element_type=F32, precision=lax.Precision.HIGHEST
    )


def block_columns(spots_ref, b, width):
    return pl.ds(pl.multiple_of(spots_ref[b] * width, 128), width)


def chosen(refs, place_ref, source, h, rows):
    value = refs[0][h, rows, :]
    for b in range(1, len(refs)):
        here = (place_ref[0] ^ b) == source if len(refs) == 4 else b == source
        value = jnp.where(here, refs[b][h, rows, :], value)
    return value


def softplus(x):
    return jnp.maximum(x, 0.0) + jnp.log1p(jnp.exp(-jnp.abs(x)))


def sigmoid(x):
    return 1.0 / (1.0 + jnp.exp(-x))


def iotas(n):
    return (
        lax.broadcasted_iota(jnp.int32, (n, n), 0),
        lax.broadcasted_iota(jnp.int32, (n, n), 1),
    )


def inverse_parts(mats, rows, cols):
    base = 16
    near = (rows // base) == (cols // base)
    diag = [jnp.where(near, a, 0.0) for a in mats]
    result = [-d for d in diag]
    power = [mm(d, d) for d in diag]
    span = 2
    while True:
        result = [r + p + mm(r, p) for r, p in zip(result, power)]
        span *= 2
        if span >= base:
            break
        power = [mm(p, p) for p in power]
    size = base
    n = mats[0].shape[0]
    while size < n:
        cross = ((rows // (2 * size)) == (cols // (2 * size))) & ((rows // size) != (cols // size))
        off = [jnp.where(cross, a, 0.0) for a in mats]
        left = [o + mm(r, o) for o, r in zip(off, result)]
        result = [r - x - mm(x, r) for r, x in zip(result, left)]
        size *= 2
    return result


def conv_scratch(first, proj_ref, prev_ref, halo_ref, x_ref, heads, rows):
    for h in range(heads):
        cols = slice(h * PER, h * PER + MIX)
        before = jnp.where(first, halo_ref[:, cols].astype(F32), prev_ref[:, cols].astype(F32))
        x_ref[0:8, h * MIX : (h + 1) * MIX] = before[HALO - 8 :]
        x_ref[8 : 8 + rows, h * MIX : (h + 1) * MIX] = proj_ref[:, cols].astype(F32)


def conv_pre(x_ref, taps_ref, h, row):
    cols = slice(h * MIX, (h + 1) * MIX)
    total = None
    for i in range(CONV):
        part = taps_ref[i : i + 1, cols] * x_ref[pl.ds(row + 8 - (CONV - 1) + i, CHUNK), cols]
        total = part if total is None else total + part
    return total


def unit(a):
    r = lax.rsqrt(jnp.sum(a * a, axis=-1, keepdims=True) + epsilon)
    return a * r, r


def forward_kernel(
    heads, group,
    proj_ref, prev_ref, halo_ref, rates_ref, bias_ref, taps_ref,
    olocal_ref, qmap_ref, state_ref, uw_ref, inv_ref, trans_ref, qe_ref, end_ref,
    x_ref, carry_ref,
):
    step = pl.program_id(0)
    rows_here = CHUNK * group
    conv_scratch(step == 0, proj_ref, prev_ref, halo_ref, x_ref, heads, rows_here)
    ri, ci = iotas(CHUNK)
    included = ri >= ci
    strictly = ri > ci
    lower = jnp.where(included, 1.0, 0.0)
    upper = jnp.where(ri <= ci, 1.0, 0.0)

    @pl.when(step == 0)
    def _():
        for h in range(heads):
            carry_ref[h, :DV, :] = jnp.zeros((DV, DK), F32)
            carry_ref[h, DV:, :] = jnp.where(ri == ci, 1.0, 0.0)

    pairs = [(g, h) for g in range(group) for h in range(heads)]
    logits = rates_ref[...] + bias_ref[...]
    log_decay = -softplus(logits)
    strength = sigmoid(logits)
    cums, cum_rows = [], []
    for g in range(group):
        part = log_decay[g * CHUNK : (g + 1) * CHUNK]
        cums.append(mmx(lower, part))
        cum_rows.append(mmx(part, upper, 0, 0))
    mats, scores, rhs, tails, scaled_q, finals = [], [], [], [], [], []
    for g, h in pairs:
        pre = conv_pre(x_ref, taps_ref, h, g * CHUNK)
        mixed = pre * sigmoid(pre)
        q = unit(mixed[:, :DK])[0] * DK ** (-0.5)
        k = unit(mixed[:, DK : 2 * DK])[0]
        v = mixed[:, 2 * DK :]
        cum = cums[g][:, 2 * h : 2 * h + 1]
        cum_row = cum_rows[g][2 * h : 2 * h + 1, :]
        beta = strength[g * CHUNK : (g + 1) * CHUNK, 2 * h + 1 : 2 * h + 2]
        growth = jnp.exp(cum)
        decays = jnp.where(included, jnp.exp(jnp.where(included, cum - cum_row, 0.0)), 0.0)
        grams = mm(jnp.concatenate([q, k], axis=0), k, 1, 1)
        scores.append(grams[:CHUNK] * decays)
        mats.append(jnp.where(strictly, beta * decays * grams[CHUNK:], 0.0))
        rhs.append(jnp.concatenate([beta * v, beta * growth * k], axis=1))
        last = cum[CHUNK - 1 : CHUNK, :]
        tails.append(k * jnp.exp(last - cum))
        scaled_q.append(growth * q)
        finals.append(jnp.exp(last))
    inverses = inverse_parts(mats, ri, ci)
    solved = [b + mm(r, b) for r, b in zip(inverses, rhs)]
    mixes = [mm(p, u) for p, u in zip(scores, solved)]
    adds = [mm(u, t, 0, 0) for u, t in zip(solved, tails)]
    for j, (g, h) in enumerate(pairs):
        inv_ref[h, g] = inverses[j].astype(BF16)
        uw_ref[h, g] = solved[j].astype(BF16)
        qe_ref[h, g] = (scaled_q[j] - mixes[j][:, DV:]).astype(BF16)
        trans_ref[h, g] = (-adds[j][DV:]).astype(BF16)
        olocal_ref[g * CHUNK : (g + 1) * CHUNK, h * DV : (h + 1) * DV] = mixes[j][:, :DV]
    for h in range(heads):
        now = carry_ref[h]
        for g in range(group):
            j = pairs.index((g, h))
            low = now.astype(BF16)
            state_ref[h, g] = low
            moved = finals[j] * now + mm(low, trans_ref[h, g])
            now = jnp.concatenate([moved[:DV] + adds[j][:DV], moved[DV:]], axis=0)
        carry_ref[h] = now
        end_ref[h] = now.astype(BF16)
    for j, (g, h) in enumerate(pairs):
        both = mm(qe_ref[h, g], state_ref[h, g], 1, 1)
        rows = slice(g * CHUNK, (g + 1) * CHUNK)
        olocal_ref[rows, h * DV : (h + 1) * DV] += both[:, :DV]
        qmap_ref[rows, h * DK : (h + 1) * DK] = both[:, DV:].astype(BF16)


def mixer_forward(projected, halo, rates, bias_row, taps, group):
    total = projected.shape[0]
    heads = rates.shape[1] // 2
    rows = CHUNK * group
    steps = total // rows
    chunks = total // CHUNK
    whole = lambda i: (0, 0)
    saved = lambda a, b: (
        jax.ShapeDtypeStruct((heads, chunks, a, b), BF16),
        pl.BlockSpec((heads, group, a, b), lambda i: (0, i, 0, 0)),
    )
    outs = [
        (jax.ShapeDtypeStruct((total, heads * DV), F32), pl.BlockSpec((rows, heads * DV), lambda i: (i, 0))),
        (jax.ShapeDtypeStruct((total, heads * DK), BF16), pl.BlockSpec((rows, heads * DK), lambda i: (i, 0))),
        saved(DV + DK, DK),
        saved(CHUNK, DV + DK),
        saved(CHUNK, CHUNK),
        saved(DK, DK),
        saved(CHUNK, DK),
        (jax.ShapeDtypeStruct((heads, DV + DK, DK), BF16), pl.BlockSpec((heads, DV + DK, DK), lambda i: (0, 0, 0))),
    ]
    return pl.pallas_call(
        functools.partial(forward_kernel, heads, group),
        grid=(steps,),
        in_specs=[
            pl.BlockSpec((rows, heads * PER), lambda i: (i, 0)),
            pl.BlockSpec((HALO, heads * PER), lambda i: (jnp.maximum(i * (rows // HALO) - 1, 0), 0)),
            pl.BlockSpec((HALO, heads * PER), whole),
            pl.BlockSpec((rows, 2 * heads), lambda i: (i, 0)),
            pl.BlockSpec((1, 2 * heads), whole),
            pl.BlockSpec((CONV, heads * MIX), whole),
        ],
        out_shape=[o[0] for o in outs],
        out_specs=[o[1] for o in outs],
        scratch_shapes=[
            pltpu.VMEM((rows + 8, heads * MIX), F32),
            pltpu.VMEM((heads, DV + DK, DK), F32),
        ],
        compiler_params=pltpu.CompilerParams(vmem_limit_bytes=VMEM_LIMIT),
        cost_estimate=LIGHT,
    )(projected, projected, halo, rates, bias_row, taps)


def backward_kernel(
    heads, group, steps, peers, own,
    proj_ref, prev_ref, halo_ref, rates_ref, bias_ref, taps_ref,
    state_ref, uw_ref, inv_ref, trans_ref, qe_ref,
    dout_ref, value_ref, incoming_ref, place_ref, spots_ref, *refs,
):
    maps_refs, refs = refs[:peers], refs[peers:]
    *local_refs, gp_ref, grates_ref, sums_ref, tail_ref, lead_ref, x_ref, d_ref, carry_ref, next_ref = refs
    step = pl.program_id(0)
    rows_here = CHUNK * group
    conv_scratch(step == steps - 1, proj_ref, prev_ref, halo_ref, x_ref, heads, rows_here)
    ri, ci = iotas(CHUNK)
    included = ri >= ci
    strictly = ri > ci
    lower = jnp.where(included, 1.0, 0.0)
    upper = jnp.where(ri <= ci, 1.0, 0.0)

    @pl.when(step == 0)
    def _():
        for h in range(heads):
            grad = jnp.zeros((DV, DK), F32)
            for turn in range(peers - 1):
                source = peers - 1 - turn
                share = jnp.zeros((DV, DK), F32)
                for b, local_ref in enumerate(local_refs):
                    here = (place_ref[0] ^ b) == source if peers == 4 else b == source
                    share = jnp.where(here, local_ref[h].astype(F32), share)
                moved = mm(grad, chosen(maps_refs, place_ref, source, h, slice(DV, DV + DK)), 1, 1) + share
                grad = jnp.where(source > place_ref[0], moved, grad)
            carry_ref[h] = grad
        d_ref[rows_here : rows_here + 8, :] = jnp.zeros((8, heads * MIX), F32)
        sums_ref[...] = jnp.zeros_like(sums_ref)

    @pl.when(step > 0)
    def _():
        d_ref[rows_here : rows_here + 8, :] = d_ref[0:8, :]

    def near_row(g):
        first = ((steps - 1 - step) * group + g) * CHUNK
        return pl.multiple_of(spots_ref[first // own] * own + first % own, CHUNK)

    pairs = [(g, h) for g in range(group) for h in range(heads)]
    logits = rates_ref[...] + bias_ref[...]
    log_decay = -softplus(logits)
    strength = sigmoid(logits)
    cums, cum_rows = [], []
    for g in range(group):
        part = log_decay[g * CHUNK : (g + 1) * CHUNK]
        cums.append(mmx(lower, part))
        cum_rows.append(mmx(part, upper, 0, 0))
    douts, injections = [], []
    for g, h in pairs:
        do = dout_ref[g * CHUNK : (g + 1) * CHUNK, h * DV : (h + 1) * DV]
        douts.append(do)
        injections.append(mm(do, qe_ref[h, g], 0, 0))
    for h in range(heads):
        now = carry_ref[h]
        for g in reversed(range(group)):
            j = pairs.index((g, h))
            last = cums[g][CHUNK - 1 : CHUNK, 2 * h : 2 * h + 1]
            next_ref[h, g] = now
            now = jnp.exp(last) * now + mm(now, trans_ref[h, g], 1, 1) + injections[j]
        carry_ref[h] = now
    lane = lax.broadcasted_iota(jnp.int32, (CHUNK, 2 * heads), 1)
    row_col = lax.broadcasted_iota(jnp.int32, (CHUNK, 1), 0)
    dcums = [jnp.zeros((CHUNK, 2 * heads), F32) for _ in range(group)]
    dlogits = [jnp.zeros((CHUNK, 2 * heads), F32) for _ in range(group)]
    for j, (g, h) in enumerate(pairs):
        pre = conv_pre(x_ref, taps_ref, h, g * CHUNK)
        sig = sigmoid(pre)
        mixed = pre * sig
        slope = sig * (1.0 + pre * (1.0 - sig))
        uq, rq = unit(mixed[:, :DK])
        q = uq * DK ** (-0.5)
        k, rk = unit(mixed[:, DK : 2 * DK])
        v = mixed[:, 2 * DK :]
        cum = cums[g][:, 2 * h : 2 * h + 1]
        cum_row = cum_rows[g][2 * h : 2 * h + 1, :]
        beta = strength[g * CHUNK : (g + 1) * CHUNK, 2 * h + 1 : 2 * h + 2]
        growth = jnp.exp(cum)
        decays = jnp.where(included, jnp.exp(jnp.where(included, cum - cum_row, 0.0)), 0.0)
        qb, kb = q.astype(BF16), k.astype(BF16)
        grams = mm(jnp.concatenate([qb, kb], axis=0), kb, 1, 1)
        scores = grams[:CHUNK] * decays
        last = cum[CHUNK - 1 : CHUNK, :]
        fade = jnp.exp(last - cum)
        tail = k * fade
        sl = state_ref[h, g]
        state = sl[:DV].astype(F32) + mm(incoming_ref[h], sl[DV:])
        after = next_ref[h, g]
        afterb = after.astype(BF16)
        stateb = state.astype(BF16)
        uw = uw_ref[h, g]
        errors = uw[:, :DV].astype(F32) - mm(uw[:, DV:], stateb, 1, 1)
        eb = errors.astype(BF16)
        do = douts[j]
        de = mm(scores, do, 0, 0) + mm(tail, afterb, 1, 1)
        db = de + mm(inv_ref[h, g], de, 0, 0)
        dbb = db.astype(BF16)
        stacked = jnp.concatenate([do, dbb], axis=0)
        against_e = mm(stacked, eb, 1, 1)
        against_s = mm(stacked, stateb)
        dp = against_e[:CHUNK]
        da = jnp.where(strictly, -against_e[CHUNK:], 0.0)
        dos = against_s[:CHUNK]
        dbs = against_s[CHUNK:]
        dpd = dp * decays
        dg = da * beta * decays
        dtail = mm(eb, afterb)
        dq = mm(dpd, kb) + growth * dos
        sym = dg + dg.T
        dk = (
            mm(jnp.concatenate([dpd.T, sym], axis=1), jnp.concatenate([qb, kb], axis=0))
            - beta * growth * dbs
            + fade * dtail
        )
        dv = beta * db
        dlogit = (1.0 - beta) * jnp.sum(db * errors, axis=1, keepdims=True)
        tdot = jnp.sum(tail * dtail, axis=1, keepdims=True)
        out = value_ref[g * CHUNK : (g + 1) * CHUNK, h * DV : (h + 1) * DV].astype(F32)
        dcum = jnp.sum(do.astype(F32) * out, axis=1, keepdims=True) - beta * jnp.sum(
            v * db, axis=1, keepdims=True
        )
        at_end = jnp.exp(last) * jnp.sum(jnp.sum(after * state, axis=1, keepdims=True), axis=0, keepdims=True) + jnp.sum(
            tdot, axis=0, keepdims=True
        )
        dcum = dcum + jnp.where(row_col == CHUNK - 1, at_end, 0.0)
        dcums[g] = jnp.where(lane == 2 * h, dcum, dcums[g])
        dlogits[g] = jnp.where(lane == 2 * h + 1, dlogit, dlogits[g])
        dq = dq * DK ** (-0.5)
        dmq = rq * (dq - uq * jnp.sum(uq * dq, axis=1, keepdims=True))
        dmk = rk * (dk - k * jnp.sum(k * dk, axis=1, keepdims=True))
        d_ref[g * CHUNK : (g + 1) * CHUNK, h * MIX : (h + 1) * MIX] = (
            jnp.concatenate([dmq, dmk, dv], axis=1) * slope
        )
    for g in range(group):
        rows = slice(g * CHUNK, (g + 1) * CHUNK)
        dld = mmx(upper, dcums[g])
        drate = jnp.where(lane % 2 == 0, -sigmoid(logits[rows]) * dld, dlogits[g])
        grates_ref[pl.ds(near_row(g), CHUNK), :] = drate
        sums_ref[CONV : CONV + 1, : 2 * heads] += jnp.sum(drate, axis=0, keepdims=True)
    for g, h in pairs:
        cols = slice(h * MIX, (h + 1) * MIX)
        row = g * CHUNK
        dpre = d_ref[pl.ds(row, CHUNK), cols]
        total = None
        for i in range(CONV):
            sums_ref[i : i + 1, cols] += jnp.sum(
                dpre * x_ref[pl.ds(row + 8 - (CONV - 1) + i, CHUNK), cols], axis=0, keepdims=True
            )
            part = taps_ref[i : i + 1, cols] * d_ref[pl.ds(row + CONV - 1 - i, CHUNK), cols]
            total = part if total is None else total + part
        gp_ref[pl.ds(near_row(g), CHUNK), cols] = total.astype(BF16)
        if g == group - 1:
            @pl.when(step == 0)
            def _(total=total, cols=cols):
                tail_ref[:, cols] = total[CHUNK - HALO :]

    @pl.when(step == steps - 1)
    def _():
        lead_ref[...] = d_ref[0:8, :]


def mixer_backward(projected, halo, rates, bias_row, taps, saved, dout, value, incoming, place, spots, maps, local, group):
    state, uw, inv, trans, qe = saved
    total = projected.shape[0]
    heads = rates.shape[1] // 2
    rows = CHUNK * group
    steps = total // rows
    whole = lambda i: (0, 0)
    flip = lambda i: (steps - 1 - i, 0)
    keep = lambda a, b: pl.BlockSpec((heads, group, a, b), lambda i: (0, steps - 1 - i, 0, 0))
    return pl.pallas_call(
        functools.partial(backward_kernel, heads, group, steps, len(maps), total // spots.shape[0]),
        grid=(steps,),
        in_specs=[
            pl.BlockSpec((rows, heads * PER), flip),
            pl.BlockSpec((HALO, heads * PER), lambda i: (jnp.maximum((steps - 1 - i) * (rows // HALO) - 1, 0), 0)),
            pl.BlockSpec((HALO, heads * PER), whole),
            pl.BlockSpec((rows, 2 * heads), flip),
            pl.BlockSpec((1, 2 * heads), whole),
            pl.BlockSpec((CONV, heads * MIX), whole),
            keep(DV + DK, DK),
            keep(CHUNK, DV + DK),
            keep(CHUNK, CHUNK),
            keep(DK, DK),
            keep(CHUNK, DK),
            pl.BlockSpec((rows, heads * DV), flip),
            pl.BlockSpec((rows, heads * DV), flip),
            pl.BlockSpec(incoming.shape, lambda i: (0, 0, 0)),
            pl.BlockSpec(memory_space=pltpu.SMEM),
            pl.BlockSpec(memory_space=pltpu.SMEM),
            *[pl.BlockSpec(part.shape, lambda i: (0, 0, 0)) for part in maps],
            *[pl.BlockSpec(part.shape, lambda i: (0, 0, 0)) for part in local],
        ],
        out_shape=[
            jax.ShapeDtypeStruct((total, heads * MIX), BF16),
            jax.ShapeDtypeStruct((total, 2 * heads), F32),
            jax.ShapeDtypeStruct((8, heads * MIX), F32),
            jax.ShapeDtypeStruct((HALO, heads * MIX), F32),
            jax.ShapeDtypeStruct((8, heads * MIX), F32),
        ],
        out_specs=[
            pl.BlockSpec((total, heads * MIX), whole),
            pl.BlockSpec((total, 2 * heads), whole),
            pl.BlockSpec((8, heads * MIX), whole),
            pl.BlockSpec((HALO, heads * MIX), whole),
            pl.BlockSpec((8, heads * MIX), whole),
        ],
        scratch_shapes=[
            pltpu.VMEM((rows + 8, heads * MIX), F32),
            pltpu.VMEM((rows + 8, heads * MIX), F32),
            pltpu.VMEM((heads, DV, DK), F32),
            pltpu.VMEM((heads, group, DV, DK), F32),
        ],
        compiler_params=pltpu.CompilerParams(vmem_limit_bytes=VMEM_LIMIT),
        cost_estimate=LIGHT,
    )(projected, projected, halo, rates, bias_row, taps, state, uw, inv, trans, qe, dout, value, incoming, place, spots, *maps, *local)


def pair_rows(ids_ref, step, which, rows):
    return pl.ds(pl.multiple_of(ids_ref[2 * step + which] * rows, rows), rows)


def gate_kernel(heads, peers, ids_ref, place_ref, gain_ref, w_ref, *refs):
    maps_refs, refs = refs[:peers], refs[peers:]
    olocal_refs, qmap_refs = refs[0:2], refs[2:4]
    gate_refs = refs[4 : 4 + 2 * heads]
    value_ref, gated_ref, part_ref, incoming_ref = refs[4 + 2 * heads :]
    step = pl.program_id(0)

    @pl.when(step == 0)
    def _():
        for h in range(heads):
            state = jnp.zeros((DV, DK), F32)
            for source in range(peers - 1):
                entry = chosen(maps_refs, place_ref, source, h, slice(None))
                moved = mm(state, entry[DV:]) + entry[:DV].astype(F32)
                state = jnp.where(source < place_ref[0], moved, state)
            incoming_ref[h] = state.astype(BF16)

    rows = olocal_refs[0].shape[0]
    for h in range(heads):
        cols = slice(h * DV, (h + 1) * DV)
        query_map = jnp.concatenate([ref[:, h * DK : (h + 1) * DK] for ref in qmap_refs], axis=0)
        out_local = jnp.concatenate([ref[:, cols] for ref in olocal_refs], axis=0)
        low = (out_local + mm(query_map, incoming_ref[h], 1, 1)).astype(BF16)
        for which in range(2):
            value_ref[pair_rows(ids_ref, step, which, rows), cols] = low[which * rows : (which + 1) * rows]
        value = low.astype(F32)
        normed = value * lax.rsqrt(jnp.mean(value * value, axis=-1, keepdims=True) + epsilon)
        gate = jnp.concatenate([gate_refs[2 * h + which][...] for which in range(2)], axis=0).astype(F32)
        gated_ref[:, cols] = (normed * gain_ref[...] * (gate * sigmoid(gate))).astype(BF16)
    part_ref[...] = mm(gated_ref[...], w_ref[...]).astype(BF16)


def gate_blocks(heads, rows):
    full = lambda wide: [
        pl.BlockSpec((rows, wide), lambda i, *s, which=which: (s[0][2 * i + which], 0)) for which in range(2)
    ]
    gates = [
        pl.BlockSpec(
            (rows, DV), lambda i, *s, which=which, h=h: (s[0][2 * i + which], (h + 1) * (PER // DV) - 1)
        )
        for h in range(heads)
        for which in range(2)
    ]
    return full, gates


def gate_output(ids, place, maps, out_local, query_map, projected, gain, w_out):
    heads = maps[0].shape[0]
    total = projected.shape[0]
    count = ids.shape[0]
    rows = total // count
    width = w_out.shape[1]
    mine = lambda i, *s: (i, 0)
    whole = lambda i, *s: (0, 0)
    full, gates = gate_blocks(heads, rows)
    return pl.pallas_call(
        functools.partial(gate_kernel, heads, len(maps)),
        grid_spec=pltpu.PrefetchScalarGridSpec(
            num_scalar_prefetch=2,
            grid=(count // 2,),
            in_specs=[
                pl.BlockSpec((1, DV), whole),
                pl.BlockSpec(w_out.shape, whole),
                *[pl.BlockSpec(part.shape, lambda i, *s: (0, 0, 0)) for part in maps],
                *full(heads * DV),
                *full(heads * DK),
                *gates,
            ],
            out_specs=[
                pl.BlockSpec((total, heads * DV), whole),
                pl.BlockSpec((2 * rows, heads * DV), mine),
                pl.BlockSpec((2 * rows, width), mine),
                pl.BlockSpec((heads, DV, DK), lambda i, *s: (0, 0, 0)),
            ],
        ),
        out_shape=[
            jax.ShapeDtypeStruct((total, heads * DV), BF16),
            jax.ShapeDtypeStruct((total, heads * DV), BF16),
            jax.ShapeDtypeStruct((total, width), BF16),
            jax.ShapeDtypeStruct((heads, DV, DK), BF16),
        ],
        compiler_params=pltpu.CompilerParams(vmem_limit_bytes=VMEM_LIMIT),
        cost_estimate=LIGHT,
    )(
        ids, place, gain, w_out, *maps, out_local, out_local, query_map, query_map,
        *[projected] * (2 * heads),
    )


def gate_back_kernel(heads, ids_ref, branch_ref, gain_ref, w_ref, *refs):
    value_refs, qmap_refs = refs[0:2], refs[2:4]
    gate_refs = refs[4 : 4 + 2 * heads]
    ggate_ref, dout_ref, gain_grad_ref, local_ref, sum_ref = refs[4 + 2 * heads :]
    step = pl.program_id(0)

    @pl.when(step == 0)
    def _():
        gain_grad_ref[...] = jnp.zeros_like(gain_grad_ref)
        sum_ref[...] = jnp.zeros_like(sum_ref)

    rows = value_refs[0].shape[0]
    grads = mm(branch_ref[...], w_ref[...], 1, 1)
    gain = gain_ref[...]
    for h in range(heads):
        cols = slice(h * DV, (h + 1) * DV)
        value = jnp.concatenate([ref[:, cols] for ref in value_refs], axis=0).astype(F32)
        inverse = lax.rsqrt(jnp.mean(value * value, axis=-1, keepdims=True) + epsilon)
        normed = value * inverse
        gate = jnp.concatenate([gate_refs[2 * h + which][...] for which in range(2)], axis=0).astype(F32)
        sig = sigmoid(gate)
        grad = grads[:, cols]
        through = grad * (gate * sig)
        ggate_ref[:, cols] = (grad * normed * gain * (sig * (1.0 + gate * (1.0 - sig)))).astype(BF16)
        gain_grad_ref[...] += jnp.sum(through * normed, axis=0, keepdims=True)
        scaled = through * gain
        low = (inverse * (scaled - normed * jnp.mean(scaled * normed, axis=-1, keepdims=True))).astype(BF16)
        for which in range(2):
            dout_ref[pair_rows(ids_ref, step, which, rows), cols] = low[which * rows : (which + 1) * rows]
        query_map = jnp.concatenate([ref[:, h * DK : (h + 1) * DK] for ref in qmap_refs], axis=0)
        sum_ref[h] += mm(low, query_map, 0, 0)

    @pl.when(step == pl.num_programs(0) - 1)
    def _():
        local_ref[...] = sum_ref[...].astype(BF16)


def gate_backward(ids, branch, w_out, value, projected, query_map, gain, heads):
    total = projected.shape[0]
    count = ids.shape[0]
    rows = total // count
    mine = lambda i, *s: (i, 0)
    whole = lambda i, *s: (0, 0)
    full, gates = gate_blocks(heads, rows)
    return pl.pallas_call(
        functools.partial(gate_back_kernel, heads),
        grid_spec=pltpu.PrefetchScalarGridSpec(
            num_scalar_prefetch=1,
            grid=(count // 2,),
            in_specs=[
                pl.BlockSpec((2 * rows, branch.shape[1]), mine),
                pl.BlockSpec((1, DV), whole),
                pl.BlockSpec(w_out.shape, whole),
                *full(heads * DV),
                *full(heads * DK),
                *gates,
            ],
            out_specs=[
                pl.BlockSpec((2 * rows, heads * DV), mine),
                pl.BlockSpec((total, heads * DV), whole),
                pl.BlockSpec((1, DV), whole),
                pl.BlockSpec((heads, DV, DK), lambda i, *s: (0, 0, 0)),
            ],
            scratch_shapes=[pltpu.VMEM((heads, DV, DK), F32)],
        ),
        out_shape=[
            jax.ShapeDtypeStruct((total, heads * DV), BF16),
            jax.ShapeDtypeStruct((total, heads * DV), BF16),
            jax.ShapeDtypeStruct((1, DV), F32),
            jax.ShapeDtypeStruct((heads, DV, DK), BF16),
        ],
        compiler_params=pltpu.CompilerParams(vmem_limit_bytes=VMEM_LIMIT),
        cost_estimate=LIGHT,
    )(
        ids, branch, gain, w_out, value, value, query_map, query_map, *[projected] * (2 * heads)
    )


def project_kernel(layout, pieces, ids_ref, spots_ref, rate_ref, *refs):
    x_refs = refs[: len(layout)]
    w_refs = refs[len(layout) : len(layout) + pieces]
    out_ref, rates_ref = refs[len(layout) + pieces :]
    rows = out_ref.shape[0] // ids_ref.shape[0]
    blocks = {}
    for (k, _), ref in zip(layout, x_refs):
        blocks.setdefault(k, []).append(ref)
    ks = list(blocks)
    for first in range(0, len(ks), 2):
        group = ks[first : first + 2]
        group_refs = [ref for k in group for ref in blocks[k]]
        x = jnp.concatenate([ref[...] for ref in group_refs], axis=0)
        total = None
        for b, w_ref in enumerate(w_refs):
            cols = block_columns(spots_ref, b, w_ref.shape[0])
            share = mm(jnp.concatenate([ref[:, cols] for ref in group_refs], axis=0), w_ref[...])
            total = share if total is None else total + share
        total = total.astype(BF16)
        rates = mm(x, rate_ref[...], 1, 1)
        for i, k in enumerate(group):
            place = pl.ds(pl.multiple_of(ids_ref[k] * rows, rows), rows)
            out_ref[place, :] = total[i * rows : (i + 1) * rows]
            rates_ref[place, :] = rates[i * rows : (i + 1) * rows]


def layout_of(found, total):
    rows = found[0][0].shape[0]
    count = total // rows
    ks = [0] + [k for s in range(1, count // 2) for k in (s, count - s)] + [count // 2]
    layout, arrays = [], []
    for k in ks:
        start = k * rows
        for piece in found.get(k, ()):
            layout.append((k, start))
            arrays.append(piece)
            start += piece.shape[0]
    return layout, arrays


def project(ids, spots, found, w_mix, w_rate):
    total = ids.shape[0] * found[0][0].shape[0]
    layout, arrays = layout_of(found, total)
    cols = w_mix[0].shape[1]
    rates = w_rate.shape[0]
    whole = lambda shape: pl.BlockSpec(shape, lambda i, ids, spots: (0, 0))
    return pl.pallas_call(
        functools.partial(project_kernel, layout, len(w_mix)),
        grid_spec=pltpu.PrefetchScalarGridSpec(
            num_scalar_prefetch=2,
            grid=(1,),
            in_specs=[whole(a.shape) for a in (w_rate, *arrays, *w_mix)],
            out_specs=[whole((total, cols)), whole((total, rates))],
        ),
        out_shape=[
            jax.ShapeDtypeStruct((total, cols), BF16),
            jax.ShapeDtypeStruct((total, rates), F32),
        ],
        compiler_params=pltpu.CompilerParams(vmem_limit_bytes=VMEM_LIMIT),
        cost_estimate=LIGHT,
    )(ids, spots, w_rate, *arrays, *w_mix)


def normed_back_kernel(pieces, blocks, spots_ref, *refs):
    mixes, gates, rates, normed = (refs[i * blocks : (i + 1) * blocks] for i in range(4))
    rate_ref, before_ref = refs[4 * blocks : 4 * blocks + 2]
    w_refs = refs[4 * blocks + 2 : 4 * blocks + 2 + pieces]
    part_ref, sums_ref = refs[4 * blocks + 2 + pieces :]
    heads = gates[0].shape[1] // DV
    left = jnp.concatenate(
        [
            jnp.concatenate([ref[:, h * size : (h + 1) * size] for ref in group], axis=0)
            for h in range(heads)
            for group, size in ((mixes, MIX), (gates, DV))
        ],
        axis=1,
    )
    rate = jnp.concatenate([ref[...].astype(BF16) for ref in rates], axis=0)
    count = rate.shape[1]
    sums_ref[...] = before_ref[...]
    for b, w_ref in enumerate(w_refs):
        cols = block_columns(spots_ref, b, w_ref.shape[0])
        part = mm(left, w_ref[...], 1, 1) + mm(rate, rate_ref[:, cols])
        part_ref[:, cols] = part.astype(BF16)
        right = jnp.concatenate([ref[:, cols] for ref in normed], axis=0)
        sums_ref[:count, cols] += mm(rate, right, 0, 0)
        sums_ref[4:5, cols] += jnp.sum(part * right.astype(F32), axis=0, keepdims=True)


def normed_back(spots, order, blocks, grad_mixed, grad_gates, grad_rates, normed, w_mix, w_rate, before):
    total, width = normed.shape
    rows = total // blocks
    rates = w_rate.shape[0]
    count = len(order)
    block = lambda k, wide: pl.BlockSpec((rows, wide), lambda i, spots: (k, 0))
    whole = lambda i, spots: (0, 0)
    return pl.pallas_call(
        functools.partial(normed_back_kernel, len(w_mix), count),
        grid_spec=pltpu.PrefetchScalarGridSpec(
            num_scalar_prefetch=1,
            grid=(1,),
            in_specs=[
                *[block(k, grad_mixed.shape[1]) for k in order],
                *[block(k, grad_gates.shape[1]) for k in order],
                *[block(k, rates) for k in order],
                *[block(k, width) for k in order],
                pl.BlockSpec((rates, width), whole),
                pl.BlockSpec((8, width), whole),
                *[pl.BlockSpec(w.shape, whole) for w in w_mix],
            ],
            out_specs=[pl.BlockSpec((count * rows, width), whole), pl.BlockSpec((8, width), whole)],
        ),
        out_shape=[
            jax.ShapeDtypeStruct((count * rows, width), BF16),
            jax.ShapeDtypeStruct((8, width), F32),
        ],
        compiler_params=pltpu.CompilerParams(vmem_limit_bytes=VMEM_LIMIT),
        cost_estimate=LIGHT,
    )(
        spots,
        *[grad_mixed] * count,
        *[grad_gates] * count,
        *[grad_rates] * count,
        *[normed] * count,
        w_rate,
        before,
        *w_mix,
    )


def stack_kernel(layout, *refs):
    out_ref = refs[len(layout)]
    for (_, start), ref in zip(layout, refs):
        out_ref[start : start + ref.shape[0], :] = ref[...]


def stacked(found, total):
    layout, arrays = layout_of(found, total)
    return pl.pallas_call(
        functools.partial(stack_kernel, layout),
        out_shape=jax.ShapeDtypeStruct((total, arrays[0].shape[1]), arrays[0].dtype),
        compiler_params=pltpu.CompilerParams(vmem_limit_bytes=VMEM_LIMIT),
        cost_estimate=LIGHT,
    )(*arrays)


def finish_kernel(first_ref, second_ref, buffer_ref, out_ref):
    half = first_ref.shape[0]
    out_ref[:half, :] = first_ref[...]
    out_ref[half:, :] = second_ref[...]


def finish_stack(buffer, pieces, k):
    half, width = pieces[0].shape
    whole = pl.BlockSpec((half, width), lambda i: (0, 0))
    return pl.pallas_call(
        finish_kernel,
        grid=(1,),
        in_specs=[whole, whole, pl.BlockSpec(memory_space=pl.ANY)],
        out_specs=pl.BlockSpec((2 * half, width), lambda i: (k, 0)),
        out_shape=jax.ShapeDtypeStruct(buffer.shape, buffer.dtype),
        input_output_aliases={2: 0},
        cost_estimate=LIGHT,
    )(*pieces, buffer)


def outer_kernel(left_ref, right_ref, out_ref):
    out_ref[...] = mm(left_ref[...], right_ref[...], 0, 0).astype(BF16)


def outer(left, right):
    total, m = left.shape
    n = right.shape[1]
    by_rows = m % 512 == 0 and m > 512
    rows = 512 if by_rows else m
    cols = n if by_rows or n % 512 else 512
    return pl.pallas_call(
        outer_kernel,
        grid=(m // rows, n // cols),
        in_specs=[
            pl.BlockSpec((total, rows), lambda i, j: (0, i)),
            pl.BlockSpec((total, cols), lambda i, j: (0, j)),
        ],
        out_specs=pl.BlockSpec((rows, cols), lambda i, j: (i, j)),
        out_shape=jax.ShapeDtypeStruct((m, n), BF16),
        compiler_params=pltpu.CompilerParams(vmem_limit_bytes=VMEM_LIMIT),
        cost_estimate=LIGHT,
    )(left, right)


def turn_kernel(count, *refs):
    for i in range(count):
        refs[count + i][...] = refs[i][...].astype(F32).T.astype(BF16)


def turned(arrays):
    rows, width = arrays[0].shape
    step = 512
    return pl.pallas_call(
        functools.partial(turn_kernel, len(arrays)),
        grid=(width // step,),
        in_specs=[pl.BlockSpec((rows, step), lambda i: (0, i))] * len(arrays),
        out_specs=[pl.BlockSpec((step, rows), lambda i: (i, 0))] * len(arrays),
        out_shape=[jax.ShapeDtypeStruct((width, rows), BF16)] * len(arrays),
        compiler_params=pltpu.CompilerParams(vmem_limit_bytes=VMEM_LIMIT),
        cost_estimate=LIGHT,
    )(*arrays)


def widen_kernel(count, *refs):
    for i in range(count):
        refs[count + i][...] = refs[i][...].astype(F32)


def widen(arrays):
    steps = 4
    specs = [pl.BlockSpec((a.shape[0] // steps, a.shape[1]), lambda i: (i, 0)) for a in arrays]
    return pl.pallas_call(
        functools.partial(widen_kernel, len(arrays)),
        grid=(steps,),
        in_specs=specs,
        out_specs=specs,
        out_shape=[jax.ShapeDtypeStruct(a.shape, F32) for a in arrays],
        compiler_params=pltpu.CompilerParams(vmem_limit_bytes=VMEM_LIMIT),
        cost_estimate=LIGHT,
    )(*arrays)


def join_kernel(heads, mix_ref, gate_ref, out_ref):
    for h in range(heads):
        out_ref[:, h * PER : h * PER + MIX] = mix_ref[:, h * MIX : (h + 1) * MIX].astype(F32)
        out_ref[:, h * PER + MIX : (h + 1) * PER] = gate_ref[:, h * DV : (h + 1) * DV].astype(F32)


def join_heads(mix, gate):
    rows = mix.shape[0]
    heads = gate.shape[1] // DV
    steps = 4
    spec = lambda wide: pl.BlockSpec((rows // steps, wide), lambda i: (i, 0))
    return pl.pallas_call(
        functools.partial(join_kernel, heads),
        grid=(steps,),
        in_specs=[spec(mix.shape[1]), spec(gate.shape[1])],
        out_specs=spec(heads * PER),
        out_shape=jax.ShapeDtypeStruct((rows, heads * PER), F32),
        compiler_params=pltpu.CompilerParams(vmem_limit_bytes=VMEM_LIMIT),
        cost_estimate=LIGHT,
    )(mix, gate)


def times_kernel(left_ref, right_ref, out_ref):
    out_ref[...] = mm(left_ref[...], right_ref[...])


def times(left, right):
    total, depth = left.shape
    n = right.shape[1]
    rows = 256
    return pl.pallas_call(
        times_kernel,
        grid=(total // rows,),
        in_specs=[
            pl.BlockSpec((rows, depth), lambda i: (i, 0)),
            pl.BlockSpec((depth, n), lambda i: (0, 0)),
        ],
        out_specs=pl.BlockSpec((rows, n), lambda i: (i, 0)),
        out_shape=jax.ShapeDtypeStruct((total, n), F32),
        compiler_params=pltpu.CompilerParams(vmem_limit_bytes=VMEM_LIMIT),
        cost_estimate=LIGHT,
    )(left, right)


def finish_all_kernel(heads, count, mix_ref, gate_ref, *refs):
    join_kernel(heads, mix_ref, gate_ref, refs[count])
    for i in range(count):
        refs[count + 1 + i][...] = refs[i][...].astype(F32)


def finish_all(mix, gate, others):
    heads = gate.shape[1] // DV
    steps = 4
    spec = lambda a, wide: pl.BlockSpec((a.shape[0] // steps, wide), lambda i: (i, 0))
    plain = [spec(a, a.shape[1]) for a in others]
    return pl.pallas_call(
        functools.partial(finish_all_kernel, heads, len(others)),
        grid=(steps,),
        in_specs=[spec(mix, mix.shape[1]), spec(gate, gate.shape[1]), *plain],
        out_specs=[spec(mix, heads * PER), *plain],
        out_shape=[
            jax.ShapeDtypeStruct((mix.shape[0], heads * PER), F32),
            *[jax.ShapeDtypeStruct(a.shape, F32) for a in others],
        ],
        compiler_params=pltpu.CompilerParams(vmem_limit_bytes=VMEM_LIMIT),
        cost_estimate=LIGHT,
    )(mix, gate, *others)
def ring_order(count):
    return list(range(0, count, 2)) + list(range(1, count, 2))[::-1]


def ring_step(value, axis, step):
    order = ring_order(lax.axis_size(axis))
    count = len(order)
    return lax.ppermute(value, axis, [(order[i], order[(i + step) % count]) for i in range(count)])


def ring_ids(axis):
    order = ring_order(lax.axis_size(axis))
    count = len(order)
    place = {device: i for i, device in enumerate(order)}
    ahead = [[order[(place[device] + k) % count] for k in range(count)] for device in range(count)]
    back = [[row.index(device) for device in range(count)] for row in ahead]
    row = lax.dynamic_index_in_dim(
        jnp.array([a + b for a, b in zip(ahead, back)], jnp.int32), lax.axis_index(axis), 0, False
    )
    return row[:count], row[count:]


def after(value, *earlier):
    return lax.optimization_barrier((value, *earlier))[0]


def together(*values):
    return lax.optimization_barrier(values)


def window(fillers, hop, gate):
    return fillers[hop](lambda value: after(value, gate)) if hop in fillers else ()


def ring_gather(shard, axis, fillers={}, stack=True):
    count = lax.axis_size(axis)
    far = count // 2
    half = shard.shape[0] // 2
    total = count * shard.shape[0]
    found = {0: [shard]}
    forward = backward = shard
    buffer = None
    for hop in range(1, far + 1):
        gate = forward
        extra = list(window(fillers, hop, gate))
        if hop < far:
            forward = ring_step(forward, axis, 1)
            backward = ring_step(backward, axis, -1)
            found[count - hop] = [forward]
            found[hop] = [backward]
        else:
            if stack:
                buffer = stacked({k: [after(p, gate) for p in ps] for k, ps in found.items()}, total)
                extra.append(buffer)
            forward = ring_step(forward[:half], axis, 1)
            backward = ring_step(backward[half:], axis, -1)
            found[hop] = [forward, backward]
        forward, backward, *_ = together(forward, backward, *extra)
    found[far] = [forward, backward]
    return finish_stack(buffer, found[far], far) if stack else found


def ring_scatter(take, rows, axis, fillers={}):
    count = lax.axis_size(axis)
    far = count // 2
    size = rows // 2
    flows = [[take(far, 0, size), None], [None, take(far, size, size)]]
    gate = take(far, 0, size)
    for hop in range(1, far + 1):
        flows = [
            [flow[way] if flow[way] is None else ring_step(flow[way], axis, 1 - 2 * way) for way in range(2)]
            for flow in flows
        ]
        extra = window(fillers, hop, gate)
        flat = together(*[a for flow in flows for a in flow if a is not None], *extra)
        flat = iter(flat)
        flows = [[None if a is None else next(flat) for a in flow] for flow in flows]
        s = far - hop
        if s:
            for part, flow in enumerate(flows):
                for way, k in enumerate((s, count - s)):
                    piece = take(k, part * size, size)
                    flow[way] = piece if flow[way] is None else flow[way] + piece
            gate = flows[0][0]
    totals = [
        take(0, part * size, size).astype(F32) + flow[0].astype(F32) + flow[1].astype(F32)
        for part, flow in enumerate(flows)
    ]
    return jnp.concatenate(totals, axis=0)


def near_rows(array, rows):
    return lambda k, start, size: lax.slice_in_dim(array, k * rows + start, k * rows + start + size, axis=0)


def swap(value, axis, bit):
    count = lax.axis_size(axis)
    return lax.ppermute(value, axis, [(i, i ^ bit) for i in range(count)])


def pair_spots(axis):
    count = lax.axis_size(axis)
    order = jnp.arange(count, dtype=jnp.int32)
    return lax.axis_index(axis) ^ order if count == 4 else order


def pair_far(shard, axis, *pins):
    if lax.axis_size(axis) != 4:
        return lax.all_gather(shard, axis)
    return swap(after(shard, *pins), axis, 2)


def pair_gather(shard, far, axis, *pins):
    count = lax.axis_size(axis)
    if count != 4:
        return [far[b] for b in range(count)]
    return [shard, swap(after(shard, *pins), axis, 1), far, swap(after(far, *pins), axis, 1)]


def seq_shards(value, axis):
    if lax.axis_size(axis) != 4:
        whole = lax.all_gather(value, axis)
        return [whole[b] for b in range(lax.axis_size(axis))]
    return [value] + [swap(value, axis, b) for b in range(1, 4)]


def butterfly(value, axis):
    bit = 1
    while bit < lax.axis_size(axis):
        value = value + swap(value, axis, bit)
        bit *= 2
    return value


def per_device(
    tokens,
    w_qkvg,
    w_rates,
    conv_weight,
    head_bias,
    norm_gain,
    head_gain,
    mlp_gain,
    w_out,
    w_ff_gate,
    w_ff_up,
    w_ff_down,
    cotangent,
):
    heads = head_bias.shape[1]
    own_rows = tokens.shape[0]
    contract = (((1,), (1,)), ((), ()))
    rows_first = (((0,), (0,)), ((), ()))
    dot = lambda a, b, dims: lax.dot_general(a, b, dims, preferred_element_type=F32)
    plain = (((1,), (0,)), ((), ()))
    ids, near_spots = ring_ids("head")
    spots = pair_spots("seq")
    place = lax.axis_index("seq").reshape(1)
    gain_row = head_gain.reshape(1, DV)
    bias_row = head_bias.T.reshape(1, 2 * heads)
    peers = lax.axis_size("seq")
    width = tokens.shape[1]
    keep = {}
    mix_far = pair_far(w_qkvg, "seq")
    inputs = tokens.astype(F32)
    inverse_one = lax.rsqrt(jnp.mean(inputs * inputs, axis=-1, keepdims=True) + epsilon)
    norm_normed = inputs * inverse_one
    hops = lax.axis_size("head") // 2
    last_window = hops

    rate_shard = w_rates.T
    if peers == 4:
        w_rate = jnp.zeros((2 * heads, width), BF16)
        for b in range(4):
            w_rate = lax.dynamic_update_slice_in_dim(
                w_rate,
                swap(rate_shard, "seq", b) if b else rate_shard,
                (place[0] ^ b) * rate_shard.shape[1],
                1,
            )
    else:
        w_rate = lax.all_gather(rate_shard, "seq", axis=1, tiled=True)

    count = 2 * hops
    stages = 4
    cot_found = {0: [cotangent]}
    cot_state = [cotangent, cotangent]

    def cot_hop(hop, *gates):
        forward, backward, *_ = together(*cot_state, *gates)
        if hop < hops:
            forward, backward = ring_step(forward, "head", 1), ring_step(backward, "head", -1)
            cot_found[count - hop], cot_found[hop] = [forward], [backward]
        else:
            half = own_rows // 2
            forward = ring_step(forward[:half], "head", 1)
            backward = ring_step(backward[half:], "head", -1)
            cot_found[hop] = [forward, backward]
        cot_state[:] = [forward, backward]
        return list(cot_state)

    def fetch_mix(pin):
        keep["mix"] = pair_gather(w_qkvg, pin(mix_far), "seq")
        return keep["mix"]

    fillers = {last_window: fetch_mix}
    normed_found = ring_gather((norm_normed * norm_gain).astype(BF16), "head", fillers, False)
    w_mix = keep["mix"]
    out_rows = lax.all_gather(after(w_out, mix_far), "seq", axis=1, tiled=True)

    stage_hops = {
        stage: range(1 + hops * stage // stages, 1 + hops * (stage + 1) // stages) for stage in range(stages)
    }

    def cot_stage(stage, gate):
        made = []
        for hop in stage_hops[stage]:
            made = cot_hop(hop, gate)
        return made

    cot_stage(0, normed_found[hops][0])
    projected, rates = project(ids, spots, normed_found, w_mix, w_rate)
    seq_rows = projected.shape[0]
    halo_rows = shifted(projected[seq_rows - HALO :], "seq", 1)
    projected, *_ = together(projected, *cot_state)
    cot_stage(1, projected)
    out_local, query_map, *saved, end_state = mixer_forward(
        projected, halo_rows, rates, bias_row, conv_weight, GROUP
    )
    end_state, *_ = together(end_state, *cot_state)
    cot_stage(2, end_state)
    maps = seq_shards(end_state, "seq")
    maps = list(together(*maps, *cot_state))[:peers]
    cot_stage(3, maps[1])
    value, gated, branch_part, incoming = gate_output(
        ids, place, maps, out_local, query_map, projected, gain_row, out_rows
    )
    branch_part, *_ = together(branch_part, *cot_state)
    fetch = lambda w, *pins: lax.all_gather(after(w, *pins), "seq", axis=1, tiled=True)
    down_w = fetch(w_ff_down, *maps)
    gate_w = fetch(w_ff_gate, *maps)
    up_w = fetch(w_ff_up, *maps)

    def stack_normed(pin):
        keep["normed"] = stacked({k: [pin(p) for p in ps] for k, ps in normed_found.items()}, seq_rows)
        return (keep["normed"],)

    def stack_cotangent(pin):
        keep["cot"] = stacked({k: [pin(p) for p in ps] for k, ps in cot_found.items()}, seq_rows)
        return (keep["cot"],)

    def turn_down(pin):
        keep["down_t"] = turned([pin(down_w)])
        return keep["down_t"]

    def turn_others(pin):
        keep["others_t"] = turned([pin(gate_w), pin(up_w)])
        return keep["others_t"]

    residual = inputs + ring_scatter(
        near_rows(branch_part, own_rows), own_rows, "head", {1: stack_cotangent, 2: stack_normed}
    )
    inverse_two = lax.rsqrt(jnp.mean(residual * residual, axis=-1, keepdims=True) + epsilon)
    mlp_normed = residual * inverse_two

    def hidden_gradient(pin):
        keep["gh"] = times(pin(keep["cot"]), keep["down_t"][0])
        return (keep["gh"],)

    mlp_near = ring_gather((mlp_normed * mlp_gain).astype(BF16), "head", {1: turn_down, 2: hidden_gradient, 3: turn_others})
    normed, cotangent_near, grad_hidden = keep["normed"], keep["cot"], keep["gh"]

    gate_pre, up_pre = (dot(mlp_near, w, plain) for w in keep["others_t"])
    ff_sigmoid = jax.nn.sigmoid(gate_pre)
    ff_silu = gate_pre * ff_sigmoid
    hidden = (ff_silu * up_pre).astype(BF16)
    ff_slope = ff_sigmoid * (1.0 + gate_pre * (1.0 - ff_sigmoid))
    grad_gate_pre = (grad_hidden * up_pre * ff_slope).astype(BF16)
    grad_up_pre = (grad_hidden * ff_silu).astype(BF16)
    grad_mlp_part = (dot(grad_gate_pre, gate_w, plain) + dot(grad_up_pre, up_w, plain)).astype(BF16)

    scatter = lambda a: lax.psum_scatter(a, "seq", scatter_dimension=1, tiled=True)

    def weight_product(name, left, right, before=None):
        def filler(pin):
            made = [outer(pin(left), right)] if left is not None else []
            if before is not None:
                keep[before, "sum"] = scatter(pin(keep[before]))
            if made:
                keep[name] = made[0]
            return made

        return filler

    def output_rows(pin):
        keep["up", "sum"] = scatter(pin(keep["up"]))
        keep["output"] = dot(pin(hidden), down_w, plain).astype(BF16)
        return (keep["output"],)

    grad_mlp_in = ring_scatter(
        near_rows(grad_mlp_part, own_rows),
        own_rows,
        "head",
        {
            1: weight_product("down", hidden, cotangent_near),
            2: weight_product("gate", grad_gate_pre, mlp_near, "down"),
            3: weight_product("up", grad_up_pre, mlp_near, "gate"),
            4: output_rows,
        },
    )

    output_part = keep["output"]
    mlp_gain_part = jnp.sum(grad_mlp_in * mlp_normed, axis=0)
    scaled_two = grad_mlp_in * mlp_gain
    grad_residual = cotangent.astype(F32) + inverse_two * (
        scaled_two - mlp_normed * jnp.mean(scaled_two * mlp_normed, axis=-1, keepdims=True)
    )

    grad_down_s, grad_gate_s, grad_up_s = (keep[name, "sum"] for name in ("down", "gate", "up"))
    def first_output(pin):
        start = hops * own_rows
        keep["first"] = pin(lax.slice_in_dim(output_part, start, start + own_rows, axis=0))
        return [grad_down_s, keep["first"]]

    branch_near = ring_gather(
        grad_residual.astype(BF16), "head", {2: first_output, 4: lambda pin: [grad_gate_s]}
    )
    take_output = near_rows(output_part, own_rows)
    output_state = [None, None]
    known = lambda: [a for a in output_state if a is not None]

    def output_hops(stage, *gates):
        for hop in range(hops * (stage - 1) // stages, hops * stage // stages):
            here = []
            for way, k in enumerate((hops - hop, count - hops + hop)):
                if hop == 0 and way == 1:
                    here.append(None)
                    continue
                piece = take_output(k, 0, own_rows) if hop else keep["first"]
                total = piece if output_state[way] is None else output_state[way] + piece
                here.append(ring_step(after(total, *gates), "head", 1 - 2 * way))
            output_state[:] = here

    output_hops(1, branch_near)
    grad_gate_mix, grad_mixer, head_gain_part, local_grad = gate_backward(
        ids, branch_near, out_rows, value, projected, query_map, gain_row, heads
    )
    local_low, *_ = together(local_grad, *known())
    shares = seq_shards(local_low, "seq")
    gate_grad_w = outer(keep["normed"], together(grad_gate_mix, *shares[1:])[0])
    output_hops(2, shares[1])
    first_share, gate_grad_w, *_ = together(shares[0], gate_grad_w, *known())
    gate_grad_s = lax.psum_scatter(gate_grad_w, "seq", scatter_dimension=0, tiled=True)
    output_hops(3, gate_grad_w)
    grad_mixed, grad_rates, seq_sums, tail_rows, lead_rows = mixer_backward(
        projected, halo_rows, rates, bias_row, conv_weight, saved,
        grad_mixer, value, incoming, place, near_spots, maps, [first_share, *shares[1:]], GROUP,
    )
    grad_mixed, gate_grad_s, grad_up_s, *_ = together(grad_mixed, gate_grad_s, grad_up_s, *known())
    later_rows = shifted(lead_rows, "seq", -1)
    output_hops(4, grad_mixed)
    padded = jnp.concatenate([jnp.zeros((HALO, heads * MIX), F32), later_rows])
    last_rows = tail_rows + sum(
        conv_weight[i] * padded[CONV - 1 - i : CONV - 1 - i + HALO] for i in range(CONV)
    )
    last_start = near_spots[count - 1] * own_rows + own_rows - HALO
    grad_mixed = lax.dynamic_update_slice(grad_mixed, last_rows.astype(BF16), (last_start, 0))
    mix_grad_w = outer(keep["normed"], grad_mixed)
    grad_mixed, mix_grad_w = together(grad_mixed, mix_grad_w)
    mix_grad_s = lax.psum_scatter(mix_grad_w, "seq", scatter_dimension=0, tiled=True)
    early = [hops] + ([hops - 1, hops + 1] if hops > 1 else [])
    late = [k for s in range(hops - 2, 0, -1) for k in (s, count - s)] + [0]
    place_of = {k: (0, i) for i, k in enumerate(early)} | {k: (1, i) for i, k in enumerate(late)}
    parts = []
    part, sums = normed_back(
        spots, early, count, grad_mixed, grad_gate_mix, grad_rates, normed, w_mix, w_rate, jnp.zeros((8, width), F32)
    )
    part, *_ = together(part, *known())
    parts.append(part)

    def take(k, start, size):
        which, i = place_of[k]
        return lax.slice_in_dim(parts[which], i * own_rows + start, i * own_rows + start + size, axis=0)

    def late_rows(pin):
        part, keep["sums"] = normed_back(
            spots, late, count, pin(grad_mixed), grad_gate_mix, grad_rates, normed, w_mix, w_rate, sums
        )
        parts.append(part)
        return (part,)

    def first_window(pin):
        return late_rows(pin)

    def second_window(pin):
        sums = pin(keep["sums"])
        gains = jnp.concatenate([mlp_gain_part[None], head_gain_part, jnp.zeros((1, width - DV), F32)], axis=1)
        gains = jnp.pad(gains, ((4, 3), (0, 0)))
        small = jnp.concatenate([sums, gains, seq_sums], axis=1)
        keep["small"] = small + swap(small, "seq", 1)
        out_grad_w = outer(gated, pin(branch_near))
        keep["out"] = scatter(out_grad_w)
        return (keep["small"], out_grad_w)

    def third_window(pin):
        small = pin(keep["small"])
        bit = 2
        while bit < peers:
            small = small + swap(small, "seq", bit)
            bit *= 2
        keep["small"] = small
        keep["gains"] = small[4:5, : 3 * width]
        return (small, mix_grad_s)

    grad_normed = ring_scatter(
        take, own_rows, "head", {1: first_window, 2: second_window, 3: third_window}
    )
    scaled_one = grad_normed * norm_gain
    grad_input = grad_residual + inverse_one * (
        scaled_one - norm_normed * jnp.mean(scaled_one * norm_normed, axis=-1, keepdims=True)
    )
    output = (
        residual + sum(a.astype(F32) for a in known()) + take_output(0, 0, own_rows).astype(F32)
    ).astype(BF16)
    small, gains = keep["small"], after(keep["gains"], grad_normed)
    bit = 1
    while bit < count:
        gains = gains + swap(gains, "head", bit)
        bit *= 2
    joined, *wide = finish_all(mix_grad_s, gate_grad_s, [keep["out"], grad_gate_s, grad_up_s, grad_down_s])
    per_seq = w_rates.shape[0]
    return (
        output,
        grad_input,
        joined,
        lax.dynamic_slice_in_dim(small[: 2 * heads], place[0] * per_seq, per_seq, 1).T,
        small[:CONV, 3 * width :],
        small[CONV, 3 * width : 3 * width + 2 * heads].reshape(heads, 2).T,
        gains[0, :width] / norm_gain,
        gains[0, 2 * width : 2 * width + DV],
        gains[0, width : 2 * width],
        *wide,
    )


def solution(mesh):
    in_specs = (
        P(("seq", "head"), None),
        P("seq", "head"),
        P("seq", "head"),
        P(None, "head"),
        P(None, "head"),
        P(),
        P(),
        P(),
        P("head", "seq"),
        P("head", "seq"),
        P("head", "seq"),
        P("head", "seq"),
        P(("seq", "head"), None),
    )
    out_specs = (
        P(("seq", "head"), None),
        P(("seq", "head"), None),
        P("seq", "head"),
        P("seq", "head"),
        P(None, "head"),
        P(None, "head"),
        P(),
        P(),
        P(),
        P("head", "seq"),
        P("head", "seq"),
        P("head", "seq"),
        P("head", "seq"),
    )
    return jax.shard_map(
        per_device, mesh=mesh, in_specs=in_specs, out_specs=out_specs, check_vma=False
    )
```
